32 devices in a mesh: wide: 8 (over z, y), narrow: 4 (over x, core).
Axes of the slice: x: 2, y: 2, z: 4, core: 2. Of those that a mesh axis runs over, the one named last changes fastest.
Arguments:
- tokens: bfloat16 [8192, 2048], P('wide'), may hold values from -6 to 6
- seq_lengths: int32 [8, 4], P('wide'), may hold values from 1 to 768, 1024 in all within a row
- attn_gain: float32 [2048], replicated, may hold values from 0.1 to 1.9
- w_query: bfloat16 [2048, 2048], P(None, 'narrow'), may hold values from -0.125 to 0.125
- key_weight: bfloat16 [2048, 1024], P(None, 'narrow'), may hold values from -0.125 to 0.125
- value_weight: bfloat16 [2048, 1024], P(None, 'narrow'), may hold values from -0.125 to 0.125
- query_gain: float32 [128], replicated, may hold values from 0.1 to 1.9
- key_norm_gain: float32 [128], replicated, may hold values from 0.1 to 1.9
- w_output: bfloat16 [2048, 2048], P('narrow'), may hold values from -0.5 to 0.5
- mlp_gain: float32 [2048], replicated, may hold values from 0.1 to 1.9
- w_gate: bfloat16 [2048, 6144], P(None, 'narrow'), may hold values from -0.125 to 0.125
- w_up: bfloat16 [2048, 6144], P(None, 'narrow'), may hold values from -0.125 to 0.125
- w_down: bfloat16 [6144, 2048], P('narrow'), may hold values from -0.078125 to 0.078125
- cotangent: bfloat16 [8192, 2048], P('wide'), may hold values from -6 to 6
Outputs:
- output: bfloat16 [8192, 2048], P('wide')
- grad_tokens: bfloat16 [8192, 2048], P('wide')
- grad_attn_gain: float32 [2048], P('wide')
- grad_w_query: float32 [2048, 2048], P('wide', 'narrow')
- grad_w_key: float32 [2048, 1024], P('wide', 'narrow')
- grad_w_value: float32 [2048, 1024], P('wide', 'narrow')
- grad_query_gain: float32 [128], P('wide')
- grad_key_gain: float32 [128], P('wide')
- grad_w_output: float32 [2048, 2048], P('narrow', 'wide')
- grad_mlp_gain: float32 [2048], P('wide')
- grad_w_gate: float32 [2048, 6144], P('wide', 'narrow')
- grad_w_up: float32 [2048, 6144], P('wide', 'narrow')
- grad_w_down: float32 [6144, 2048], P('narrow', 'wide')
The draws below stay inside these ranges and needn't reach their ends.
Inputs may be any that keep to these rules, and one draw needn't show every extreme that they name: `seq_lengths`: each row's 4 lengths sum to 1024, and the longest of each row is 768.
All inputs are finite; a program needn't handle non-finite values.
Results may differ from the reference program's by a relative error of at most 0.015.
Values sent between devices are 32-bit elements; how exact they have to be, the bound alone decides.
A program may use at most 256 MiB of HBM per device.

```python
import math
import jax
import jax.numpy as jnp
import numpy as np
from jax import lax

MODEL_WIDTH = 2048
QUERY_HEADS = 16
KEY_VALUE_HEADS = 8
HEAD_SIZE = 128
FF = 6144
TOKENS_PER_ROW = 1024
SEQ_ROW = 4
MOST_LEN = 768
ROWS = 8
TOKENS = 8192


def block_scale(own_key, extent, pieces, low, top_value):
    level = 1.0
    for axis_at, parts in pieces:
        heights = jax.random.uniform(jax.random.fold_in(jax.random.fold_in(own_key, 6), axis_at), (parts,), jnp.float32, low / len(pieces), top_value / len(pieces))
        level = level * jnp.repeat(jnp.exp(heights), extent[axis_at] // parts).reshape((-1,) + (1,) * (len(extent) - 1 - axis_at))
    return level


def length_profile(number_of, total, reach, skew):
    loads = [(1 << 20) // math.isqrt(rank ** skew) + 1 for rank in range(2, number_of + 1)]
    surplus, holding = total - reach - (number_of - 1), [1] * (number_of - 1)
    while surplus > 0:
        candidates = [i for i in range(number_of - 1) if holding[i] < reach]
        mass, left = sum([loads[i] for i in candidates]), surplus
        for i in candidates:
            more = min(reach - holding[i], max(1, left * loads[i] // mass), surplus)
            holding[i] = holding[i] + more
            surplus = surplus - more
    return np.array([reach] + holding)


def uneven(stream_key, count, total, reach, skew):
    if count == 2:
        one = jax.random.randint(stream_key, (), max(1, total - reach), min(reach, total - 1) + 1)
        return jnp.stack([one, total - one])
    lengths = jnp.asarray(length_profile(count, total, reach, skew), jnp.int32)
    twos = (count - 1) // 2
    source_of, sink = lengths[1:1 + 2 * twos:2], lengths[2:2 + 2 * twos:2]
    slack = jnp.minimum(source_of - 1, reach - sink)
    moved = jax.random.randint(jax.random.fold_in(stream_key, 1), (twos,), 0, 1 << 20) % (slack + 1)
    lengths = lengths.at[1:1 + 2 * twos:2].set(source_of - moved).at[2:2 + 2 * twos:2].set(sink + moved)
    return lengths[jax.random.permutation(jax.random.fold_in(stream_key, 2), count)]


def bell_draw(stream_key, shape, width, limit, shards=(), kind=jnp.bfloat16):
    entries = width * jax.random.normal(stream_key, shape, jnp.float32)
    if shards:
        entries = entries * block_scale(stream_key, shape, shards, -0.22, 0.18)
    return jnp.clip(entries, -limit, limit).astype(kind)


def setup_inputs(seed: int = 0) -> dict:
    splits = jax.random.split(jax.random.key(seed), 15)
    tokens = bell_draw(splits[0], (TOKENS, MODEL_WIDTH), 1.0, 6.0, ((0, 8),))
    seq_lengths = jax.vmap(lambda own: uneven(own, SEQ_ROW, TOKENS_PER_ROW, MOST_LEN, 2))(jax.random.split(splits[1], ROWS)).reshape((ROWS, SEQ_ROW)).astype(jnp.int32)
    attn_gain = jnp.clip(1.0 + 0.18 * jax.random.normal(splits[2], (MODEL_WIDTH,), jnp.float32), 0.1, 1.9)
    w_query = bell_draw(splits[3], (MODEL_WIDTH, QUERY_HEADS * HEAD_SIZE), MODEL_WIDTH ** -0.5, 0.125, ((1, 4),))
    key_weight = bell_draw(splits[4], (MODEL_WIDTH, KEY_VALUE_HEADS * HEAD_SIZE), MODEL_WIDTH ** -0.5, 0.125, ((1, 4),))
    value_weight = bell_draw(splits[5], (MODEL_WIDTH, KEY_VALUE_HEADS * HEAD_SIZE), MODEL_WIDTH ** -0.5, 0.125, ((1, 4),))
    query_gain = jnp.clip(1.0 + 0.18 * jax.random.normal(splits[6], (HEAD_SIZE,), jnp.float32), 0.1, 1.9)
    key_norm_gain = jnp.clip(1.0 + 0.18 * jax.random.normal(splits[7], (HEAD_SIZE,), jnp.float32), 0.1, 1.9)
    w_output = bell_draw(splits[8], (QUERY_HEADS * HEAD_SIZE, MODEL_WIDTH), (QUERY_HEADS * HEAD_SIZE // 16) ** -0.5, 0.5, ((0, 4),))
    mlp_gain = jnp.clip(1.0 + 0.18 * jax.random.normal(splits[9], (MODEL_WIDTH,), jnp.float32), 0.1, 1.9)
    w_gate = bell_draw(splits[10], (MODEL_WIDTH, FF), MODEL_WIDTH ** -0.5, 0.125, ((1, 4),))
    w_up = bell_draw(splits[11], (MODEL_WIDTH, FF), MODEL_WIDTH ** -0.5, 0.125, ((1, 4),))
    w_down = bell_draw(splits[12], (FF, MODEL_WIDTH), FF ** -0.5, 0.078125, ((0, 4),))
    cotangent = bell_draw(splits[13], (TOKENS, MODEL_WIDTH), 1.0, 6.0, ((0, 8),))
    return {"tokens": tokens, "seq_lengths": seq_lengths, "attn_gain": attn_gain, "w_query": w_query, "key_weight": key_weight, "value_weight": value_weight, "query_gain": query_gain, "key_norm_gain": key_norm_gain, "w_output": w_output, "mlp_gain": mlp_gain, "w_gate": w_gate, "w_up": w_up, "w_down": w_down, "cotangent": cotangent}


@jax.custom_vjp
def lowered_copy(v):
    return lax.optimization_barrier(v.astype(jnp.bfloat16)).astype(jnp.float32)

@jax.custom_vjp
def low_back(v):
    return v

def low_keep(v):
    return (lowered_copy(v), None)

def low_pass(kept, grad):
    return (grad,)

def back_keep(v):
    return (v, None)

def back_low(kept, grad):
    return (lowered_copy(grad),)
lowered_copy.defvjp(low_keep, low_pass)
low_back.defvjp(back_keep, back_low)
norm_eps = 1e-06
rope_base = 1000000.0
masked_score = -1e+30
highest = lax.Precision.HIGHEST

def root_mean_scale(values, gain):
    return values * lax.rsqrt(lax.optimization_barrier(jnp.mean(values * values, axis=-1, keepdims=True)) + norm_eps) * gain

def rotate_pairs(values, cosine_table, sine_table):
    half_width = values.shape[-1] // 2
    turned = jnp.concatenate([-values[..., half_width:], values[..., :half_width]], axis=-1)
    return values * cosine_table + turned * sine_table

def layout(seq_lengths, row_len):
    seq_ends = jnp.cumsum(seq_lengths, axis=-1)
    starts = seq_ends - seq_lengths
    places = jnp.arange(row_len, dtype=jnp.int32)
    segment_index = lax.optimization_barrier(jnp.sum((places[None, :, None] >= seq_ends[:, None, :]).astype(jnp.int32), axis=-1))
    belongs = segment_index[:, :, None] == jnp.arange(seq_lengths.shape[-1], dtype=jnp.int32)[None, None, :]
    seq_start = lax.optimization_barrier(jnp.sum(jnp.where(belongs, starts[:, None, :], 0), axis=-1))
    return (segment_index, places[None, :] - seq_start)

def tables(token_positions, head_dim):
    half_width = head_dim // 2
    frequency = rope_base ** (-2.0 * jnp.arange(half_width, dtype=jnp.float32) / head_dim)
    angles = token_positions.astype(jnp.float32)[:, None] * frequency[None, :]
    angles = jnp.concatenate([angles, angles], axis=-1)
    return (jnp.cos(angles)[:, None, :], jnp.sin(angles)[:, None, :])

def attend_causal(bundle):
    query_rows, key_rows, value_rows, segment_index, token_positions = bundle
    score_scale = query_rows.shape[-1] ** (-0.5)
    scores = low_back(jnp.einsum('tkgd,skd->kgts', query_rows, key_rows, precision=highest) * score_scale)
    allowed = (segment_index[:, None] == segment_index[None, :]) & (token_positions[:, None] >= token_positions[None, :])
    scores = jnp.where(allowed[None, None], scores, masked_score)
    top_score = lax.optimization_barrier(jnp.max(scores, axis=-1, keepdims=True))
    weights = jnp.exp(scores - top_score)
    weights = weights / lax.optimization_barrier(jnp.sum(weights, axis=-1, keepdims=True))
    return jnp.einsum('kgts,skd->tkgd', lowered_copy(weights), value_rows, precision=highest)

def forward(tokens32, attn_gain, w_query, key_weight, value_weight, query_gain, key_norm_gain, w_output, mlp_gain, w_gate, w_up, w_down, segment_index, token_positions):
    token_count = tokens32.shape[0]
    row_number = token_count // TOKENS_PER_ROW
    group_width = QUERY_HEADS // KEY_VALUE_HEADS
    cosine_table, sine_table = tables(token_positions.reshape(-1), HEAD_SIZE)
    normed = lowered_copy(root_mean_scale(tokens32, attn_gain))
    query_proj = low_back(jnp.dot(normed, w_query, precision=highest))
    key_projected = low_back(jnp.dot(normed, key_weight, precision=highest))
    value_projected = low_back(lowered_copy(jnp.dot(normed, value_weight, precision=highest)))
    query_head_rows = lowered_copy(rotate_pairs(root_mean_scale(query_proj.reshape(token_count, QUERY_HEADS, HEAD_SIZE), query_gain), cosine_table, sine_table))
    key_head_rows = lowered_copy(rotate_pairs(root_mean_scale(key_projected.reshape(token_count, KEY_VALUE_HEADS, HEAD_SIZE), key_norm_gain), cosine_table, sine_table))
    mixed_heads = lax.map(jax.checkpoint(attend_causal), (query_head_rows.reshape(row_number, TOKENS_PER_ROW, KEY_VALUE_HEADS, group_width, HEAD_SIZE), key_head_rows.reshape(row_number, TOKENS_PER_ROW, KEY_VALUE_HEADS, HEAD_SIZE), value_projected.reshape(row_number, TOKENS_PER_ROW, KEY_VALUE_HEADS, HEAD_SIZE), segment_index, token_positions))
    context = low_back(lowered_copy(mixed_heads.reshape(token_count, QUERY_HEADS * HEAD_SIZE)))
    hidden = tokens32 + low_back(jnp.dot(context, w_output, precision=highest))
    mlp_in = lowered_copy(root_mean_scale(hidden, mlp_gain))
    gate_act = low_back(jnp.dot(mlp_in, w_gate, precision=highest))
    up_act = low_back(jnp.dot(mlp_in, w_up, precision=highest))
    inner_act = lowered_copy(jax.nn.silu(gate_act) * up_act)
    return hidden + low_back(jnp.dot(inner_act, w_down, precision=highest))

def reference(tokens, seq_lengths, attn_gain, w_query, key_weight, value_weight, query_gain, key_norm_gain, w_output, mlp_gain, w_gate, w_up, w_down, cotangent):
    segment_index, token_positions = layout(seq_lengths, TOKENS_PER_ROW)

    def run(tokens32, attn32, query32, key32, value32, qgain32, kgain32, output32, mgain32, gate32, up32, down32):
        return forward(tokens32, attn32, query32, key32, value32, qgain32, kgain32, output32, mgain32, gate32, up32, down32, segment_index, token_positions)
    result, pullback = jax.vjp(run, tokens.astype(jnp.float32), attn_gain.astype(jnp.float32), w_query.astype(jnp.float32), key_weight.astype(jnp.float32), value_weight.astype(jnp.float32), query_gain.astype(jnp.float32), key_norm_gain.astype(jnp.float32), w_output.astype(jnp.float32), mlp_gain.astype(jnp.float32), w_gate.astype(jnp.float32), w_up.astype(jnp.float32), w_down.astype(jnp.float32))
    grads = pullback(cotangent.astype(jnp.float32))
    return (result.astype(jnp.bfloat16), grads[0].astype(jnp.bfloat16), grads[1], grads[2], grads[3], grads[4], grads[5], grads[6], grads[7], grads[8], grads[9], grads[10], grads[11])
```

```python
import jax
import jax.numpy as jnp
from jax import lax
from jax.experimental import pallas as pl
from jax.experimental.pallas import tpu as pltpu
from jax.sharding import PartitionSpec as P

norm_eps = 1e-06
rope_base = 1000000.0
masked_score = -1e30
bf16 = jnp.bfloat16
f32 = jnp.float32


def inverse_rms(values):
    return lax.rsqrt(jnp.mean(values * values, axis=-1, keepdims=True) + norm_eps)


def root_mean_scale(values, gain):
    return values * inverse_rms(values) * gain


def rotate_pairs(values, cosine_table, sine_table):
    half_width = values.shape[-1] // 2
    turned = jnp.concatenate([-values[..., half_width:], values[..., :half_width]], axis=-1)
    return values * cosine_table + turned * sine_table


def layout(seq_lengths, row_len):
    seq_ends = jnp.cumsum(seq_lengths, axis=-1)
    starts = seq_ends - seq_lengths
    places = jnp.arange(row_len, dtype=jnp.int32)
    segment_index = jnp.sum(
        (places[None, :, None] >= seq_ends[:, None, :]).astype(jnp.int32), axis=-1
    )
    belongs = (
        segment_index[:, :, None]
        == jnp.arange(seq_lengths.shape[-1], dtype=jnp.int32)[None, None, :]
    )
    seq_start = jnp.sum(jnp.where(belongs, starts[:, None, :], 0), axis=-1)
    return (segment_index, places[None, :] - seq_start)


def tables(token_positions, head_dim):
    half_width = head_dim // 2
    frequency = rope_base ** (-2.0 * jnp.arange(half_width, dtype=f32) / head_dim)
    angles = token_positions.astype(f32)[:, None] * frequency[None, :]
    angles = jnp.concatenate([angles, angles], axis=-1)
    return (jnp.cos(angles)[:, None, :], jnp.sin(angles)[:, None, :])


def swiglu(gate_act, up_act):
    return jax.nn.silu(gate_act) * up_act


def forward_dot(left_side, right_side):
    return jnp.dot(left_side, right_side, preferred_element_type=f32)


def outer_sum(left_side, right_side):
    return lax.dot_general(
        left_side, right_side, (((0,), (0,)), ((), ())), preferred_element_type=f32
    )


def back_dot(left_side, right_side):
    return lax.dot_general(
        left_side, right_side, (((1,), (1,)), ((), ())), preferred_element_type=f32
    )


def score_block(query_low, key_low, allowed, score_scale):
    scores = (
        jnp.einsum("tkgd,skd->kgts", query_low, key_low, preferred_element_type=f32)
        * score_scale
    )
    return jnp.where(allowed[None, None], scores, masked_score)


MESH = pl.DeviceIdType.MESH
any_space = pl.BlockSpec(memory_space=pl.ANY)
in_vmem = pl.BlockSpec(memory_space=pltpu.VMEM)


def nt_dot(left_side, right_side):
    return lax.dot_general(
        left_side, right_side, (((1,), (1,)), ((), ())), preferred_element_type=f32
    )


def fetch(source, target, sem):
    copy = pltpu.make_async_copy(source, target, sem)
    copy.start()
    return copy


class Spot:
    def __init__(self, wide):
        self.line = wide // 2
        self.w = lax.axis_index("wide")
        self.n = lax.axis_index("narrow")
        self.spot = lax.div(self.w, 2)
        self.side = lax.rem(self.w, 2)
        self.core = lax.rem(self.n, 2)
        self.chip = lax.div(self.n, 2)
        self.to_core = {"narrow": self.n + 1 - 2 * self.core}
        self.to_chip = {"narrow": self.n + 2 - 4 * self.chip}
        self.to_side = {"wide": self.w + 1 - 2 * self.side}
        self.to_up = {"wide": self.w + 2}
        self.to_down = {"wide": self.w - 2}

    def greet(self, wide_too):
        barrier = pltpu.get_barrier_semaphore()

        def tell(who):
            pl.semaphore_signal(barrier, inc=1, device_id=who, device_id_type=MESH)

        tell(self.to_core)
        tell(self.to_chip)
        if wide_too:
            tell(self.to_side)
            pl.when(self.spot > 0)(lambda: tell(self.to_down))
            pl.when(self.spot < self.line - 1)(lambda: tell(self.to_up))
        peers = 2
        if wide_too:
            ends = (self.spot == 0).astype(jnp.int32) + (self.spot == self.line - 1).astype(jnp.int32)
            peers = 5 - ends
        pl.semaphore_wait(barrier, peers)


def remote(source, target, send, recv, who):
    return pltpu.make_async_remote_copy(
        src_ref=source, dst_ref=target, send_sem=send, recv_sem=recv,
        device_id=who, device_id_type=MESH,
    )


class WideSum:
    ahead = 4

    @staticmethod
    def lands(tiles, line, rows, cols):
        return [
            jax.ShapeDtypeStruct((tiles, line, 2, rows, cols), f32),
            jax.ShapeDtypeStruct((tiles, line, rows, cols), f32),
            jax.ShapeDtypeStruct((tiles, line, rows, cols), f32),
            jax.ShapeDtypeStruct((tiles, line, rows, cols), f32),
            jax.ShapeDtypeStruct((tiles, rows, cols), f32),
        ]

    @staticmethod
    def sems(tiles):
        dma = pltpu.SemaphoreType.DMA
        return [dma((tiles,)), dma((tiles,)), dma((2,)), dma((tiles,)), dma((2,)), dma((tiles,)), dma((6,))]

    @staticmethod
    def buffers(line, rows, cols):
        tile = (line, rows, cols)
        return [
            pltpu.VMEM(tile, f32),
            pltpu.VMEM(tile, f32),
            pltpu.VMEM((line + 3,) + tile, f32),
            pltpu.VMEM((2, line - 1, rows, cols), f32),
            pltpu.VMEM((2, line - 1, rows, cols), f32),
            pltpu.VMEM((line - 1, rows, cols), f32),
            pltpu.VMEM((line - 1, rows, cols), f32),
            pltpu.VMEM((3, rows, cols), f32),
        ]

    def __init__(self, me, lands, sems):
        self.me = me
        self.parts, self.y_land, self.up_land, self.down_land, self.result = lands
        (self.y_send, self.y_recv, self.up_send, self.up_recv,
         self.down_send, self.down_recv, self.local) = sems
        self.tiles, self.line = self.parts.shape[0], me.line

    def y_copy(self, tile):
        return remote(
            self.parts.at[tile, :, 1 - self.me.side], self.y_land.at[tile],
            self.y_send.at[tile], self.y_recv.at[tile], self.me.to_side,
        )

    def up_copy(self, tile, count):
        slot = lax.rem(tile, 2)
        return remote(
            self.up_buf.at[slot, 0:count], self.up_land.at[tile, 0:count],
            self.up_send.at[slot], self.up_recv.at[tile], self.me.to_up,
        )

    def down_copy(self, tile, count):
        slot = lax.rem(tile, 2)
        return remote(
            self.down_buf.at[slot, 0:count], self.down_land.at[tile, 0:count],
            self.down_send.at[slot], self.down_recv.at[tile], self.me.to_down,
        )

    def await_up(self, tile, count):
        land = self.up_land.at[tile, 0:count]
        remote(land, land, self.up_send.at[0], self.up_recv.at[tile], self.me.to_up).wait_recv()

    def await_down(self, tile, count):
        land = self.down_land.at[tile, 0:count]
        remote(
            land, land, self.down_send.at[0], self.down_recv.at[tile], self.me.to_down
        ).wait_recv()

    @property
    def slots(self):
        return self.tiles + self.line + 2

    def use(self, buffers):
        (self.own, self.got, self.ring, self.up_buf, self.down_buf,
         self.up_load, self.down_load, self.last) = buffers

    def step(self, s):
        me, line, tiles = self.me, self.line, self.tiles
        depth = self.ring.shape[0]

        @pl.when(s + self.ahead < tiles)
        def _():
            self.y_copy(s + self.ahead).start()

        @pl.when(s < tiles)
        def _():
            self.y_copy(s).wait()
            a = fetch(self.parts.at[s, :, me.side], self.own, self.local.at[0])
            b = fetch(self.y_land.at[s], self.got, self.local.at[1])
            a.wait()
            b.wait()
            self.ring[lax.rem(s, depth)] = self.own[...] + self.got[...]

        for k in range(line - 1):
            tile, count = s - 1 - k, line - 1 - k

            @pl.when((me.spot == k) & (tile >= 0) & (tile < tiles))
            def _(k=k, tile=tile, count=count):
                slot, held = lax.rem(tile, 2), lax.rem(tile, depth)

                @pl.when(tile >= 2)
                def _():
                    self.up_copy(tile, count).wait_send()

                if k > 0:
                    self.await_up(tile, count + 1)
                    fetch(
                        self.up_land.at[tile, 1 : count + 1], self.up_load.at[0:count],
                        self.local.at[2],
                    ).wait()
                    self.up_buf[slot, 0:count] = (
                        self.ring[held, k + 1 : line] + self.up_load[0:count]
                    )
                else:
                    self.up_buf[slot, 0:count] = self.ring[held, k + 1 : line]
                self.up_copy(tile, count).start()

        for k in range(1, line):
            tile, count = s - 1 - (line - 1 - k), k

            @pl.when((me.spot == k) & (tile >= 0) & (tile < tiles))
            def _(k=k, tile=tile, count=count):
                slot, held = lax.rem(tile, 2), lax.rem(tile, depth)

                @pl.when(tile >= 2)
                def _():
                    self.down_copy(tile, count).wait_send()

                if k < line - 1:
                    self.await_down(tile, count + 1)
                    fetch(
                        self.down_land.at[tile, 0:count], self.down_load.at[0:count],
                        self.local.at[3],
                    ).wait()
                    self.down_buf[slot, 0:count] = (
                        self.ring[held, 0:count] + self.down_load[0:count]
                    )
                else:
                    self.down_buf[slot, 0:count] = self.ring[held, 0:count]
                self.down_copy(tile, count).start()

        tile = s - 1 - line

        @pl.when((tile >= 0) & (tile < tiles))
        def _():
            held = lax.rem(tile, depth)
            self.last[2] = self.ring[held, me.spot]

            @pl.when(me.spot == line - 1)
            def _():
                self.await_up(tile, 1)

            @pl.when(me.spot == 0)
            def _():
                self.await_down(tile, 1)

            @pl.when(me.spot > 0)
            def _():
                fetch(self.up_land.at[tile, 0], self.last.at[0], self.local.at[4]).wait()
                self.last[2] = self.last[2] + self.last[0]

            @pl.when(me.spot < line - 1)
            def _():
                fetch(self.down_land.at[tile, me.spot], self.last.at[1], self.local.at[5]).wait()
                self.last[2] = self.last[2] + self.last[1]

            fetch(self.last.at[2], self.result.at[tile], self.local.at[4]).wait()

    def finish(self):
        me, line = self.me, self.line
        for k in range(line - 1):
            @pl.when(me.spot == k)
            def _(k=k):
                for tile in range(max(0, self.tiles - 2), self.tiles):
                    self.up_copy(tile, line - 1 - k).wait_send()

        for k in range(1, line):
            @pl.when(me.spot == k)
            def _(k=k):
                for tile in range(max(0, self.tiles - 2), self.tiles):
                    self.down_copy(tile, k).wait_send()


class NarrowSum:
    @staticmethod
    def lands(chunks, quarter, width):
        return [
            jax.ShapeDtypeStruct((chunks, 2, quarter, width), f32),
            jax.ShapeDtypeStruct((chunks, quarter, width), f32),
            jax.ShapeDtypeStruct((chunks, quarter, width), f32),
            jax.ShapeDtypeStruct((chunks, 2, quarter, width), f32),
        ]

    @staticmethod
    def sems(chunks):
        dma = pltpu.SemaphoreType.DMA
        return [dma((chunks,)) for _ in range(8)] + [dma((5,))]

    @staticmethod
    def buffers(quarter, width):
        return [
            pltpu.VMEM((2, 2, 2, quarter, width), f32),
            pltpu.VMEM((2, quarter, width), f32),
            pltpu.VMEM((2, 2, quarter, width), f32),
            pltpu.VMEM((quarter, width), f32),
            pltpu.VMEM((2, quarter, width), f32),
            pltpu.VMEM((2, 2, quarter, width), f32),
            pltpu.VMEM((2, quarter, width), f32),
            pltpu.VMEM((2, 2, quarter, width), bf16),
        ]

    def __init__(self, me, lands, sems, out):
        self.me, self.out = me, out
        self.core_land, self.chip_land, self.back_land, self.last_land = lands
        (self.s0, self.r0, self.s1, self.r1, self.s2, self.r2, self.s3, self.r3, self.local) = sems
        self.chunks = self.chip_land.shape[0]

    def use(self, buffers):
        (self.part, self.core_load, self.half, self.chip_load,
         self.done, self.pair, self.last_load, self.low) = buffers

    def copies(self, stage, c):
        me, slot = self.me, lax.rem(c, 2)
        if stage == 0:
            return remote(self.part.at[slot, 1 - me.core], self.core_land.at[c],
                          self.s0.at[c], self.r0.at[c], me.to_core)
        if stage == 1:
            return remote(self.half.at[slot, 1 - me.chip], self.chip_land.at[c],
                          self.s1.at[c], self.r1.at[c], me.to_chip)
        if stage == 2:
            return remote(self.done.at[slot], self.back_land.at[c],
                          self.s2.at[c], self.r2.at[c], me.to_chip)
        return remote(self.pair.at[slot], self.last_land.at[c],
                      self.s3.at[c], self.r3.at[c], me.to_core)

    @property
    def slots(self):
        return self.chunks + 4

    def step(self, s, produce, work, lower):
        me = self.me

        def stage(number, body):
            c = s - number

            @pl.when((c >= 0) & (c < self.chunks))
            def _():
                if number > 0:
                    self.copies(number - 1, c).wait()
                body(c, lax.rem(c, 2))
                if number < 4:
                    self.copies(number, c).start()

        def four(c, slot):
            fetch(self.last_land.at[c], self.last_load, self.local.at[3]).wait()
            self.low[me.core] = lower(self.pair[slot])
            self.low[1 - me.core] = lower(self.last_load[...])
            fetch(self.low, self.out(c), self.local.at[4]).wait()

        def three(c, slot):
            fetch(self.back_land.at[c], self.pair.at[slot, 1 - me.chip], self.local.at[2]).wait()
            self.pair[slot, me.chip] = self.done[slot]

        def two(c, slot):
            fetch(self.chip_land.at[c], self.chip_load, self.local.at[1]).wait()
            self.done[slot] = work(c, self.half[slot, me.chip] + self.chip_load[...])

        def one(c, slot):
            fetch(self.core_land.at[c], self.core_load, self.local.at[0]).wait()
            self.half[slot] = self.part[slot, me.core] + self.core_load[...]

        def zero(c, slot):
            produce(c, self.part.at[slot])

        stage(4, four)
        stage(3, three)
        stage(2, two)
        stage(1, one)
        stage(0, zero)


def take(refs, count):
    return refs[:count], refs[count:]


def store_part(part, value, columns):
    half, quarter = 2, value.shape[0] // 4
    part[:, :, :, columns] = value.reshape(half, 2, quarter, value.shape[1])


def attend_out_kernel(wide, chunks, *refs):
    (context, w_output, tokens, gain), refs = take(refs, 4)
    (mlp_in, hidden_out), refs = take(refs, 2)
    lands, refs = take(refs, 4)
    sems, refs = take(refs, 9)
    buffers, refs = take(refs, 8)
    token_load, hidden_buf, sem = refs
    me = Spot(wide)
    me.greet(False)
    summing = NarrowSum(me, lands, sems, lambda c: mlp_in.at[c])
    summing.use(buffers)
    rows = context.shape[0] // chunks
    width = w_output.shape[1]
    step = min(512, width)

    def produce(c, part):
        left = context[pl.ds(pl.multiple_of(c * rows, rows), rows), :]
        for at in range(0, width, step):
            store_part(part, forward_dot(left, w_output[:, at : at + step]), slice(at, at + step))

    def work(c, total):
        fetch(tokens.at[c, me.core, me.chip], token_load, sem.at[0]).wait()
        hidden = token_load[...].astype(f32) + total
        hidden_buf[...] = hidden
        fetch(hidden_buf, hidden_out.at[c], sem.at[1]).wait()
        return hidden * inverse_rms(hidden)

    def lower(value):
        return (value * gain[...]).astype(bf16)

    def body(s, carry):
        summing.step(s, produce, work, lower)
        return carry

    lax.fori_loop(0, summing.slots, body, 0)


def norm_back(pulled, unit, scale, gain):
    scaled = pulled * gain
    return scale * (scaled - unit * jnp.mean(scaled * unit, axis=-1, keepdims=True))


def outer_tile(left_t, right, stage):
    line, _, rows, _ = stage.shape
    group = max(1, 512 // (2 * rows))
    while line % group:
        group -= 1

    def body(m, carry):
        at = pl.multiple_of(m * group * 2 * rows, group * 2 * rows)
        value = forward_dot(left_t[pl.ds(at, group * 2 * rows), :], right)
        stage[pl.ds(m * group, group)] = value.reshape((group, 2, rows, value.shape[1]))
        return carry

    lax.fori_loop(0, line // group, body, 0)


def mlp_kernel(wide, chunks, *refs):
    (mlp_in, mlp_in_t, cot, cot_t, cot_parts, hidden, w_gate, w_up, w_down, gain), refs = take(refs, 10)
    (output, attn_low, grad_hidden, gain_part), refs = take(refs, 4)
    wide_lands, refs = take(refs, 5)
    lands, refs = take(refs, 4)
    wide_sems, refs = take(refs, 7)
    sems, refs = take(refs, 9)
    acts, gain_sum, sem, w_sem, store_sem = refs
    me = Spot(wide)
    me.greet(True)
    tokens, width = mlp_in.shape
    hidden_units = w_gate.shape[1]
    cols = wide_lands[0].shape[-1]
    blocks = hidden_units // cols
    line, side_rows = wide_lands[0].shape[1], wide_lands[0].shape[3]
    total = WideSum(me, wide_lands, wide_sems)
    half = tokens // 2

    def compute(xs, xt, cs, ct, gate_w, up_w, down_w, staged):
        for at, (a, b) in enumerate(((mlp_in, xs), (mlp_in_t, xt), (cot, cs), (cot_t, ct))):
            fetch(a, b, sem.at[at])

        def weights(b, slot):
            at = pl.ds(pl.multiple_of(b * cols, cols), cols)
            return (
                pltpu.make_async_copy(w_gate.at[:, at], gate_w.at[slot], w_sem.at[slot, 0]),
                pltpu.make_async_copy(w_up.at[:, at], up_w.at[slot], w_sem.at[slot, 1]),
                pltpu.make_async_copy(w_down.at[at, :], down_w.at[slot], w_sem.at[slot, 2]),
            )

        for copy in weights(0, 0):
            copy.start()
        for at, (a, b) in enumerate(((mlp_in, xs), (mlp_in_t, xt), (cot, cs), (cot_t, ct))):
            pltpu.make_async_copy(a, b, sem.at[at]).wait()

        def store(tile):
            slot = lax.rem(tile, 2)
            return pltpu.make_async_copy(staged.at[slot], total.parts.at[tile], store_sem.at[slot])

        def block(b, carry):
            slot = lax.rem(b, 2)
            for copy in weights(b, slot):
                copy.wait()

            @pl.when(b + 1 < blocks)
            def _():
                for copy in weights(b + 1, 1 - slot):
                    copy.start()

            at = pl.ds(pl.multiple_of(b * cols, cols), cols)

            def rows(m, carry):
                own = pl.ds(pl.multiple_of(m * half, half), half)
                gate = forward_dot(xs[own, :], gate_w[slot])
                up = forward_dot(xs[own, :], up_w[slot])
                back = nt_dot(cs[own, :], down_w[slot])
                sig = 1.0 / (1.0 + jnp.exp(-gate))
                silu = gate * sig
                acts[0, own, at] = (silu * up).astype(bf16)
                acts[1, own, at] = (back * up * sig * (1.0 + gate * (1.0 - sig))).astype(bf16)
                acts[2, own, at] = (back * silu).astype(bf16)
                return carry

            lax.fori_loop(0, 2, rows, 0)
            for j in range(3):
                tile = 3 * b + j

                @pl.when(tile >= 2)
                def _(tile=tile):
                    store(tile - 2).wait()

                    @pl.when(tile - 2 < total.ahead)
                    def _():
                        total.y_copy(tile - 2).start()

                outer_tile(ct if j == 0 else xt, acts[j, :, at], staged.at[lax.rem(tile, 2)])
                store(tile).start()
            return carry

        lax.fori_loop(0, blocks, block, 0)
        for tile in range(total.tiles - 2, total.tiles):
            store(tile).wait()
            if tile < total.ahead:
                total.y_copy(tile).start()

    pl.run_scoped(
        compute,
        pltpu.VMEM(mlp_in.shape, bf16),
        pltpu.VMEM(mlp_in_t.shape, bf16),
        pltpu.VMEM(mlp_in.shape, bf16),
        pltpu.VMEM(mlp_in_t.shape, bf16),
        pltpu.VMEM((2, width, cols), bf16),
        pltpu.VMEM((2, width, cols), bf16),
        pltpu.VMEM((2, cols, width), bf16),
        pltpu.VMEM((2, line, 2, side_rows, cols), f32),
    )

    def pass_on(*held):
        wide_buffers, held = take(held, 8)
        buffers, held = take(held, 8)
        gate_w, up_w, down_w, hidden_load, cot_load, out_buf = held
        total.use(wide_buffers)
        step = gate_w.shape[1]
        rows = tokens // chunks

        def out(c):
            return both.at[c]

        both = output
        summing = NarrowSum(me, lands, sems, out)
        summing.use(buffers)
        gain_sum[...] = jnp.zeros_like(gain_sum)

        def produce(c, part):
            @pl.when(c < chunks)
            def _():
                own = pl.ds(pl.multiple_of(c * rows, rows), rows)

                def copies(at, slot):
                    cut = pl.ds(at * step, step)
                    return (
                        pltpu.make_async_copy(w_gate.at[cut, :], gate_w.at[slot], w_sem.at[slot, 0]),
                        pltpu.make_async_copy(w_up.at[cut, :], up_w.at[slot], w_sem.at[slot, 1]),
                    )

                count = width // step
                for copy in copies(0, 0):
                    copy.start()
                for at in range(count):
                    if at + 1 < count:
                        for copy in copies(at + 1, (at + 1) % 2):
                            copy.start()
                    for copy in copies(at, at % 2):
                        copy.wait()
                    value = nt_dot(acts[1, own, :], gate_w[at % 2])
                    value = value + nt_dot(acts[2, own, :], up_w[at % 2])
                    store_part(part, value, slice(at * step, (at + 1) * step))

            @pl.when(c >= chunks)
            def _():
                own = pl.ds(pl.multiple_of((c - chunks) * rows, rows), rows)

                def copy(at, slot):
                    cut = pl.ds(at * step, step)
                    return pltpu.make_async_copy(w_down.at[:, cut], down_w.at[slot], w_sem.at[slot, 2])

                count = width // step
                copy(0, 0).start()
                for at in range(count):
                    if at + 1 < count:
                        copy(at + 1, (at + 1) % 2).start()
                    copy(at, at % 2).wait()
                    value = forward_dot(acts[0, own, :], down_w[at % 2])
                    store_part(part, value, slice(at * step, (at + 1) * step))

        def work(c, pulled):
            chunk = lax.rem(c, chunks)
            a = fetch(hidden.at[chunk], hidden_load, sem.at[0])
            b = fetch(cot_parts.at[chunk, me.core, me.chip], cot_load, sem.at[1])
            a.wait()
            b.wait()

            @pl.when(c < chunks)
            def _():
                mid = hidden_load[...]
                scale = inverse_rms(mid)
                unit = mid * scale
                gain_sum[...] += jnp.sum(pulled * unit, axis=0, keepdims=True)
                grad = cot_load[...].astype(f32) + norm_back(pulled, unit, scale, gain[...])
                out_buf[...] = grad
                fetch(out_buf, grad_hidden.at[chunk], sem.at[2]).wait()

            @pl.when(c >= chunks)
            def _():
                out_buf[...] = hidden_load[...] + pulled

            return out_buf[...]

        def lower(value):
            return value.astype(bf16)

        def body(s, carry):
            pl.when(s < total.slots)(lambda: total.step(s))
            pl.when(s < summing.slots)(lambda: summing.step(s, produce, work, lower))
            return carry

        lax.fori_loop(0, max(total.slots, summing.slots), body, 0)
        total.finish()

    quarter = hidden.shape[1]
    step = min(256, width)
    pl.run_scoped(
        pass_on,
        *WideSum.buffers(line, side_rows, cols),
        *NarrowSum.buffers(quarter, width),
        pltpu.VMEM((2, step, hidden_units), bf16),
        pltpu.VMEM((2, step, hidden_units), bf16),
        pltpu.VMEM((2, hidden_units, step), bf16),
        pltpu.VMEM((quarter, width), f32),
        pltpu.VMEM((quarter, width), bf16),
        pltpu.VMEM((quarter, width), f32),
    )
    fetch(gain_sum, gain_part, sem.at[0]).wait()


def attn_grad_kernel(wide, chunks, *refs):
    (low_t, context, normed_t, grad_heads, weights, tokens, grad_hidden, gain), refs = take(refs, 8)
    (grad_tokens, gain_part), refs = take(refs, 2)
    wide_lands, refs = take(refs, 5)
    lands, refs = take(refs, 4)
    wide_sems, refs = take(refs, 7)
    sems, refs = take(refs, 9)
    gain_sum, sem, store_sem = refs
    me = Spot(wide)
    me.greet(True)
    width, count = low_t.shape
    cols = wide_lands[0].shape[-1]
    line, side_rows = wide_lands[0].shape[1], wide_lands[0].shape[3]
    total = WideSum(me, wide_lands, wide_sems)
    out_tiles = context.shape[1] // cols

    def compute(lt, nt, ctx, heads, staged):
        pairs = ((low_t, lt), (normed_t, nt), (context, ctx), (grad_heads, heads))
        for at, (a, b) in enumerate(pairs):
            fetch(a, b, sem.at[at])
        for at, (a, b) in enumerate(pairs):
            pltpu.make_async_copy(a, b, sem.at[at]).wait()

        def store(tile):
            slot = lax.rem(tile, 2)
            return pltpu.make_async_copy(staged.at[slot], total.parts.at[tile], store_sem.at[slot])

        def one(tile, left, right, at):
            @pl.when(tile >= 2)
            def _():
                store(tile - 2).wait()

                @pl.when(tile - 2 < total.ahead)
                def _():
                    total.y_copy(tile - 2).start()

            cut = pl.ds(pl.multiple_of(at * cols, cols), cols)
            outer_tile(left, right[:, cut], staged.at[lax.rem(tile, 2)])
            store(tile).start()

        def first(t, carry):
            one(t, lt, ctx, t)
            return carry

        def second(t, carry):
            one(t, nt, heads, t - out_tiles)
            return carry

        lax.fori_loop(0, out_tiles, first, 0)
        lax.fori_loop(out_tiles, total.tiles, second, 0)
        for tile in range(total.tiles - 2, total.tiles):
            store(tile).wait()
            if tile < total.ahead:
                total.y_copy(tile).start()

    pl.run_scoped(
        compute,
        pltpu.VMEM(low_t.shape, bf16),
        pltpu.VMEM(normed_t.shape, bf16),
        pltpu.VMEM(context.shape, bf16),
        pltpu.VMEM(grad_heads.shape, bf16),
        pltpu.VMEM((2, line, 2, side_rows, cols), f32),
    )

    def pass_on(*held):
        wide_buffers, held = take(held, 8)
        buffers, held = take(held, 8)
        heads, w_all, hidden_load, token_load = held
        total.use(wide_buffers)
        rows = count // chunks
        step = min(512, width)
        a = fetch(grad_heads, heads, sem.at[0])
        b = fetch(weights, w_all, sem.at[1])
        summing = NarrowSum(me, lands, sems, lambda c: grad_tokens.at[c])
        summing.use(buffers)
        gain_sum[...] = jnp.zeros_like(gain_sum)
        a.wait()
        b.wait()

        def produce(c, part):
            left = heads[pl.ds(pl.multiple_of(c * rows, rows), rows), :]
            for at in range(0, width, step):
                store_part(part, nt_dot(left, w_all[at : at + step, :]), slice(at, at + step))

        def work(c, pulled):
            a = fetch(grad_hidden.at[c], hidden_load, sem.at[0])
            b = fetch(tokens.at[c, me.core, me.chip], token_load, sem.at[1])
            a.wait()
            b.wait()
            mid = token_load[...].astype(f32)
            scale = inverse_rms(mid)
            unit = mid * scale
            gain_sum[...] += jnp.sum(pulled * unit, axis=0, keepdims=True)
            return hidden_load[...] + norm_back(pulled, unit, scale, gain[...])

        def lower(value):
            return value.astype(bf16)

        def body(s, carry):
            pl.when(s < total.slots)(lambda: total.step(s))
            pl.when(s < summing.slots)(lambda: summing.step(s, produce, work, lower))
            return carry

        lax.fori_loop(0, max(total.slots, summing.slots), body, 0)
        total.finish()

    quarter = grad_hidden.shape[1]
    pl.run_scoped(
        pass_on,
        *WideSum.buffers(line, side_rows, cols),
        *NarrowSum.buffers(quarter, width),
        pltpu.VMEM(grad_heads.shape, bf16),
        pltpu.VMEM(weights.shape, bf16),
        pltpu.VMEM((quarter, width), f32),
        pltpu.VMEM((quarter, width), bf16),
    )
    fetch(gain_sum, gain_part, sem.at[0]).wait()


def call(kernel, collective_id, out_shape, in_specs, out_specs, scratch, arrays, limit):
    return pl.pallas_call(
        kernel,
        out_shape=out_shape,
        in_specs=in_specs,
        out_specs=out_specs,
        scratch_shapes=scratch,
        compiler_params=pltpu.CompilerParams(
            collective_id=collective_id, has_side_effects=True, vmem_limit_bytes=limit
        ),
    )(*arrays)


def swap_cores(values):
    return lax.ppermute(values, "narrow", [(0, 1), (1, 0), (2, 3), (3, 2)])


def swap_chips(values):
    return lax.ppermute(values, "narrow", [(0, 2), (2, 0), (1, 3), (3, 1)])


def per_device(
    wide,
    tokens,
    seq_lengths,
    attn_gain,
    w_query,
    key_weight,
    value_weight,
    query_gain,
    key_norm_gain,
    w_output,
    mlp_gain,
    w_gate,
    w_up,
    w_down,
    cotangent,
):
    token_count, model_width = tokens.shape
    head_dim = query_gain.shape[0]
    kv_heads = key_weight.shape[1] // head_dim
    q_heads = w_query.shape[1] // head_dim
    group_width = q_heads // kv_heads
    score_scale = head_dim ** (-0.5)
    line = wide // 2
    side_rows = model_width // wide
    first_chunks, chunks = 8, 8
    dma = pltpu.SemaphoreType.DMA
    limit = 60 * 1024 * 1024

    segment_index, token_positions = layout(seq_lengths, token_count)
    segment_index = segment_index.reshape(-1)
    token_positions = token_positions.reshape(-1)
    allowed = (segment_index[:, None] == segment_index[None, :]) & (
        token_positions[:, None] >= token_positions[None, :]
    )
    cosine_table, sine_table = tables(token_positions, head_dim)

    def prepare(raw_heads, gain):
        return rotate_pairs(root_mean_scale(raw_heads, gain), cosine_table, sine_table)

    def parts_of(values, count):
        return values.reshape(count, 2, 2, token_count // count // 4, model_width)

    tokens32 = tokens.astype(f32)
    normed = (tokens32 * inverse_rms(tokens32) * attn_gain).astype(bf16)
    query_proj = forward_dot(normed, w_query)
    key_projected = forward_dot(normed, key_weight)
    value_low = (
        forward_dot(normed, value_weight).astype(bf16).reshape(token_count, kv_heads, head_dim)
    )
    query32, query_pull = jax.vjp(
        prepare, query_proj.reshape(token_count, q_heads, head_dim), query_gain
    )
    key32, key_pull = jax.vjp(
        prepare, key_projected.reshape(token_count, kv_heads, head_dim), key_norm_gain
    )
    query_low = query32.astype(bf16).reshape(token_count, kv_heads, group_width, head_dim)
    key_low = key32.astype(bf16)
    scores = score_block(query_low, key_low, allowed, score_scale)
    top_score = jnp.max(scores, axis=-1, keepdims=True)
    expd = jnp.exp(scores - top_score)
    row_total = jnp.sum(expd, axis=-1, keepdims=True)
    probs_low = (expd / row_total).astype(bf16)
    log_total = top_score + jnp.log(row_total)
    mixed_heads = jnp.einsum("kgts,skd->tkgd", probs_low, value_low, preferred_element_type=f32)
    context = mixed_heads.reshape(token_count, q_heads * head_dim).astype(bf16)

    quarter = token_count // first_chunks // 4
    outs = call(
        lambda *refs: attend_out_kernel(wide, first_chunks, *refs),
        1,
        [
            jax.ShapeDtypeStruct((first_chunks, 2, 2, quarter, model_width), bf16),
            jax.ShapeDtypeStruct((first_chunks, quarter, model_width), f32),
            *NarrowSum.lands(first_chunks, quarter, model_width),
        ],
        [in_vmem, in_vmem, any_space, in_vmem],
        [any_space] * 6,
        [
            *NarrowSum.sems(first_chunks),
            *NarrowSum.buffers(quarter, model_width),
            pltpu.VMEM((quarter, model_width), bf16),
            pltpu.VMEM((quarter, model_width), f32),
            dma((2,)),
        ],
        (context, w_output, parts_of(tokens, first_chunks), mlp_gain[None]),
        limit,
    )
    mlp_in = outs[0].reshape(token_count, model_width)
    hidden = outs[1]

    quarter = token_count // chunks // 4
    cols = min(256, w_gate.shape[1])
    order = first_chunks // chunks
    rows_held = token_count // first_chunks // 4

    def regroup(values):
        return (
            values.reshape(chunks, order, 2, 2, rows_held, model_width)
            .transpose(0, 2, 3, 1, 4, 5)
            .reshape(chunks, 2, 2, quarter, model_width)
        )

    def restore(values):
        return (
            values.reshape(chunks, 2, 2, order, rows_held, model_width)
            .transpose(0, 3, 1, 2, 4, 5)
            .reshape(token_count, model_width)
        )

    cot_parts = regroup(cotangent)
    token_parts = regroup(tokens)
    mlp_rows = regroup(mlp_in).reshape(token_count, model_width)
    cot_rows = cot_parts.reshape(token_count, model_width)
    tiles = 3 * (w_gate.shape[1] // cols)
    outs = call(
        lambda *refs: mlp_kernel(wide, chunks, *refs),
        2,
        [
            jax.ShapeDtypeStruct((2 * chunks, 2, 2, quarter, model_width), bf16),
            jax.ShapeDtypeStruct((8, 128), bf16),
            jax.ShapeDtypeStruct((chunks, quarter, model_width), f32),
            jax.ShapeDtypeStruct((1, model_width), f32),
            *WideSum.lands(tiles, line, side_rows, cols),
            *NarrowSum.lands(2 * chunks, quarter, model_width),
        ],
        [any_space] * 9 + [in_vmem],
        [any_space] * 13,
        [
            *WideSum.sems(tiles),
            *NarrowSum.sems(2 * chunks),
            pltpu.VMEM((3, token_count, w_gate.shape[1]), bf16),
            pltpu.VMEM((1, model_width), f32),
            dma((4,)),
            dma((2, 3)),
            dma((2,)),
        ],
        (
            mlp_rows,
            mlp_rows.T,
            cot_rows,
            cot_rows.T,
            cot_parts,
            hidden.reshape(chunks, quarter, model_width),
            w_gate,
            w_up,
            w_down,
            mlp_gain[None],
        ),
        limit,
    )
    attn_rows = outs[0][:chunks]
    output = restore(outs[0][chunks:])
    grad_hidden, mlp_gain_part, mlp_tiles = outs[2], outs[3][0], outs[8]
    attn_low = restore(attn_rows)

    grad_context = (
        back_dot(attn_low, w_output)
        .astype(bf16)
        .reshape(token_count, kv_heads, group_width, head_dim)
    )
    again = score_block(query_low, key_low, allowed, score_scale)
    probs = jnp.exp(again - log_total)
    again_low = probs.astype(bf16)
    grad_value = jnp.einsum("kgts,tkgd->skd", again_low, grad_context, preferred_element_type=f32)
    grad_probs = jnp.einsum("tkgd,skd->kgts", grad_context, value_low, preferred_element_type=f32)
    grad_scores = probs * (grad_probs - jnp.sum(probs * grad_probs, axis=-1, keepdims=True))
    scores_low = grad_scores.astype(bf16)
    grad_query_heads = (
        jnp.einsum("kgts,skd->tkgd", scores_low, key_low, preferred_element_type=f32) * score_scale
    )
    grad_key_heads = (
        jnp.einsum("kgts,tkgd->skd", scores_low, query_low, preferred_element_type=f32)
        * score_scale
    )
    grad_query32, query_gain_part = query_pull(
        grad_query_heads.reshape(token_count, q_heads, head_dim)
    )
    grad_key32, key_gain_part = key_pull(grad_key_heads)
    grad_query_proj = grad_query32.reshape(token_count, q_heads * head_dim).astype(bf16)
    grad_key_proj = grad_key32.reshape(token_count, kv_heads * head_dim).astype(bf16)
    grad_value_low = grad_value.reshape(token_count, kv_heads * head_dim).astype(bf16)
    grad_heads = jnp.concatenate([grad_query_proj, grad_key_proj, grad_value_low], axis=1)
    head_weights = jnp.concatenate([w_query, key_weight, value_weight], axis=1)

    def regroup_heads(values):
        return (
            values.reshape(chunks, order, 2, 2, rows_held, -1)
            .transpose(0, 2, 3, 1, 4, 5)
            .reshape(token_count, -1)
        )

    tiles = (context.shape[1] + grad_heads.shape[1]) // cols
    outs = call(
        lambda *refs: attn_grad_kernel(wide, chunks, *refs),
        3,
        [
            jax.ShapeDtypeStruct((chunks, 2, 2, quarter, model_width), bf16),
            jax.ShapeDtypeStruct((1, model_width), f32),
            *WideSum.lands(tiles, line, side_rows, cols),
            *NarrowSum.lands(chunks, quarter, model_width),
        ],
        [any_space] * 7 + [in_vmem],
        [any_space] * 11,
        [
            *WideSum.sems(tiles),
            *NarrowSum.sems(chunks),
            pltpu.VMEM((1, model_width), f32),
            dma((4,)),
            dma((2,)),
        ],
        (
            attn_rows.reshape(token_count, model_width).T,
            regroup_heads(context),
            regroup(normed).reshape(token_count, model_width).T,
            regroup_heads(grad_heads),
            head_weights,
            token_parts,
            grad_hidden,
            attn_gain[None],
        ),
        limit,
    )
    grad_tokens = restore(outs[0])
    attn_gain_part, attn_tiles = outs[1][0], outs[6]

    blocks = w_gate.shape[1] // cols
    mlp_tiles = mlp_tiles.reshape(blocks, 3, side_rows, cols)
    shard_down = mlp_tiles[:, 0].transpose(0, 2, 1).reshape(blocks * cols, side_rows)
    shard_gate = mlp_tiles[:, 1].transpose(1, 0, 2).reshape(side_rows, blocks * cols)
    shard_up = mlp_tiles[:, 2].transpose(1, 0, 2).reshape(side_rows, blocks * cols)
    out_tiles = context.shape[1] // cols
    shard_output = attn_tiles[:out_tiles].transpose(0, 2, 1).reshape(context.shape[1], side_rows)
    shard_heads = attn_tiles[out_tiles:].transpose(1, 0, 2).reshape(side_rows, -1)
    query_width, kv_width = w_query.shape[1], key_weight.shape[1]
    shard_query = shard_heads[:, :query_width]
    shard_key = shard_heads[:, query_width : query_width + kv_width]
    shard_value = shard_heads[:, query_width + kv_width :]

    gains = jnp.concatenate(
        [
            v.reshape(wide, -1)
            for v in (attn_gain_part, mlp_gain_part, query_gain_part, key_gain_part)
        ],
        axis=1,
    )
    gains = lax.psum(gains, ("wide", "narrow"))
    gains = lax.dynamic_index_in_dim(gains, lax.axis_index("wide"), 0, keepdims=False)
    wide_width, head_width = model_width // wide, head_dim // wide
    shard_attn_gain = gains[:wide_width]
    shard_mlp_gain = gains[wide_width : 2 * wide_width]
    shard_query_gain = gains[2 * wide_width : 2 * wide_width + head_width]
    shard_key_gain = gains[2 * wide_width + head_width :]
    return (
        output,
        grad_tokens,
        shard_attn_gain,
        shard_query,
        shard_key,
        shard_value,
        shard_query_gain,
        shard_key_gain,
        shard_output,
        shard_mlp_gain,
        shard_gate,
        shard_up,
        shard_down,
    )


def solution(mesh):
    def run(*arrays):
        return per_device(mesh.shape["wide"], *arrays)

    return jax.shard_map(
        run,
        mesh=mesh,
        in_specs=(
            P("wide", None),
            P("wide", None),
            P(),
            P(None, "narrow"),
            P(None, "narrow"),
            P(None, "narrow"),
            P(),
            P(),
            P("narrow", None),
            P(),
            P(None, "narrow"),
            P(None, "narrow"),
            P("narrow", None),
            P("wide", None),
        ),
        out_specs=(
            P("wide", None),
            P("wide", None),
            P("wide"),
            P("wide", "narrow"),
            P("wide", "narrow"),
            P("wide", "narrow"),
            P("wide"),
            P("wide"),
            P("narrow", "wide"),
            P("wide"),
            P("wide", "narrow"),
            P("wide", "narrow"),
            P("narrow", "wide"),
        ),
        check_vma=False,
    )
```

```python
import functools

import jax
import jax.numpy as jnp
from jax import lax
from jax.experimental import pallas as pl
from jax.experimental.pallas import tpu as pltpu
from jax.sharding import PartitionSpec as P

norm_eps = 1e-06
rope_base = 1000000.0
masked_score = -1e30
bf16 = jnp.bfloat16
f32 = jnp.float32


def inverse_rms(values):
    return lax.rsqrt(jnp.mean(values * values, axis=-1, keepdims=True) + norm_eps)


def layout(seq_lengths, row_len):
    seq_ends = jnp.cumsum(seq_lengths, axis=-1)
    starts = seq_ends - seq_lengths
    places = jnp.arange(row_len, dtype=jnp.int32)
    segment_index = jnp.sum(
        (places[None, :, None] >= seq_ends[:, None, :]).astype(jnp.int32), axis=-1
    )
    belongs = (
        segment_index[:, :, None]
        == jnp.arange(seq_lengths.shape[-1], dtype=jnp.int32)[None, None, :]
    )
    seq_start = jnp.sum(jnp.where(belongs, starts[:, None, :], 0), axis=-1)
    return (segment_index, places[None, :] - seq_start)


def tables(token_positions, head_dim):
    half_width = head_dim // 2
    frequency = rope_base ** (-2.0 * jnp.arange(half_width, dtype=f32) / head_dim)
    angles = token_positions.astype(f32)[:, None] * frequency[None, :]
    angles = jnp.concatenate([angles, angles], axis=-1)
    return (jnp.cos(angles)[:, None, :], jnp.sin(angles)[:, None, :])


def forward_dot(left_side, right_side):
    return jnp.dot(left_side, right_side, preferred_element_type=f32)


MESH = pl.DeviceIdType.MESH
any_space = pl.BlockSpec(memory_space=pl.ANY)
in_vmem = pl.BlockSpec(memory_space=pltpu.VMEM)


def nt_dot(left_side, right_side):
    return lax.dot_general(
        left_side, right_side, (((1,), (1,)), ((), ())), preferred_element_type=f32
    )


def fetch(source, target, sem):
    copy = pltpu.make_async_copy(source, target, sem)
    copy.start()
    return copy


class Spot:
    def __init__(self, wide):
        self.line = wide // 2
        self.w = lax.axis_index("wide")
        self.n = lax.axis_index("narrow")
        self.spot = lax.div(self.w, 2)
        self.side = lax.rem(self.w, 2)
        self.core = lax.rem(self.n, 2)
        self.chip = lax.div(self.n, 2)
        self.to_core = {"narrow": self.n + 1 - 2 * self.core}
        self.to_chip = {"narrow": self.n + 2 - 4 * self.chip}
        self.to_side = {"wide": self.w + 1 - 2 * self.side}
        self.to_up = {"wide": self.w + 2}
        self.to_down = {"wide": self.w - 2}

    def along(self, distance):
        there = lax.rem(self.spot + distance, self.line)
        return {"wide": there * 2 + self.side}

    def greet(self, wide_too):
        barrier = pltpu.get_barrier_semaphore()

        def tell(who):
            pl.semaphore_signal(barrier, inc=1, device_id=who, device_id_type=MESH)

        tell(self.to_core)
        tell(self.to_chip)
        if wide_too:
            tell(self.to_side)
            for distance in range(1, self.line):
                tell(self.along(distance))
        pl.semaphore_wait(barrier, 2 + self.line if wide_too else 2)


def remote(source, target, send, recv, who):
    return pltpu.make_async_remote_copy(
        src_ref=source, dst_ref=target, send_sem=send, recv_sem=recv,
        device_id=who, device_id_type=MESH,
    )


class WideSum:
    ahead = 4

    @staticmethod
    def lands(tiles, line, rows, cols):
        return [
            jax.ShapeDtypeStruct((tiles, line, 2, rows, cols), f32),
            jax.ShapeDtypeStruct((tiles, line, rows, cols), f32),
            jax.ShapeDtypeStruct((tiles, line, rows, cols), f32),
            jax.ShapeDtypeStruct((tiles, line, rows, cols), f32),
        ]

    @staticmethod
    def sems(tiles):
        dma = pltpu.SemaphoreType.DMA
        return [dma((tiles,)), dma((tiles,)), dma((2,)), dma((tiles,)), dma((2,)), dma((tiles,)), dma((6,))]

    @staticmethod
    def buffers(line, rows, cols):
        tile = (line, rows, cols)
        return [
            pltpu.VMEM(tile, f32),
            pltpu.VMEM(tile, f32),
            pltpu.VMEM((line + 3,) + tile, f32),
            pltpu.VMEM((2, line - 1, rows, cols), f32),
            pltpu.VMEM((2, line - 1, rows, cols), f32),
            pltpu.VMEM((line - 1, rows, cols), f32),
            pltpu.VMEM((line - 1, rows, cols), f32),
            pltpu.VMEM((3, rows, cols), f32),
        ]

    def __init__(self, me, lands, sems):
        self.me = me
        self.parts, self.y_land, self.up_land, self.down_land = lands
        (self.y_send, self.y_recv, self.up_send, self.up_recv,
         self.down_send, self.down_recv, self.local) = sems
        self.tiles, self.line = self.parts.shape[0], me.line

    def y_copy(self, tile):
        return remote(
            self.parts.at[tile, :, 1 - self.me.side], self.y_land.at[tile],
            self.y_send.at[tile], self.y_recv.at[tile], self.me.to_side,
        )

    def up_copy(self, tile, count):
        slot = lax.rem(tile, 2)
        return remote(
            self.up_buf.at[slot, 0:count], self.up_land.at[tile, 0:count],
            self.up_send.at[slot], self.up_recv.at[tile], self.me.to_up,
        )

    def down_copy(self, tile, count):
        slot = lax.rem(tile, 2)
        return remote(
            self.down_buf.at[slot, 0:count], self.down_land.at[tile, 0:count],
            self.down_send.at[slot], self.down_recv.at[tile], self.me.to_down,
        )

    def await_up(self, tile, count):
        land = self.up_land.at[tile, 0:count]
        remote(land, land, self.up_send.at[0], self.up_recv.at[tile], self.me.to_up).wait_recv()

    def await_down(self, tile, count):
        land = self.down_land.at[tile, 0:count]
        remote(
            land, land, self.down_send.at[0], self.down_recv.at[tile], self.me.to_down
        ).wait_recv()

    @property
    def slots(self):
        return self.tiles + self.line + 2

    def use(self, buffers):
        (self.own, self.got, self.ring, self.up_buf, self.down_buf,
         self.up_load, self.down_load, self.last) = buffers

    def step(self, s, emit):
        me, line, tiles = self.me, self.line, self.tiles
        depth = self.ring.shape[0]

        @pl.when(s + self.ahead < tiles)
        def _():
            self.y_copy(s + self.ahead).start()

        @pl.when(s < tiles)
        def _():
            self.y_copy(s).wait()
            a = fetch(self.parts.at[s, :, me.side], self.own, self.local.at[0])
            b = fetch(self.y_land.at[s], self.got, self.local.at[1])
            a.wait()
            b.wait()
            self.ring[lax.rem(s, depth)] = self.own[...] + self.got[...]

        for k in range(line - 1):
            tile, count = s - 1 - k, line - 1 - k

            @pl.when((me.spot == k) & (tile >= 0) & (tile < tiles))
            def _(k=k, tile=tile, count=count):
                slot, held = lax.rem(tile, 2), lax.rem(tile, depth)

                @pl.when(tile >= 2)
                def _():
                    self.up_copy(tile, count).wait_send()

                if k > 0:
                    self.await_up(tile, count + 1)
                    fetch(
                        self.up_land.at[tile, 1 : count + 1], self.up_load.at[0:count],
                        self.local.at[2],
                    ).wait()
                    self.up_buf[slot, 0:count] = (
                        self.ring[held, k + 1 : line] + self.up_load[0:count]
                    )
                else:
                    self.up_buf[slot, 0:count] = self.ring[held, k + 1 : line]
                self.up_copy(tile, count).start()

        for k in range(1, line):
            tile, count = s - 1 - (line - 1 - k), k

            @pl.when((me.spot == k) & (tile >= 0) & (tile < tiles))
            def _(k=k, tile=tile, count=count):
                slot, held = lax.rem(tile, 2), lax.rem(tile, depth)

                @pl.when(tile >= 2)
                def _():
                    self.down_copy(tile, count).wait_send()

                if k < line - 1:
                    self.await_down(tile, count + 1)
                    fetch(
                        self.down_land.at[tile, 0:count], self.down_load.at[0:count],
                        self.local.at[3],
                    ).wait()
                    self.down_buf[slot, 0:count] = (
                        self.ring[held, 0:count] + self.down_load[0:count]
                    )
                else:
                    self.down_buf[slot, 0:count] = self.ring[held, 0:count]
                self.down_copy(tile, count).start()

        tile = s - 1 - line

        @pl.when((tile >= 0) & (tile < tiles))
        def _():
            held = lax.rem(tile, depth)
            self.last[2] = self.ring[held, me.spot]

            @pl.when(me.spot == line - 1)
            def _():
                self.await_up(tile, 1)

            @pl.when(me.spot == 0)
            def _():
                self.await_down(tile, 1)

            @pl.when(me.spot > 0)
            def _():
                fetch(self.up_land.at[tile, 0], self.last.at[0], self.local.at[4]).wait()
                self.last[2] = self.last[2] + self.last[0]

            @pl.when(me.spot < line - 1)
            def _():
                fetch(self.down_land.at[tile, me.spot], self.last.at[1], self.local.at[5]).wait()
                self.last[2] = self.last[2] + self.last[1]

            emit(tile, self.last.at[2])

    def finish(self):
        me, line = self.me, self.line
        for k in range(line - 1):
            @pl.when(me.spot == k)
            def _(k=k):
                for tile in range(max(0, self.tiles - 2), self.tiles):
                    self.up_copy(tile, line - 1 - k).wait_send()

        for k in range(1, line):
            @pl.when(me.spot == k)
            def _(k=k):
                for tile in range(max(0, self.tiles - 2), self.tiles):
                    self.down_copy(tile, k).wait_send()


class NarrowSum:
    @staticmethod
    def lands(chunks, quarter, width):
        return [
            jax.ShapeDtypeStruct((chunks, 2, quarter, width), f32),
            jax.ShapeDtypeStruct((chunks, quarter, width), f32),
            jax.ShapeDtypeStruct((chunks, quarter, width), f32),
            jax.ShapeDtypeStruct((chunks, 2, quarter, width), f32),
        ]

    @staticmethod
    def sems(chunks):
        dma = pltpu.SemaphoreType.DMA
        return [dma((chunks,)) for _ in range(8)] + [dma((5,))]

    @staticmethod
    def buffers(quarter, width):
        return [
            pltpu.VMEM((2, 2, 2, quarter, width), f32),
            pltpu.VMEM((2, quarter, width), f32),
            pltpu.VMEM((2, 2, quarter, width), f32),
            pltpu.VMEM((quarter, width), f32),
            pltpu.VMEM((2, quarter, width), f32),
            pltpu.VMEM((2, 2, quarter, width), f32),
            pltpu.VMEM((2, quarter, width), f32),
            pltpu.VMEM((2, 2, quarter, width), bf16),
        ]

    def __init__(self, me, lands, sems):
        self.me = me
        self.core_land, self.chip_land, self.back_land, self.last_land = lands
        (self.s0, self.r0, self.s1, self.r1, self.s2, self.r2, self.s3, self.r3, self.local) = sems
        self.chunks = self.chip_land.shape[0]

    def use(self, buffers):
        (self.part, self.core_load, self.half, self.chip_load,
         self.done, self.pair, self.last_load, self.low) = buffers

    def copies(self, stage, c):
        me, slot = self.me, lax.rem(c, 2)
        if stage == 0:
            return remote(self.part.at[slot, 1 - me.core], self.core_land.at[c],
                          self.s0.at[c], self.r0.at[c], me.to_core)
        if stage == 1:
            return remote(self.half.at[slot, 1 - me.chip], self.chip_land.at[c],
                          self.s1.at[c], self.r1.at[c], me.to_chip)
        if stage == 2:
            return remote(self.done.at[slot], self.back_land.at[c],
                          self.s2.at[c], self.r2.at[c], me.to_chip)
        return remote(self.pair.at[slot], self.last_land.at[c],
                      self.s3.at[c], self.r3.at[c], me.to_core)

    @property
    def slots(self):
        return self.chunks + 4

    def step(self, s, produce, work, lower, emit):
        me = self.me

        def stage(number, body):
            c = s - number

            @pl.when((c >= 0) & (c < self.chunks))
            def _():
                if number > 0:
                    self.copies(number - 1, c).wait()
                body(c, lax.rem(c, 2))
                if number < 4:
                    self.copies(number, c).start()

        def four(c, slot):
            fetch(self.last_land.at[c], self.last_load, self.local.at[3]).wait()
            self.low[me.core] = lower(self.pair[slot])
            self.low[1 - me.core] = lower(self.last_load[...])
            emit(c, self.low)

        def three(c, slot):
            fetch(self.back_land.at[c], self.pair.at[slot, 1 - me.chip], self.local.at[2]).wait()
            self.pair[slot, me.chip] = self.done[slot]

        def two(c, slot):
            fetch(self.chip_land.at[c], self.chip_load, self.local.at[1]).wait()
            self.done[slot] = work(c, self.half[slot, me.chip] + self.chip_load[...])

        def one(c, slot):
            fetch(self.core_land.at[c], self.core_load, self.local.at[0]).wait()
            self.half[slot] = self.part[slot, me.core] + self.core_load[...]

        def zero(c, slot):
            produce(c, self.part.at[slot])

        stage(4, four)
        stage(3, three)
        stage(2, two)
        stage(1, one)
        stage(0, zero)


def take(refs, count):
    return refs[:count], refs[count:]


def store_part(part, value, columns):
    half, quarter = 2, value.shape[0] // 4
    part[:, :, :, columns] = value.reshape(half, 2, quarter, value.shape[1])


def norm_back(pulled, unit, scale, gain):
    scaled = pulled * gain
    return scale * (scaled - unit * jnp.mean(scaled * unit, axis=-1, keepdims=True))


def half_turn(values):
    return pltpu.roll(values, values.shape[-1] // 2, values.ndim - 1)


def allowed_pairs(keys, rows, starts):
    count = rows.stop - rows.start
    key = lax.broadcasted_iota(jnp.int32, (keys, count), 0)
    query = lax.broadcasted_iota(jnp.int32, (keys, count), 1) + rows.start
    return (key <= query) & (key >= starts)


def attend_kernel(wide, chunks, *refs):
    (tokens, cot, w_query, w_key, w_value, w_output, attn_gain, mlp_gain, query_gain, key_gain,
     cosine, sine, starts), refs = take(refs, 13)
    (mlp_in, mlp_in_t, cot_t, normed_t, hidden_out, q_out, k_out, v_out, q_raw_out, k_raw_out,
     context_out, lse_out), refs = take(refs, 12)
    lands, refs = take(refs, 4)
    sems, refs = take(refs, 9)
    buffers, refs = take(refs, 8)
    (hidden_buf, q_low, k_low, v_low, v_t, q_raw, k_raw, context, lse, normed, normed_turn,
     cot_load, cot_turn, low_turn, sem, out_sem) = refs
    me = Spot(wide)
    me.greet(False)
    summing = NarrowSum(me, lands, sems)
    summing.use(buffers)
    token_count, width = tokens.shape
    rows = token_count // chunks
    quarter = rows // 4
    block = normed.shape[0]
    per_block = block // rows
    head = query_gain.shape[1]
    q_heads = w_query.shape[1] // head
    group = q_heads // (w_key.shape[1] // head)
    scale = head ** (-0.5)
    step = min(512, width)
    kept = (
        (q_low, q_out), (k_low, k_out), (v_low, v_out), (q_raw, q_raw_out), (k_raw, k_raw_out),
        (context, context_out), (lse, lse_out),
    )

    def attend(i):
        own = slice(i * block, (i + 1) * block)
        keys = (i + 1) * block
        x = tokens[own, :].astype(f32)
        normed[...] = (x * inverse_rms(x) * attn_gain[...]).astype(bf16)
        cos, sin = cosine[own, :], sine[own, :]

        def heads_of(raw, low, gain):
            for h in range(raw.shape[1] // head):
                cut = slice(h * head, (h + 1) * head)
                u = raw[own, cut]
                y = u * inverse_rms(u) * gain[...]
                low[own, cut] = (y * cos + half_turn(y) * sin).astype(bf16)

        q_raw[own, :] = forward_dot(normed[...], w_query[...])
        k_raw[own, :] = forward_dot(normed[...], w_key[...])
        value = forward_dot(normed[...], w_value[...])
        v_low[own, :] = value.astype(bf16)
        v_t[:, own] = value.T.astype(bf16)
        heads_of(q_raw, q_low, query_gain)
        heads_of(k_raw, k_low, key_gain)
        allowed = allowed_pairs(keys, own, starts[:, own])
        for h in range(q_heads):
            cut, kv = slice(h * head, (h + 1) * head), h // group
            kv_cut = slice(kv * head, (kv + 1) * head)
            scores = nt_dot(k_low[0:keys, kv_cut], q_low[own, cut]) * scale
            scores = jnp.where(allowed, scores, masked_score)
            top = jnp.max(scores, axis=0, keepdims=True)
            expd = jnp.exp(scores - top)
            total = jnp.sum(expd, axis=0, keepdims=True)
            probs = (expd / total).astype(bf16)
            lse[h : h + 1, own] = top + jnp.log(total)
            mixed = forward_dot(v_t[kv_cut, 0:keys], probs)
            context[own, cut] = mixed.T.astype(bf16)

    def produce(c, part):
        for i in range(token_count // block):
            pl.when(c == i * per_block)(functools.partial(attend, i))
        left = context[pl.ds(pl.multiple_of(c * rows, rows), rows), :]
        for at in range(0, width, step):
            store_part(part, forward_dot(left, w_output[:, at : at + step]), slice(at, at + step))

    def work(c, total):
        at = pl.multiple_of(c * rows + me.core * 2 * quarter + me.chip * quarter, quarter)
        hidden = tokens[pl.ds(at, quarter), :].astype(f32) + total
        hidden_buf[...] = hidden
        fetch(hidden_buf, hidden_out.at[c], sem.at[1]).wait()
        return hidden * inverse_rms(hidden)

    def lower(value):
        return (value * mlp_gain[...]).astype(bf16)

    def emit(c, low):
        a = fetch(low, mlp_in.at[c], sem.at[0])
        low_turn[...] = low[...].reshape(rows, width).T
        at = pl.ds(pl.multiple_of(c * rows, rows), rows)
        fetch(low_turn, mlp_in_t.at[:, at], sem.at[1]).wait()
        a.wait()

    def turn_rows(s):
        at = pl.ds(pl.multiple_of(s * rows, rows), rows)
        fetch(cot.at[at, :], cot_load, sem.at[0]).wait()
        cot_turn[...] = cot_load[...].T
        a = fetch(cot_turn, cot_t.at[:, at], sem.at[1])

        @pl.when(lax.rem(s, per_block) == 0)
        def _():
            normed_turn[...] = normed[...].T
            wide_at = pl.ds(pl.multiple_of(s * rows, block), block)
            fetch(normed_turn, normed_t.at[:, wide_at], sem.at[0]).wait()

        a.wait()

    def body(s, carry):
        summing.step(s, produce, work, lower, emit)
        pl.when(s < chunks)(lambda: turn_rows(s))

        @pl.when(s == chunks - 1)
        def _():
            for at, (a, b) in enumerate(kept):
                fetch(a, b, out_sem.at[at])

        return carry

    lax.fori_loop(0, summing.slots, body, 0)
    for at, (a, b) in enumerate(kept):
        pltpu.make_async_copy(a, b, out_sem.at[at]).wait()


def outer_tile(left_t, right, stage):
    line, _, rows, _ = stage.shape
    group = max(1, 512 // (2 * rows))
    while line % group:
        group -= 1

    def body(m, carry):
        at = pl.multiple_of(m * group * 2 * rows, group * 2 * rows)
        value = forward_dot(left_t[pl.ds(at, group * 2 * rows), :], right)
        stage[pl.ds(m * group, group)] = value.reshape((group, 2, rows, value.shape[1]))
        return carry

    lax.fori_loop(0, line // group, body, 0)


class SmallSum:
    def __init__(self, me, value, lands, sends, recvs):
        self.me, self.value, self.lands, self.sends, self.recvs = me, value, lands, sends, recvs

    def copy(self, k):
        me = self.me
        who = (me.to_core, me.to_chip, me.to_side)[k] if k < 3 else me.along(k - 2)
        return remote(self.value, self.lands.at[k], self.sends.at[k], self.recvs.at[k], who)

    def step(self, at):
        last = 2 + self.me.line
        stages = [[0], [1], [2], list(range(3, last)), []]
        for number, copies in enumerate(stages):
            @pl.when(at == number)
            def _(number=number, copies=copies):
                if number > 0:
                    for k in stages[number - 1]:
                        self.copy(k).wait()
                    for k in stages[number - 1]:
                        self.value[...] = self.value[...] + self.lands[k]
                for k in copies:
                    self.copy(k).start()


def main_kernel(wide, chunks, *refs):
    (mlp_in, mlp_in_t, cot, cot_t, normed_t, hidden, q_in, k_in, v_in, q_raw, k_raw, context,
     lse_in, tokens, w_gate, w_up, w_down, w_output, w_query, w_key, w_value, cosine, sine,
     starts, attn_gain, mlp_gain, query_gain, key_gain), refs = take(refs, 28)
    (output, grad_tokens, grad_query, grad_key, grad_value, grad_output, grad_gate, grad_up,
     grad_down, gains_out, grad_hidden), refs = take(refs, 11)
    wide_lands, refs = take(refs, 4)
    lands, refs = take(refs, 4)
    wide_sems, refs = take(refs, 7)
    sems, refs = take(refs, 9)
    acts, gains, gain_lands, gain_send, gain_recv, sem, w_sem, store_sem = refs
    me = Spot(wide)
    me.greet(True)
    token_count, width = mlp_in.shape
    hidden_units = w_gate.shape[1]
    tiles, line, _, side_rows, cols = wide_lands[0].shape
    blocks = hidden_units // cols
    mlp_tiles = 3 * blocks
    query_width, kv_width = w_query.shape[1], w_key.shape[1]
    all_heads = query_width + 2 * kv_width
    head = query_gain.shape[1]
    q_heads = query_width // head
    group = q_heads // (kv_width // head)
    scale = head ** (-0.5)
    out_tiles = query_width // cols
    total = WideSum(me, wide_lands, wide_sems)
    half = token_count // 2
    rows = token_count // chunks
    quarter = rows // 4

    def compute(xs, xt, cs, ct, gate_w, up_w, down_w, staged):
        pairs = ((mlp_in, xs), (cot, cs), (cot_t, ct), (mlp_in_t, xt))
        for at, (a, b) in enumerate(pairs):
            fetch(a, b, sem.at[at])

        def weights(b, slot):
            at = pl.ds(pl.multiple_of(b * cols, cols), cols)
            return (
                pltpu.make_async_copy(w_gate.at[:, at], gate_w.at[slot], w_sem.at[slot, 0]),
                pltpu.make_async_copy(w_up.at[:, at], up_w.at[slot], w_sem.at[slot, 1]),
                pltpu.make_async_copy(w_down.at[at, :], down_w.at[slot], w_sem.at[slot, 2]),
            )

        for copy in weights(0, 0):
            copy.start()
        for at, (a, b) in enumerate(pairs):
            pltpu.make_async_copy(a, b, sem.at[at]).wait()

        def store(tile):
            slot = lax.rem(tile, 2)
            return pltpu.make_async_copy(staged.at[slot], total.parts.at[tile], store_sem.at[slot])

        def block(b, carry):
            slot = lax.rem(b, 2)
            for copy in weights(b, slot):
                copy.wait()

            @pl.when(b + 1 < blocks)
            def _():
                for copy in weights(b + 1, 1 - slot):
                    copy.start()

            at = pl.ds(pl.multiple_of(b * cols, cols), cols)

            def some(m, carry):
                own = pl.ds(pl.multiple_of(m * half, half), half)
                gate = forward_dot(xs[own, :], gate_w[slot])
                up = forward_dot(xs[own, :], up_w[slot])
                back = nt_dot(cs[own, :], down_w[slot])
                sig = 1.0 / (1.0 + jnp.exp(-gate))
                silu = gate * sig
                acts[0, own, at] = (silu * up).astype(bf16)
                acts[1, own, at] = (back * up * sig * (1.0 + gate * (1.0 - sig))).astype(bf16)
                acts[2, own, at] = (back * silu).astype(bf16)
                return carry

            lax.fori_loop(0, 2, some, 0)
            for j in range(3):
                tile = 3 * b + j

                @pl.when(tile >= 2)
                def _(tile=tile):
                    store(tile - 2).wait()

                    @pl.when(tile - 2 < total.ahead)
                    def _():
                        total.y_copy(tile - 2).start()

                outer_tile(ct if j == 0 else xt, acts[j, :, at], staged.at[lax.rem(tile, 2)])
                store(tile).start()
            return carry

        lax.fori_loop(0, blocks, block, 0)
        for tile in range(mlp_tiles - 2, mlp_tiles):
            store(tile).wait()

    pl.run_scoped(
        compute,
        pltpu.VMEM(mlp_in.shape, bf16),
        pltpu.VMEM(mlp_in_t.shape, bf16),
        pltpu.VMEM(mlp_in.shape, bf16),
        pltpu.VMEM(mlp_in_t.shape, bf16),
        pltpu.VMEM((2, width, cols), bf16),
        pltpu.VMEM((2, width, cols), bf16),
        pltpu.VMEM((2, cols, width), bf16),
        pltpu.VMEM((2, line, 2, side_rows, cols), f32),
    )

    def pass_on(*held):
        wide_buffers, held = take(held, 8)
        buffers, held = take(held, 8)
        (gate_w, up_w, down_w, hidden_load, token_load, out_buf, out_w, left_t, staged, q_low,
         k_low, v_low, k_t, d_context, right, lse, cos, sin, raw, d_query, d_key, d_value,
         heads, turned) = held
        total.use(wide_buffers)
        summing = NarrowSum(me, lands, sems)
        summing.use(buffers)
        small = SmallSum(me, gains, gain_lands, gain_send, gain_recv)
        gains[...] = jnp.zeros_like(gains)
        gain_at = (
            slice(0, width), slice(width, 2 * width), slice(2 * width, 2 * width + head),
            slice(2 * width + head, 2 * width + 2 * head),
        )
        loads = ((w_output, out_w), (q_in, q_low), (k_in, k_low), (v_in, v_low), (lse_in, lse),
                 (cosine, cos), (sine, sin))
        for a, b in loads:
            fetch(a, b, sem.at[0]).wait()
        k_t[...] = k_low[...].T
        step = gate_w.shape[1]
        first_attend = chunks + 4
        first_heads = first_attend + q_heads

        def stream(copies, use):
            count = width // step
            for copy in copies(0, 0):
                copy.start()
            for at in range(count):
                if at + 1 < count:
                    for copy in copies(at + 1, (at + 1) % 2):
                        copy.start()
                for copy in copies(at, at % 2):
                    copy.wait()
                use(at % 2, slice(at * step, (at + 1) * step))

        def produce(c, part):
            chunk = lax.rem(c, chunks)
            own = pl.ds(pl.multiple_of(chunk * rows, rows), rows)
            kind = lax.div(c, chunks)

            @pl.when(kind == 0)
            def _():
                def copies(at, slot):
                    cut = pl.ds(at * step, step)
                    gate = gate_w.at[slot, :, 0:hidden_units]
                    return (
                        pltpu.make_async_copy(w_gate.at[cut, :], gate, w_sem.at[slot, 0]),
                        pltpu.make_async_copy(w_up.at[cut, :], up_w.at[slot], w_sem.at[slot, 1]),
                    )

                def use(slot, cut):
                    value = nt_dot(acts[1, own, :], gate_w[slot, :, 0:hidden_units])
                    store_part(part, value + nt_dot(acts[2, own, :], up_w[slot]), cut)

                stream(copies, use)

            @pl.when(kind == 1)
            def _():
                def copies(at, slot):
                    cut = pl.ds(at * step, step)
                    return (
                        pltpu.make_async_copy(w_down.at[:, cut], down_w.at[slot], w_sem.at[slot, 2]),
                    )

                def use(slot, cut):
                    store_part(part, forward_dot(acts[0, own, :], down_w[slot]), cut)

                stream(copies, use)

            @pl.when(kind == 2)
            def _():
                def copies(at, slot):
                    cut, start, found = pl.ds(at * step, step), 0, []
                    for j, w in enumerate((w_query, w_key, w_value)):
                        there = gate_w.at[slot, :, start : start + w.shape[1]]
                        found.append(pltpu.make_async_copy(w.at[cut, :], there, w_sem.at[slot, j]))
                        start += w.shape[1]
                    return found

                def use(slot, cut):
                    store_part(part, nt_dot(heads[own, :], gate_w[slot, :, 0:all_heads]), cut)

                stream(copies, use)

        def work(c, pulled):
            chunk = lax.rem(c, chunks)
            kind = lax.div(c, chunks)

            @pl.when(kind == 0)
            def _():
                a = fetch(hidden.at[chunk], hidden_load, sem.at[0])
                b = fetch(cot.at[own_rows(chunk), :], token_load, sem.at[1])
                a.wait()
                b.wait()
                mid = hidden_load[...]
                inverse = inverse_rms(mid)
                unit = mid * inverse
                gains[:, gain_at[1]] += jnp.sum(pulled * unit, axis=0, keepdims=True)
                back = norm_back(pulled, unit, inverse, mlp_gain[...])
                out_buf[...] = token_load[...].astype(f32) + back
                fetch(out_buf, grad_hidden.at[chunk], sem.at[0]).wait()

            @pl.when(kind == 1)
            def _():
                fetch(hidden.at[chunk], hidden_load, sem.at[0]).wait()
                out_buf[...] = hidden_load[...] + pulled

            @pl.when(kind == 2)
            def _():
                a = fetch(grad_hidden.at[chunk], hidden_load, sem.at[0])
                b = fetch(tokens.at[own_rows(chunk), :], token_load, sem.at[1])
                a.wait()
                b.wait()
                mid = token_load[...].astype(f32)
                inverse = inverse_rms(mid)
                unit = mid * inverse
                gains[:, gain_at[0]] += jnp.sum(pulled * unit, axis=0, keepdims=True)
                out_buf[...] = hidden_load[...] + norm_back(pulled, unit, inverse, attn_gain[...])

            return out_buf[...]

        def own_rows(chunk):
            at = chunk * rows + me.core * 2 * quarter + me.chip * quarter
            return pl.ds(pl.multiple_of(at, quarter), quarter)

        def lower(value):
            return value.astype(bf16)

        def emit_rows(c, low):
            chunk = lax.rem(c, chunks)
            kind = lax.div(c, chunks)

            @pl.when(kind == 0)
            def _():
                own = pl.ds(pl.multiple_of(chunk * rows, rows), rows)
                value = low[...].reshape(rows, width)
                d_context[own, :] = nt_dot(value, out_w[...]).astype(bf16)
                left_t[:, own] = value.T

            @pl.when(kind == 1)
            def _():
                fetch(low, output.at[chunk], sem.at[0]).wait()

            @pl.when(kind == 2)
            def _():
                fetch(low, grad_tokens.at[chunk], sem.at[0]).wait()

        def put(tile, right_value):
            outer_tile(left_t, right_value, staged)
            fetch(staged, total.parts.at[tile], store_sem.at[0]).wait()

        def rope_norm_back(grad, raw_value, gain, at):
            scaled = grad * cos[...] - half_turn(grad) * sin[...]
            inverse = inverse_rms(raw_value)
            unit = raw_value * inverse
            gains[:, at] += jnp.sum(scaled * unit, axis=0, keepdims=True)
            return norm_back(scaled, unit, inverse, gain[...])

        def attend_back(h):
            kv = lax.div(h, group)
            cut = pl.ds(pl.multiple_of(h * head, head), head)
            kv_cut = pl.ds(pl.multiple_of(kv * head, head), head)

            @pl.when(lax.rem(h, group) == 0)
            def _():
                d_key[...] = jnp.zeros_like(d_key)
                d_value[...] = jnp.zeros_like(d_value)

            load = fetch(q_raw.at[:, cut], raw, sem.at[0])
            size = min(256, token_count)
            for i in range(token_count // size):
                own, keys = slice(i * size, (i + 1) * size), (i + 1) * size
                q, dc = q_low[own, cut], d_context[own, cut]
                scores = nt_dot(k_low[0:keys, kv_cut], q) * scale
                expd = jnp.exp(scores - lse[pl.ds(h, 1), own])
                probs = jnp.where(allowed_pairs(keys, own, starts[:, own]), expd, 0.0)
                d_value[0:keys, :] += forward_dot(probs.astype(bf16), dc)
                d_probs = nt_dot(v_low[0:keys, kv_cut], dc)
                mean = jnp.sum(probs * d_probs, axis=0, keepdims=True)
                d_scores = (probs * (d_probs - mean)).astype(bf16)
                d_key[0:keys, :] += forward_dot(d_scores, q)
                d_query[own, :] = forward_dot(k_t[kv_cut, 0:keys], d_scores).T
            load.wait()
            heads[:, cut] = rope_norm_back(
                d_query[...] * scale, raw[...], query_gain, gain_at[2]
            ).astype(bf16)

            @pl.when(lax.rem(h, group) == group - 1)
            def _():
                fetch(k_raw.at[:, kv_cut], raw, sem.at[0]).wait()
                there = pl.ds(pl.multiple_of(query_width + kv * head, head), head)
                heads[:, there] = rope_norm_back(
                    d_key[...] * scale, raw[...], key_gain, gain_at[3]
                ).astype(bf16)
                there = pl.ds(pl.multiple_of(query_width + kv_width + kv * head, head), head)
                heads[:, there] = d_value[...].astype(bf16)

        def emit_tile(tile, value):
            def part(first, count, target, turn, every=1, offset=0):
                inside = (tile >= first) & (tile < first + count)
                at = tile - first
                if every > 1:
                    inside = inside & (lax.rem(at, every) == offset)
                    at = lax.div(at, every)

                @pl.when(inside)
                def _():
                    cut = pl.ds(pl.multiple_of(at * cols, cols), cols)
                    if turn:
                        turned[...] = value[...].T
                        fetch(turned, target.at[cut, :], sem.at[0]).wait()
                    else:
                        fetch(value, target.at[:, cut], sem.at[0]).wait()

            part(0, mlp_tiles, grad_down, True, 3, 0)
            part(0, mlp_tiles, grad_gate, False, 3, 1)
            part(0, mlp_tiles, grad_up, False, 3, 2)
            at = mlp_tiles
            part(at, out_tiles, grad_output, True)
            at += out_tiles
            part(at, query_width // cols, grad_query, False)
            at += query_width // cols
            part(at, kv_width // cols, grad_key, False)
            at += kv_width // cols
            part(at, kv_width // cols, grad_value, False)

        small_at = summing.slots - 1

        def body(s, carry):
            @pl.when(s == first_attend)
            def _():
                for t in range(out_tiles):
                    cut = slice(t * cols, (t + 1) * cols)
                    fetch(context.at[:, cut], right, sem.at[0]).wait()
                    put(mlp_tiles + t, right[...])

            @pl.when((s >= first_attend) & (s < first_heads))
            def _():
                attend_back(s - first_attend)

            @pl.when(s == first_heads)
            def _():
                fetch(normed_t, left_t, sem.at[0]).wait()

                def one(t, carry):
                    put(mlp_tiles + out_tiles + t, heads[:, pl.ds(pl.multiple_of(t * cols, cols), cols)])
                    return carry

                lax.fori_loop(0, all_heads // cols, one, 0)

            pl.when(s < total.slots)(lambda: total.step(s, emit_tile))
            pl.when(s < summing.slots)(
                lambda: summing.step(s, produce, work, lower, emit_rows)
            )
            pl.when(s >= small_at)(lambda: small.step(s - small_at))
            return carry

        lax.fori_loop(0, max(total.slots, small_at + 5), body, 0)
        total.finish()

    step = min(256, width)
    pl.run_scoped(
        pass_on,
        *WideSum.buffers(line, side_rows, cols),
        *NarrowSum.buffers(quarter, width),
        pltpu.VMEM((2, step, max(hidden_units, all_heads)), bf16),
        pltpu.VMEM((2, step, hidden_units), bf16),
        pltpu.VMEM((2, hidden_units, step), bf16),
        pltpu.VMEM((quarter, width), f32),
        pltpu.VMEM((quarter, width), bf16),
        pltpu.VMEM((quarter, width), f32),
        pltpu.VMEM(w_output.shape, bf16),
        pltpu.VMEM(normed_t.shape, bf16),
        pltpu.VMEM((line, 2, side_rows, cols), f32),
        pltpu.VMEM(q_in.shape, bf16),
        pltpu.VMEM(k_in.shape, bf16),
        pltpu.VMEM(v_in.shape, bf16),
        pltpu.VMEM((kv_width, token_count), bf16),
        pltpu.VMEM(q_in.shape, bf16),
        pltpu.VMEM((token_count, cols), bf16),
        pltpu.VMEM(lse_in.shape, f32),
        pltpu.VMEM(cosine.shape, f32),
        pltpu.VMEM(sine.shape, f32),
        pltpu.VMEM((token_count, head), f32),
        pltpu.VMEM((token_count, head), f32),
        pltpu.VMEM((token_count, head), f32),
        pltpu.VMEM((token_count, head), f32),
        pltpu.VMEM((token_count, all_heads), bf16),
        pltpu.VMEM((cols, side_rows), f32),
    )
    fetch(gains, gains_out, sem.at[0]).wait()


def call(kernel, collective_id, out_shape, in_specs, out_specs, scratch, arrays):
    return pl.pallas_call(
        kernel,
        out_shape=out_shape,
        in_specs=in_specs,
        out_specs=out_specs,
        scratch_shapes=scratch,
        compiler_params=pltpu.CompilerParams(
            collective_id=collective_id,
            has_side_effects=True,
            vmem_limit_bytes=62 * 1024 * 1024,
        ),
    )(*arrays)


def per_device(
    wide,
    tokens,
    seq_lengths,
    attn_gain,
    w_query,
    key_weight,
    value_weight,
    query_gain,
    key_norm_gain,
    w_output,
    mlp_gain,
    w_gate,
    w_up,
    w_down,
    cotangent,
):
    token_count, width = tokens.shape
    head_dim = query_gain.shape[0]
    query_width, kv_width = w_query.shape[1], key_weight.shape[1]
    hidden_units = w_gate.shape[1]
    all_heads = query_width + 2 * kv_width
    line = wide // 2
    side_rows = width // wide
    chunks = 8
    rows = token_count // chunks
    quarter = rows // 4
    block = min(256, token_count)
    dma = pltpu.SemaphoreType.DMA
    shape = jax.ShapeDtypeStruct

    segment_index, token_positions = layout(seq_lengths, token_count)
    token_positions = token_positions.reshape(-1)
    starts = (jnp.arange(token_count, dtype=jnp.int32) - token_positions)[None]
    cosine, sine = tables(token_positions, head_dim)
    cosine = cosine.reshape(token_count, head_dim)
    sign = jnp.where(jnp.arange(head_dim) < head_dim // 2, -1.0, 1.0).astype(f32)
    sine = sine.reshape(token_count, head_dim) * sign
    q_heads = query_width // head_dim

    kept = [
        shape((token_count, query_width), bf16),
        shape((token_count, kv_width), bf16),
        shape((token_count, kv_width), bf16),
        shape((token_count, query_width), f32),
        shape((token_count, kv_width), f32),
        shape((token_count, query_width), bf16),
        shape((q_heads, token_count), f32),
    ]
    vmem = [pltpu.VMEM(k.shape, k.dtype) for k in kept]
    outs = call(
        lambda *refs: attend_kernel(wide, chunks, *refs),
        1,
        [
            shape((chunks, 2, 2, quarter, width), bf16),
            shape((width, token_count), bf16),
            shape((width, token_count), bf16),
            shape((width, token_count), bf16),
            shape((chunks, quarter, width), f32),
            *kept,
            *NarrowSum.lands(chunks, quarter, width),
        ],
        [in_vmem, any_space] + [in_vmem] * 11,
        [any_space] * 16,
        [
            *NarrowSum.sems(chunks),
            *NarrowSum.buffers(quarter, width),
            pltpu.VMEM((quarter, width), f32),
            *vmem[:3],
            pltpu.VMEM((kv_width, token_count), bf16),
            *vmem[3:],
            pltpu.VMEM((block, width), bf16),
            pltpu.VMEM((width, block), bf16),
            pltpu.VMEM((rows, width), bf16),
            pltpu.VMEM((width, rows), bf16),
            pltpu.VMEM((width, rows), bf16),
            dma((2,)),
            dma((7,)),
        ],
        (
            tokens, cotangent, w_query, key_weight, value_weight, w_output, attn_gain[None],
            mlp_gain[None], query_gain[None], key_norm_gain[None], cosine, sine, starts,
        ),
    )
    (mlp_in, mlp_in_t, cot_t, normed_t, hidden, q_low, k_low, v_low, q_raw, k_raw, context,
     lse) = outs[:12]

    cols = min(256 if line <= 4 else 128, hidden_units // 6)
    tiles = (3 * hidden_units + query_width + all_heads) // cols
    gain_width = 2 * width + 2 * head_dim
    outs = call(
        lambda *refs: main_kernel(wide, chunks, *refs),
        2,
        [
            shape((chunks, 2, 2, quarter, width), bf16),
            shape((chunks, 2, 2, quarter, width), bf16),
            shape((side_rows, query_width), f32),
            shape((side_rows, kv_width), f32),
            shape((side_rows, kv_width), f32),
            shape((query_width, side_rows), f32),
            shape((side_rows, hidden_units), f32),
            shape((side_rows, hidden_units), f32),
            shape((hidden_units, side_rows), f32),
            shape((1, gain_width), f32),
            shape((chunks, quarter, width), f32),
            *WideSum.lands(tiles, line, side_rows, cols),
            *NarrowSum.lands(3 * chunks, quarter, width),
        ],
        [any_space] * 23 + [in_vmem] * 5,
        [any_space] * 19,
        [
            *WideSum.sems(tiles),
            *NarrowSum.sems(3 * chunks),
            pltpu.VMEM((3, token_count, hidden_units), bf16),
            pltpu.VMEM((1, gain_width), f32),
            pltpu.VMEM((2 + line, 1, gain_width), f32),
            dma((2 + line,)),
            dma((2 + line,)),
            dma((4,)),
            dma((2, 3)),
            dma((2,)),
        ],
        (
            mlp_in.reshape(token_count, width), mlp_in_t, cotangent, cot_t, normed_t, hidden,
            q_low, k_low, v_low, q_raw, k_raw, context, lse, tokens, w_gate, w_up, w_down,
            w_output, w_query, key_weight, value_weight, cosine, sine, starts, attn_gain[None],
            mlp_gain[None], query_gain[None], key_norm_gain[None],
        ),
    )
    (output, grad_tokens, shard_query, shard_key, shard_value, shard_output, shard_gate,
     shard_up, shard_down, gains) = outs[:10]
    gains = gains[0]
    at = lax.axis_index("wide")
    head_part = head_dim // wide

    def own(start, size):
        return lax.dynamic_slice_in_dim(gains, start + at * size, size)

    return (
        output.reshape(token_count, width),
        grad_tokens.reshape(token_count, width),
        own(0, side_rows),
        shard_query,
        shard_key,
        shard_value,
        own(2 * width, head_part),
        own(2 * width + head_dim, head_part),
        shard_output,
        own(width, side_rows),
        shard_gate,
        shard_up,
        shard_down,
    )


def solution(mesh):
    def run(*arrays):
        return per_device(mesh.shape["wide"], *arrays)

    return jax.shard_map(
        run,
        mesh=mesh,
        in_specs=(
            P("wide", None),
            P("wide", None),
            P(),
            P(None, "narrow"),
            P(None, "narrow"),
            P(None, "narrow"),
            P(),
            P(),
            P("narrow", None),
            P(),
            P(None, "narrow"),
            P(None, "narrow"),
            P("narrow", None),
            P("wide", None),
        ),
        out_specs=(
            P("wide", None),
            P("wide", None),
            P("wide"),
            P("wide", "narrow"),
            P("wide", "narrow"),
            P("wide", "narrow"),
            P("wide"),
            P("wide"),
            P("narrow", "wide"),
            P("wide"),
            P("wide", "narrow"),
            P("wide", "narrow"),
            P("narrow", "wide"),
        ),
        check_vma=False,
    )
```

```python
import functools

import jax
import jax.numpy as jnp
from jax import lax
from jax.experimental import pallas as pl
from jax.experimental.pallas import tpu as pltpu
from jax.sharding import PartitionSpec as P

norm_eps = 1e-06
rope_base = 1000000.0
masked_score = -1e30
bf16 = jnp.bfloat16
f32 = jnp.float32


def inverse_rms(values):
    return lax.rsqrt(jnp.mean(values * values, axis=-1, keepdims=True) + norm_eps)


def layout(seq_lengths, row_len):
    seq_ends = jnp.cumsum(seq_lengths, axis=-1)
    starts = seq_ends - seq_lengths
    places = jnp.arange(row_len, dtype=jnp.int32)
    segment_index = jnp.sum(
        (places[None, :, None] >= seq_ends[:, None, :]).astype(jnp.int32), axis=-1
    )
    belongs = (
        segment_index[:, :, None]
        == jnp.arange(seq_lengths.shape[-1], dtype=jnp.int32)[None, None, :]
    )
    seq_start = jnp.sum(jnp.where(belongs, starts[:, None, :], 0), axis=-1)
    return (segment_index, places[None, :] - seq_start)


def tables(token_positions, head_dim):
    half_width = head_dim // 2
    frequency = rope_base ** (-2.0 * jnp.arange(half_width, dtype=f32) / head_dim)
    angles = token_positions.astype(f32)[:, None] * frequency[None, :]
    angles = jnp.concatenate([angles, angles], axis=-1)
    return (jnp.cos(angles)[:, None, :], jnp.sin(angles)[:, None, :])


def forward_dot(left_side, right_side):
    return jnp.dot(left_side, right_side, preferred_element_type=f32)


MESH = pl.DeviceIdType.MESH
any_space = pl.BlockSpec(memory_space=pl.ANY)
in_vmem = pl.BlockSpec(memory_space=pltpu.VMEM)


def nt_dot(left_side, right_side):
    return lax.dot_general(
        left_side, right_side, (((1,), (1,)), ((), ())), preferred_element_type=f32
    )


def fetch(source, target, sem):
    copy = pltpu.make_async_copy(source, target, sem)
    copy.start()
    return copy


class Spot:
    def __init__(self, wide):
        self.line = wide // 2
        self.w = lax.axis_index("wide")
        self.n = lax.axis_index("narrow")
        self.spot = lax.div(self.w, 2)
        self.side = lax.rem(self.w, 2)
        self.core = lax.rem(self.n, 2)
        self.chip = lax.div(self.n, 2)
        self.to_core = {"narrow": self.n + 1 - 2 * self.core}
        self.to_chip = {"narrow": self.n + 2 - 4 * self.chip}
        self.to_side = {"wide": self.w + 1 - 2 * self.side}
        self.to_up = {"wide": self.w + 2}
        self.to_down = {"wide": self.w - 2}

    def along(self, distance):
        there = lax.rem(self.spot + distance, self.line)
        return {"wide": there * 2 + self.side}

    def greet(self, wide_too):
        barrier = pltpu.get_barrier_semaphore()

        def tell(who):
            pl.semaphore_signal(barrier, inc=1, device_id=who, device_id_type=MESH)

        tell(self.to_core)
        tell(self.to_chip)
        if wide_too:
            tell(self.to_side)
            for distance in range(1, self.line):
                tell(self.along(distance))
        pl.semaphore_wait(barrier, 2 + self.line if wide_too else 2)


def remote(source, target, send, recv, who):
    return pltpu.make_async_remote_copy(
        src_ref=source, dst_ref=target, send_sem=send, recv_sem=recv,
        device_id=who, device_id_type=MESH,
    )


class WideSum:
    group = 6
    ahead = 3

    @staticmethod
    def lag(line):
        return 2 if line <= 4 else 1

    @classmethod
    def counts(cls, tiles):
        groups = tiles // cls.group
        return groups, tiles - groups, tiles + groups

    @classmethod
    def lands(cls, tiles, line, rows, cols):
        groups, firsts, items = cls.counts(tiles)
        return [
            jax.ShapeDtypeStruct((tiles, line, 2, rows, cols), f32),
            jax.ShapeDtypeStruct((firsts, line, rows, cols), f32),
            jax.ShapeDtypeStruct((items, line - 1, rows, cols), f32),
            jax.ShapeDtypeStruct((items, line - 1, rows, cols), f32),
            jax.ShapeDtypeStruct((groups, rows, cols), f32),
        ]

    @classmethod
    def sems(cls, tiles):
        dma = pltpu.SemaphoreType.DMA
        groups, firsts, items = cls.counts(tiles)
        return [
            dma((firsts,)), dma((firsts,)), dma((2,)), dma((items,)), dma((2,)), dma((items,)),
            dma((groups,)), dma((groups,)), dma((7,)),
        ]

    @staticmethod
    def buffers(line, rows, cols):
        tile = (line, rows, cols)
        return [
            pltpu.VMEM(tile, f32),
            pltpu.VMEM((WideSum.lag(line) * (line - 1) + 1,) + tile, f32),
            pltpu.VMEM((2, line - 1, rows, cols), f32),
            pltpu.VMEM((2, line - 1, rows, cols), f32),
            pltpu.VMEM((line - 1, rows, cols), f32),
            pltpu.VMEM((line - 1, rows, cols), f32),
            pltpu.VMEM((6, rows, cols), f32),
        ]

    def __init__(self, me, lands, sems, buffers):
        self.me = me
        self.parts, self.y_land, self.up_land, self.down_land, self.last_land = lands
        (self.y_send, self.y_recv, self.up_send, self.up_recv,
         self.down_send, self.down_recv, self.last_send, self.last_recv, self.local) = sems
        (self.got, self.ring, self.up_buf, self.down_buf,
         self.up_load, self.down_load, self.last) = buffers
        self.tiles, self.line = self.parts.shape[0], me.line
        self.groups, self.firsts, self.items = self.counts(self.tiles)

    def tile_of(self, first):
        each = self.group - 1
        return lax.div(first, each) * self.group + lax.rem(first, each) + 1

    def begin(self, tile):
        first = tile - lax.div(tile, self.group) - 1

        @pl.when((lax.rem(tile, self.group) != 0) & (first < self.ahead))
        def _():
            self.y_copy(first).start()

    def y_copy(self, first):
        return remote(
            self.parts.at[self.tile_of(first), :, 1 - self.me.side], self.y_land.at[first],
            self.y_send.at[first], self.y_recv.at[first], self.me.to_side,
        )

    def last_copy(self, group):
        return remote(
            self.last.at[3], self.last_land.at[group],
            self.last_send.at[group], self.last_recv.at[group], self.me.to_side,
        )

    def up_copy(self, item, count):
        slot = lax.rem(item, 2)
        return remote(
            self.up_buf.at[slot, 0:count], self.up_land.at[item, 0:count],
            self.up_send.at[slot], self.up_recv.at[item], self.me.to_up,
        )

    def down_copy(self, item, count):
        slot = lax.rem(item, 2)
        return remote(
            self.down_buf.at[slot, 0:count], self.down_land.at[item, 0:count],
            self.down_send.at[slot], self.down_recv.at[item], self.me.to_down,
        )

    def await_up(self, item, count):
        land = self.up_land.at[item, 0:count]
        remote(land, land, self.up_send.at[0], self.up_recv.at[item], self.me.to_up).wait_recv()

    def await_down(self, item, count):
        land = self.down_land.at[item, 0:count]
        remote(
            land, land, self.down_send.at[0], self.down_recv.at[item], self.me.to_down
        ).wait_recv()

    @property
    def slots(self):
        return self.items + self.lag(self.line) * (self.line - 1)

    def stages(self, s, first, up, down, last):
        me, line, items = self.me, self.line, self.items
        lag, span = self.lag(line), self.group + 1
        pl.when(s < items)(lambda: first(lax.div(s, span), lax.rem(s, span)))

        def at(item, found, body, *more):
            pl.when(found & (item >= 0) & (item < items))(lambda: body(item, *more))

        for k in range(line - 1):
            at(s - lag * k, me.spot == k, up, k, line - 1 - k)
        for k in range(1, line):
            at(s - lag * (line - 1 - k), me.spot == k, down, k, k)
        at(s - lag * (line - 1), s >= 0, last)

    def fetches(self, s):
        me, line = self.me, self.line
        depth, span = self.ring.shape[0], self.group + 1

        def first(at, kind):
            held = self.ring.at[lax.rem(s, depth)]

            @pl.when(kind < 2)
            def _():
                side = jnp.where(kind == 0, 1 - me.side, me.side)
                fetch(self.parts.at[at * self.group, :, side], held, self.local.at[0])

            @pl.when(kind >= 2)
            def _():
                number = at * (self.group - 1) + kind - 2

                @pl.when(number + self.ahead < self.firsts)
                def _():
                    self.y_copy(number + self.ahead).start()

                fetch(self.parts.at[self.tile_of(number), :, me.side], held, self.local.at[0])
                self.y_copy(number).wait()
                fetch(self.y_land.at[number], self.got, self.local.at[1])

        def up(item, k, count):
            if k > 0:
                self.await_up(item, count + 1)
                fetch(
                    self.up_land.at[item, 1 : count + 1], self.up_load.at[0:count],
                    self.local.at[2],
                )

        def down(item, k, count):
            if k < line - 1:
                self.await_down(item, count + 1)
                fetch(
                    self.down_land.at[item, 0:count], self.down_load.at[0:count],
                    self.local.at[3],
                )

        def last(item):
            @pl.when(me.spot == line - 1)
            def _():
                self.await_up(item, 1)

            @pl.when(me.spot == 0)
            def _():
                self.await_down(item, 1)

            @pl.when(me.spot > 0)
            def _():
                fetch(self.up_land.at[item, 0], self.last.at[0], self.local.at[4])

            @pl.when(me.spot < line - 1)
            def _():
                fetch(self.down_land.at[item, me.spot], self.last.at[1], self.local.at[5])

            @pl.when(lax.rem(item, span) == self.group - 2)
            def _():
                at = lax.div(item, span)
                self.last_copy(at).wait()
                fetch(self.last_land.at[at], self.last.at[5], self.local.at[6])

        self.stages(s, first, up, down, last)

    def loaded(self, target, at):
        pltpu.make_async_copy(target, target, self.local.at[at]).wait()

    def sums(self, s, emit):
        me, line = self.me, self.line
        depth, span = self.ring.shape[0], self.group + 1

        def first(at, kind):
            held = lax.rem(s, depth)
            self.loaded(self.ring.at[held], 0)

            @pl.when(kind >= 2)
            def _():
                self.loaded(self.got, 1)
                self.ring[held] = self.ring[held] + self.got[...]

        def up(item, k, count):
            slot, held = lax.rem(item, 2), lax.rem(item, depth)

            @pl.when(item >= 2)
            def _():
                self.up_copy(item, count).wait_send()

            if k > 0:
                self.loaded(self.up_load.at[0:count], 2)
                self.up_buf[slot, 0:count] = self.ring[held, k + 1 : line] + self.up_load[0:count]
            else:
                self.up_buf[slot, 0:count] = self.ring[held, k + 1 : line]
            self.up_copy(item, count).start()

        def down(item, k, count):
            slot, held = lax.rem(item, 2), lax.rem(item, depth)

            @pl.when(item >= 2)
            def _():
                self.down_copy(item, count).wait_send()

            if k < line - 1:
                self.loaded(self.down_load.at[0:count], 3)
                self.down_buf[slot, 0:count] = self.ring[held, 0:count] + self.down_load[0:count]
            else:
                self.down_buf[slot, 0:count] = self.ring[held, 0:count]
            self.down_copy(item, count).start()

        def last(item):
            at, kind = lax.div(item, span), lax.rem(item, span)
            self.last[2] = self.ring[lax.rem(item, depth), me.spot]

            @pl.when(me.spot > 0)
            def _():
                self.loaded(self.last.at[0], 4)
                self.last[2] = self.last[2] + self.last[0]

            @pl.when(me.spot < line - 1)
            def _():
                self.loaded(self.last.at[1], 5)
                self.last[2] = self.last[2] + self.last[1]

            @pl.when(kind == 0)
            def _():
                self.last[3] = self.last[2]
                self.last_copy(at).start()

            @pl.when(kind == 1)
            def _():
                self.last[4] = self.last[2]

            @pl.when(kind > 1)
            def _():
                emit(at * self.group + kind - 1, self.last.at[2], 0)

            @pl.when(kind == self.group - 2)
            def _():
                self.loaded(self.last.at[5], 6)
                self.last[4] = self.last[4] + self.last[5]
                emit(at * self.group, self.last.at[4], 1)

        self.stages(s, first, up, down, last)

    def settle(self, s, emitted):
        def nothing(*_):
            pass

        def last(item):
            kind = lax.rem(item, self.group + 1)
            pl.when(kind > 1)(lambda: emitted(0))
            pl.when(kind == self.group - 2)(lambda: emitted(1))

        self.stages(s, nothing, nothing, nothing, last)

    def step(self, s, emit, emitted):
        self.fetches(s)
        self.sums(s, emit)
        self.settle(s, emitted)

    def finish(self):
        me, line = self.me, self.line
        for k in range(line - 1):
            @pl.when(me.spot == k)
            def _(k=k):
                for item in range(self.items - 2, self.items):
                    self.up_copy(item, line - 1 - k).wait_send()

        for k in range(1, line):
            @pl.when(me.spot == k)
            def _(k=k):
                for item in range(self.items - 2, self.items):
                    self.down_copy(item, k).wait_send()


class NarrowSum:
    @staticmethod
    def sems(chunks):
        dma = pltpu.SemaphoreType.DMA
        return [dma((chunks,)) for _ in range(8)]

    @staticmethod
    def buffers(quarter, width):
        return [
            pltpu.VMEM((2, 2, 2, quarter, width), f32),
            pltpu.VMEM((2, 2, quarter, width), f32),
            pltpu.VMEM((2, 2, quarter, width), f32),
            pltpu.VMEM((2, quarter, width), f32),
            pltpu.VMEM((3, 2, quarter, width), f32),
            pltpu.VMEM((2, 2, quarter, width), f32),
            pltpu.VMEM((2, 2, quarter, width), bf16),
        ]

    def __init__(self, me, sems, buffers):
        self.me = me
        (self.s0, self.r0, self.s1, self.r1, self.s2, self.r2, self.s3, self.r3) = sems
        (self.part, self.core_land, self.half, self.chip_land, self.pair, self.last_land,
         self.low) = buffers
        self.chunks = self.s0.shape[0]

    def copies(self, stage, c):
        me, slot, third = self.me, lax.rem(c, 2), lax.rem(c, 3)
        if stage == 0:
            return remote(self.part.at[slot, 1 - me.core], self.core_land.at[slot],
                          self.s0.at[c], self.r0.at[c], me.to_core)
        if stage == 1:
            return remote(self.half.at[slot, 1 - me.chip], self.chip_land.at[slot],
                          self.s1.at[c], self.r1.at[c], me.to_chip)
        if stage == 2:
            return remote(self.pair.at[third, me.chip], self.pair.at[third, me.chip],
                          self.s2.at[c], self.r2.at[c], me.to_chip)
        return remote(self.pair.at[third], self.last_land.at[slot],
                      self.s3.at[c], self.r3.at[c], me.to_core)

    @property
    def slots(self):
        return self.chunks + 4

    def at_stage(self, s, number, body):
        c = s - number
        pl.when((c >= 0) & (c < self.chunks))(lambda: body(c))

    def step(self, s, produce, work, lower, emit):
        me = self.me

        def stage(number, body):
            def run(c):
                if number > 0:
                    self.copies(number - 1, c).wait()
                body(c, lax.rem(c, 2), lax.rem(c, 3))
                if number < 4:
                    self.copies(number, c).start()

            self.at_stage(s, number, run)

        def four(c, slot, third):
            self.low[me.core] = lower(self.pair[third])
            self.low[1 - me.core] = lower(self.last_land[slot])
            emit(c, self.low)

        def three(c, slot, third):
            pass

        def two(c, slot, third):
            self.pair[third, me.chip] = work(c, self.half[slot, me.chip] + self.chip_land[slot])

        def one(c, slot, third):
            self.half[slot] = self.part[slot, me.core] + self.core_land[slot]

        def zero(c, slot, third):
            pl.when(slot == 0)(lambda: produce(c, self.part))

        stage(4, four)
        stage(3, three)
        stage(2, two)
        stage(1, one)
        stage(0, zero)


def take(refs, count):
    return refs[:count], refs[count:]


def store_part(part, value, columns):
    part[:, :, :, :, columns] = value.reshape(2, 2, 2, value.shape[0] // 8, value.shape[1])


def norm_back(pulled, unit, scale, gain):
    scaled = pulled * gain
    return scale * (scaled - unit * jnp.mean(scaled * unit, axis=-1, keepdims=True))


def half_turn(values):
    return pltpu.roll(values, values.shape[-1] // 2, values.ndim - 1)


def allowed_pairs(keys, rows, starts):
    count = rows.stop - rows.start
    key = lax.broadcasted_iota(jnp.int32, (keys, count), 0)
    query = lax.broadcasted_iota(jnp.int32, (keys, count), 1) + rows.start
    return (key <= query) & (key >= starts)


def attend_kernel(wide, chunks, *refs):
    (tokens, cot, w_query, w_key, w_value, w_output, attn_gain, mlp_gain, query_gain, key_gain,
     cosine, sine, starts), refs = take(refs, 13)
    (mlp_in, mlp_in_t, cot_t, normed_t, hidden_out, q_out, k_out, v_out, q_raw_out, k_raw_out,
     context_out, lse_out), refs = take(refs, 12)
    sems, refs = take(refs, 8)
    buffers, refs = take(refs, 7)
    (hidden_buf, q_low, k_low, v_low, v_t, q_raw, k_raw, context, lse, normed, normed_turn,
     cot_load, cot_turn, low_turn, sem, out_sem) = refs
    me = Spot(wide)
    me.greet(False)
    summing = NarrowSum(me, sems, buffers)
    token_count, width = tokens.shape
    rows = token_count // chunks
    quarter = rows // 4
    block = normed.shape[0]
    per_block = block // rows
    head = query_gain.shape[1]
    q_heads = w_query.shape[1] // head
    group = q_heads // (w_key.shape[1] // head)
    scale = head ** (-0.5)
    step = min(512, width)
    kept = (
        (q_low, q_out), (k_low, k_out), (v_low, v_out), (q_raw, q_raw_out), (k_raw, k_raw_out),
        (context, context_out), (lse, lse_out),
    )

    def attend(i):
        own = slice(i * block, (i + 1) * block)
        keys = (i + 1) * block
        x = tokens[own, :].astype(f32)
        normed[...] = (x * inverse_rms(x) * attn_gain[...]).astype(bf16)
        cos, sin = cosine[own, :], sine[own, :]

        def heads_of(raw, low, gain):
            for h in range(raw.shape[1] // head):
                cut = slice(h * head, (h + 1) * head)
                u = raw[own, cut]
                y = u * inverse_rms(u) * gain[...]
                low[own, cut] = (y * cos + half_turn(y) * sin).astype(bf16)

        q_raw[own, :] = forward_dot(normed[...], w_query[...])
        k_raw[own, :] = forward_dot(normed[...], w_key[...])
        value = forward_dot(normed[...], w_value[...])
        v_low[own, :] = value.astype(bf16)
        v_t[:, own] = value.T.astype(bf16)
        heads_of(q_raw, q_low, query_gain)
        heads_of(k_raw, k_low, key_gain)
        allowed = allowed_pairs(keys, own, starts[:, own])
        for h in range(q_heads):
            cut, kv = slice(h * head, (h + 1) * head), h // group
            kv_cut = slice(kv * head, (kv + 1) * head)
            scores = nt_dot(k_low[0:keys, kv_cut], q_low[own, cut]) * scale
            scores = jnp.where(allowed, scores, masked_score)
            top = jnp.max(scores, axis=0, keepdims=True)
            expd = jnp.exp(scores - top)
            total = jnp.sum(expd, axis=0, keepdims=True)
            probs = (expd / total).astype(bf16)
            lse[h : h + 1, own] = top + jnp.log(total)
            mixed = forward_dot(v_t[kv_cut, 0:keys], probs)
            context[own, cut] = mixed.T.astype(bf16)

    def produce(c, part):
        for i in range(token_count // block):
            pl.when(c == i * per_block)(functools.partial(attend, i))
        left = context[pl.ds(pl.multiple_of(c * rows, 2 * rows), 2 * rows), :]
        for at in range(0, width, step):
            store_part(part, forward_dot(left, w_output[:, at : at + step]), slice(at, at + step))

    def work(c, total):
        at = pl.multiple_of(c * rows + me.core * 2 * quarter + me.chip * quarter, quarter)
        hidden = tokens[pl.ds(at, quarter), :].astype(f32) + total
        hidden_buf[...] = hidden
        fetch(hidden_buf, hidden_out.at[c], sem.at[2])
        return hidden * inverse_rms(hidden)

    def lower(value):
        return (value * mlp_gain[...]).astype(bf16)

    def emit(c, low):
        fetch(low, mlp_in.at[c], sem.at[3])
        low_turn[...] = low[...].reshape(rows, width).T
        at = pl.ds(pl.multiple_of(c * rows, rows), rows)
        fetch(low_turn, mlp_in_t.at[:, at], sem.at[4])

    def settle(s):
        def two(c):
            pltpu.make_async_copy(hidden_buf, hidden_out.at[c], sem.at[2]).wait()

        def four(c):
            pltpu.make_async_copy(summing.low, mlp_in.at[c], sem.at[3]).wait()
            at = pl.ds(pl.multiple_of(c * rows, rows), rows)
            pltpu.make_async_copy(low_turn, mlp_in_t.at[:, at], sem.at[4]).wait()

        summing.at_stage(s, 2, two)
        summing.at_stage(s, 4, four)

    def turn_rows(s):
        at = pl.ds(pl.multiple_of(s * rows, rows), rows)
        fetch(cot.at[at, :], cot_load, sem.at[0]).wait()
        cot_turn[...] = cot_load[...].T
        a = fetch(cot_turn, cot_t.at[:, at], sem.at[1])

        @pl.when(lax.rem(s, per_block) == 0)
        def _():
            normed_turn[...] = normed[...].T
            wide_at = pl.ds(pl.multiple_of(s * rows, block), block)
            fetch(normed_turn, normed_t.at[:, wide_at], sem.at[0]).wait()

        a.wait()

    def body(s, carry):
        summing.step(s, produce, work, lower, emit)
        pl.when(s < chunks)(lambda: turn_rows(s))

        @pl.when(s == chunks - 1)
        def _():
            for at, (a, b) in enumerate(kept):
                fetch(a, b, out_sem.at[at])

        settle(s)
        return carry

    lax.fori_loop(0, summing.slots, body, 0)
    for at, (a, b) in enumerate(kept):
        pltpu.make_async_copy(a, b, out_sem.at[at]).wait()


def outer_tile(left_t, right, stage):
    line, _, rows, _ = stage.shape
    group = max(1, 512 // (2 * rows))
    while line % group:
        group -= 1

    def body(m, carry):
        at = pl.multiple_of(m * group * 2 * rows, group * 2 * rows)
        value = forward_dot(left_t[pl.ds(at, group * 2 * rows), :], right)
        stage[pl.ds(m * group, group)] = value.reshape((group, 2, rows, value.shape[1]))
        return carry

    lax.fori_loop(0, line // group, body, 0)


class SmallSum:
    def __init__(self, me, value, lands, sends, recvs):
        self.me, self.value, self.lands, self.sends, self.recvs = me, value, lands, sends, recvs

    def copy(self, k):
        me = self.me
        who = (me.to_core, me.to_chip, me.to_side)[k] if k < 3 else me.along(k - 2)
        return remote(self.value, self.lands.at[k], self.sends.at[k], self.recvs.at[k], who)

    def step(self, at):
        last = 2 + self.me.line
        stages = [[0], [1], [2], list(range(3, last)), []]
        for number, copies in enumerate(stages):
            @pl.when(at == number)
            def _(number=number, copies=copies):
                if number > 0:
                    for k in stages[number - 1]:
                        self.copy(k).wait()
                    for k in stages[number - 1]:
                        self.value[...] = self.value[...] + self.lands[k]
                for k in copies:
                    self.copy(k).start()


def main_kernel(wide, chunks, *refs):
    (mlp_in, mlp_in_t, cot, cot_t, normed_t, hidden, q_in, k_in, v_in, q_raw, k_raw, context,
     lse_in, tokens, w_gate, w_up, w_down, w_output, w_query, w_key, w_value, cosine, sine,
     starts, attn_gain, mlp_gain, query_gain, key_gain), refs = take(refs, 28)
    (output, grad_tokens, grad_query, grad_key, grad_value, grad_output, grad_gate, grad_up,
     grad_down, gains_out, grad_hidden), refs = take(refs, 11)
    wide_lands, refs = take(refs, 5)
    wide_sems, refs = take(refs, 9)
    sems, refs = take(refs, 8)
    wide_buffers, refs = take(refs, 7)
    buffers, refs = take(refs, 7)
    (acts, gains, gain_lands, turned, gain_send, gain_recv, sem, w_sem, store_sem, emit_sem,
     att_sem) = refs
    me = Spot(wide)
    me.greet(True)
    token_count, width = mlp_in.shape
    hidden_units = w_gate.shape[1]
    tiles, line, _, side_rows, cols = wide_lands[0].shape
    blocks = hidden_units // cols
    mlp_tiles = 3 * blocks
    query_width, kv_width = w_query.shape[1], w_key.shape[1]
    all_heads = query_width + 2 * kv_width
    head = query_gain.shape[1]
    q_heads = query_width // head
    group = q_heads // (kv_width // head)
    scale = head ** (-0.5)
    out_tiles = query_width // cols
    total = WideSum(me, wide_lands, wide_sems, wide_buffers)
    half = token_count // 2
    rows = token_count // chunks
    quarter = rows // 4

    early = (0, 1, 4)

    def emit_tile(tile, value, number):
        def part(first, count, target, turn, every=1, offset=0):
            inside = (tile >= first) & (tile < first + count)
            at = tile - first
            if every > 1:
                inside = inside & (lax.rem(at, every) == offset)
                at = lax.div(at, every)

            @pl.when(inside)
            def _():
                cut = pl.ds(pl.multiple_of(at * cols, cols), cols)
                if turn:
                    turned[number] = value[...].T
                    fetch(turned.at[number], target.at[cut, :], emit_sem.at[number])
                else:
                    fetch(value, target.at[:, cut], emit_sem.at[number])

        part(0, mlp_tiles, grad_down, True, 3, 0)
        part(0, mlp_tiles, grad_gate, False, 3, 1)
        part(0, mlp_tiles, grad_up, False, 3, 2)
        at = mlp_tiles
        part(at, out_tiles, grad_output, True)
        at += out_tiles
        part(at, query_width // cols, grad_query, False)
        at += query_width // cols
        part(at, kv_width // cols, grad_key, False)
        at += kv_width // cols
        part(at, kv_width // cols, grad_value, False)

    def emitted(number):
        pltpu.make_async_copy(turned.at[number], turned.at[number], emit_sem.at[number]).wait()

    def compute(xs, xt, cs, ct, gate_w, up_w, down_w, staged):
        pairs = ((mlp_in, xs), (cot, cs), (cot_t, ct), (mlp_in_t, xt))
        for at, (a, b) in enumerate(pairs):
            fetch(a, b, sem.at[at])

        def weights(b, slot):
            at = pl.ds(pl.multiple_of(b * cols, cols), cols)
            return (
                pltpu.make_async_copy(w_gate.at[:, at], gate_w.at[slot], w_sem.at[slot, 0]),
                pltpu.make_async_copy(w_up.at[:, at], up_w.at[slot], w_sem.at[slot, 1]),
                pltpu.make_async_copy(w_down.at[at, :], down_w.at[slot], w_sem.at[slot, 2]),
            )

        for copy in weights(0, 0):
            copy.start()
        for at, (a, b) in enumerate(pairs):
            pltpu.make_async_copy(a, b, sem.at[at]).wait()

        def store(tile):
            slot = lax.rem(tile, 2)
            return pltpu.make_async_copy(staged.at[slot], total.parts.at[tile], store_sem.at[slot])

        def block(b, carry):
            slot = lax.rem(b, 2)
            for copy in weights(b, slot):
                copy.wait()

            @pl.when(b + 1 < blocks)
            def _():
                for copy in weights(b + 1, 1 - slot):
                    copy.start()

            at = pl.ds(pl.multiple_of(b * cols, cols), cols)

            def some(m, carry):
                own = pl.ds(pl.multiple_of(m * half, half), half)
                gate = forward_dot(xs[own, :], gate_w[slot])
                up = forward_dot(xs[own, :], up_w[slot])
                back = nt_dot(cs[own, :], down_w[slot])
                sig = 1.0 / (1.0 + jnp.exp(-gate))
                silu = gate * sig
                acts[0, own, at] = (silu * up).astype(bf16)
                acts[1, own, at] = (back * up * sig * (1.0 + gate * (1.0 - sig))).astype(bf16)
                acts[2, own, at] = (back * silu).astype(bf16)
                return carry

            lax.fori_loop(0, 2, some, 0)
            for j in range(3):
                tile = 3 * b + j
                outer_tile(ct if j == 0 else xt, acts[j, :, at], staged.at[lax.rem(tile, 2)])
                store(tile).start()

                @pl.when(tile > 0)
                def _(tile=tile):
                    store(tile - 1).wait()
                    total.begin(tile - 1)

            for number, after in enumerate(early):
                pl.when(b == after)(lambda: total.step(number, emit_tile, emitted))
            return carry

        lax.fori_loop(0, blocks, block, 0)
        store(mlp_tiles - 1).wait()

    pl.run_scoped(
        compute,
        pltpu.VMEM(mlp_in.shape, bf16),
        pltpu.VMEM(mlp_in_t.shape, bf16),
        pltpu.VMEM(mlp_in.shape, bf16),
        pltpu.VMEM(mlp_in_t.shape, bf16),
        pltpu.VMEM((2, width, cols), bf16),
        pltpu.VMEM((2, width, cols), bf16),
        pltpu.VMEM((2, cols, width), bf16),
        pltpu.VMEM((2, line, 2, side_rows, cols), f32),
    )

    def pass_on(*held):
        (gate_w, up_w, down_w, hidden_load, token_load, out_buf, out_w, left_t, staged, q_low,
         k_low, v_low, k_t, d_context, right, lse, cos, sin, raw, d_query, d_key, d_value,
         heads) = held
        summing = NarrowSum(me, sems, buffers)
        small = SmallSum(me, gains, gain_lands, gain_send, gain_recv)
        gains[...] = jnp.zeros_like(gains)
        gain_at = (
            slice(0, width), slice(width, 2 * width), slice(2 * width, 2 * width + head),
            slice(2 * width + head, 2 * width + 2 * head),
        )
        loads = ((w_output, out_w), (q_in, q_low), (k_in, k_low), (v_in, v_low), (lse_in, lse),
                 (cosine, cos), (sine, sin))
        for a, b in loads:
            fetch(a, b, sem.at[0]).wait()
        k_t[...] = k_low[...].T
        step = gate_w.shape[1]
        narrow_from = len(early)
        first_attend = narrow_from + chunks + 4
        first_heads = first_attend + q_heads

        def stream(copies, use):
            count = width // step
            for copy in copies(0, 0):
                copy.start()
            for at in range(count):
                if at + 1 < count:
                    for copy in copies(at + 1, (at + 1) % 2):
                        copy.start()
                for copy in copies(at, at % 2):
                    copy.wait()
                use(at % 2, slice(at * step, (at + 1) * step))

        def produce(c, part):
            chunk = lax.rem(c, chunks)
            own = pl.ds(pl.multiple_of(chunk * rows, 2 * rows), 2 * rows)
            kind = lax.div(c, chunks)

            @pl.when(kind == 0)
            def _():
                def copies(at, slot):
                    cut = pl.ds(at * step, step)
                    gate = gate_w.at[slot, :, 0:hidden_units]
                    return (
                        pltpu.make_async_copy(w_gate.at[cut, :], gate, w_sem.at[slot, 0]),
                        pltpu.make_async_copy(w_up.at[cut, :], up_w.at[slot], w_sem.at[slot, 1]),
                    )

                def use(slot, cut):
                    value = nt_dot(acts[1, own, :], gate_w[slot, :, 0:hidden_units])
                    store_part(part, value + nt_dot(acts[2, own, :], up_w[slot]), cut)

                stream(copies, use)

            @pl.when(kind == 1)
            def _():
                def copies(at, slot):
                    cut = pl.ds(at * step, step)
                    return (
                        pltpu.make_async_copy(w_down.at[:, cut], down_w.at[slot], w_sem.at[slot, 2]),
                    )

                def use(slot, cut):
                    store_part(part, forward_dot(acts[0, own, :], down_w[slot]), cut)

                stream(copies, use)

            @pl.when(kind == 2)
            def _():
                def copies(at, slot):
                    cut, start, found = pl.ds(at * step, step), 0, []
                    for j, w in enumerate((w_query, w_key, w_value)):
                        there = gate_w.at[slot, :, start : start + w.shape[1]]
                        found.append(pltpu.make_async_copy(w.at[cut, :], there, w_sem.at[slot, j]))
                        start += w.shape[1]
                    return found

                def use(slot, cut):
                    store_part(part, nt_dot(heads[own, :], gate_w[slot, :, 0:all_heads]), cut)

                stream(copies, use)

        def preload(c):
            chunk, kind = lax.rem(c, chunks), lax.div(c, chunks)

            @pl.when(kind < 2)
            def _():
                fetch(hidden.at[chunk], hidden_load, sem.at[0])

            @pl.when(kind == 0)
            def _():
                fetch(cot.at[own_rows(chunk), :], token_load, sem.at[1])

            @pl.when(kind == 2)
            def _():
                fetch(grad_hidden.at[chunk], hidden_load, sem.at[0])
                fetch(tokens.at[own_rows(chunk), :], token_load, sem.at[1])

        def work(c, pulled):
            kind = lax.div(c, chunks)
            pltpu.make_async_copy(hidden_load, hidden_load, sem.at[0]).wait()

            @pl.when(kind != 1)
            def _():
                pltpu.make_async_copy(token_load, token_load, sem.at[1]).wait()

            @pl.when(kind == 0)
            def _():
                mid = hidden_load[...]
                inverse = inverse_rms(mid)
                unit = mid * inverse
                gains[:, gain_at[1]] += jnp.sum(pulled * unit, axis=0, keepdims=True)
                back = norm_back(pulled, unit, inverse, mlp_gain[...])
                out_buf[...] = token_load[...].astype(f32) + back
                fetch(out_buf, grad_hidden.at[lax.rem(c, chunks)], sem.at[2])

            @pl.when(kind == 1)
            def _():
                out_buf[...] = hidden_load[...] + pulled

            @pl.when(kind == 2)
            def _():
                mid = token_load[...].astype(f32)
                inverse = inverse_rms(mid)
                unit = mid * inverse
                gains[:, gain_at[0]] += jnp.sum(pulled * unit, axis=0, keepdims=True)
                out_buf[...] = hidden_load[...] + norm_back(pulled, unit, inverse, attn_gain[...])

            return out_buf[...]

        def settle(s):
            def two(c):
                @pl.when(lax.div(c, chunks) == 0)
                def _():
                    pltpu.make_async_copy(out_buf, out_buf, sem.at[2]).wait()

            def four(c):
                @pl.when(lax.div(c, chunks) > 0)
                def _():
                    pltpu.make_async_copy(summing.low, summing.low, sem.at[3]).wait()

            summing.at_stage(s, 2, two)
            summing.at_stage(s, 4, four)

        def own_rows(chunk):
            at = chunk * rows + me.core * 2 * quarter + me.chip * quarter
            return pl.ds(pl.multiple_of(at, quarter), quarter)

        def lower(value):
            return value.astype(bf16)

        def emit_rows(c, low):
            chunk = lax.rem(c, chunks)
            kind = lax.div(c, chunks)

            @pl.when(kind == 0)
            def _():
                own = pl.ds(pl.multiple_of(chunk * rows, rows), rows)
                value = low[...].reshape(rows, width)
                d_context[own, :] = nt_dot(value, out_w[...]).astype(bf16)
                left_t[:, own] = value.T

            @pl.when(kind == 1)
            def _():
                fetch(low, output.at[chunk], sem.at[3])

            @pl.when(kind == 2)
            def _():
                fetch(low, grad_tokens.at[chunk], sem.at[3])

        def put(tile, right_value):
            outer_tile(left_t, right_value, staged)
            fetch(staged, total.parts.at[tile], store_sem.at[0]).wait()

        def rope_norm_back(grad, raw_value, gain, at):
            scaled = grad * cos[...] - half_turn(grad) * sin[...]
            inverse = inverse_rms(raw_value)
            unit = raw_value * inverse
            gains[:, at] += jnp.sum(scaled * unit, axis=0, keepdims=True)
            return norm_back(scaled, unit, inverse, gain[...])

        def attend_back(h):
            kv = lax.div(h, group)
            cut = pl.ds(pl.multiple_of(h * head, head), head)
            kv_cut = pl.ds(pl.multiple_of(kv * head, head), head)

            @pl.when(lax.rem(h, group) == 0)
            def _():
                d_key[...] = jnp.zeros_like(d_key)
                d_value[...] = jnp.zeros_like(d_value)

            load = fetch(q_raw.at[:, cut], raw, att_sem.at[0])
            size = min(256, token_count)
            for i in range(token_count // size):
                own, keys = slice(i * size, (i + 1) * size), (i + 1) * size
                q, dc = q_low[own, cut], d_context[own, cut]
                scores = nt_dot(k_low[0:keys, kv_cut], q) * scale
                expd = jnp.exp(scores - lse[pl.ds(h, 1), own])
                probs = jnp.where(allowed_pairs(keys, own, starts[:, own]), expd, 0.0)
                d_value[0:keys, :] += forward_dot(probs.astype(bf16), dc)
                d_probs = nt_dot(v_low[0:keys, kv_cut], dc)
                mean = jnp.sum(probs * d_probs, axis=0, keepdims=True)
                d_scores = (probs * (d_probs - mean)).astype(bf16)
                d_key[0:keys, :] += forward_dot(d_scores, q)
                d_query[own, :] = forward_dot(k_t[kv_cut, 0:keys], d_scores).T
            load.wait()
            heads[:, cut] = rope_norm_back(
                d_query[...] * scale, raw[...], query_gain, gain_at[2]
            ).astype(bf16)

            @pl.when(lax.rem(h, group) == group - 1)
            def _():
                fetch(k_raw.at[:, kv_cut], raw, att_sem.at[0]).wait()
                there = pl.ds(pl.multiple_of(query_width + kv * head, head), head)
                heads[:, there] = rope_norm_back(
                    d_key[...] * scale, raw[...], key_gain, gain_at[3]
                ).astype(bf16)
                there = pl.ds(pl.multiple_of(query_width + kv_width + kv * head, head), head)
                heads[:, there] = d_value[...].astype(bf16)

        small_at = narrow_from + summing.slots - 1

        def body(s, carry):
            @pl.when(s == first_attend)
            def _():
                for t in range(out_tiles):
                    cut = slice(t * cols, (t + 1) * cols)
                    fetch(context.at[:, cut], right, att_sem.at[0]).wait()
                    put(mlp_tiles + t, right[...])

            @pl.when((s >= first_attend) & (s < first_heads))
            def _():
                attend_back(s - first_attend)

            @pl.when(s == first_heads)
            def _():
                fetch(normed_t, left_t, att_sem.at[0]).wait()

                def one(t, carry):
                    put(mlp_tiles + out_tiles + t, heads[:, pl.ds(pl.multiple_of(t * cols, cols), cols)])
                    return carry

                lax.fori_loop(0, all_heads // cols, one, 0)

            summing.at_stage(s - narrow_from, 2, preload)
            total.fetches(s)
            summing.step(s - narrow_from, produce, work, lower, emit_rows)
            total.sums(s, emit_tile)
            total.settle(s, emitted)
            settle(s - narrow_from)
            pl.when(s >= small_at)(lambda: small.step(s - small_at))
            return carry

        lax.fori_loop(narrow_from, max(total.slots, small_at + 5), body, 0)
        total.finish()

    step = min(256, width)
    pl.run_scoped(
        pass_on,
        pltpu.VMEM((2, step, max(hidden_units, all_heads)), bf16),
        pltpu.VMEM((2, step, hidden_units), bf16),
        pltpu.VMEM((2, hidden_units, step), bf16),
        pltpu.VMEM((quarter, width), f32),
        pltpu.VMEM((quarter, width), bf16),
        pltpu.VMEM((quarter, width), f32),
        pltpu.VMEM(w_output.shape, bf16),
        pltpu.VMEM(normed_t.shape, bf16),
        pltpu.VMEM((line, 2, side_rows, cols), f32),
        pltpu.VMEM(q_in.shape, bf16),
        pltpu.VMEM(k_in.shape, bf16),
        pltpu.VMEM(v_in.shape, bf16),
        pltpu.VMEM((kv_width, token_count), bf16),
        pltpu.VMEM(q_in.shape, bf16),
        pltpu.VMEM((token_count, cols), bf16),
        pltpu.VMEM(lse_in.shape, f32),
        pltpu.VMEM(cosine.shape, f32),
        pltpu.VMEM(sine.shape, f32),
        pltpu.VMEM((token_count, head), f32),
        pltpu.VMEM((token_count, head), f32),
        pltpu.VMEM((token_count, head), f32),
        pltpu.VMEM((token_count, head), f32),
        pltpu.VMEM((token_count, all_heads), bf16),
    )
    fetch(gains, gains_out, sem.at[0]).wait()


def call(kernel, collective_id, out_shape, in_specs, out_specs, scratch, arrays):
    return pl.pallas_call(
        kernel,
        out_shape=out_shape,
        in_specs=in_specs,
        out_specs=out_specs,
        scratch_shapes=scratch,
        compiler_params=pltpu.CompilerParams(
            collective_id=collective_id,
            has_side_effects=True,
            vmem_limit_bytes=62 * 1024 * 1024,
        ),
    )(*arrays)


def per_device(
    wide,
    tokens,
    seq_lengths,
    attn_gain,
    w_query,
    key_weight,
    value_weight,
    query_gain,
    key_norm_gain,
    w_output,
    mlp_gain,
    w_gate,
    w_up,
    w_down,
    cotangent,
):
    token_count, width = tokens.shape
    head_dim = query_gain.shape[0]
    query_width, kv_width = w_query.shape[1], key_weight.shape[1]
    hidden_units = w_gate.shape[1]
    all_heads = query_width + 2 * kv_width
    line = wide // 2
    side_rows = width // wide
    chunks = 8
    rows = token_count // chunks
    quarter = rows // 4
    block = min(256, token_count)
    dma = pltpu.SemaphoreType.DMA
    shape = jax.ShapeDtypeStruct

    segment_index, token_positions = layout(seq_lengths, token_count)
    token_positions = token_positions.reshape(-1)
    starts = (jnp.arange(token_count, dtype=jnp.int32) - token_positions)[None]
    cosine, sine = tables(token_positions, head_dim)
    cosine = cosine.reshape(token_count, head_dim)
    sign = jnp.where(jnp.arange(head_dim) < head_dim // 2, -1.0, 1.0).astype(f32)
    sine = sine.reshape(token_count, head_dim) * sign
    q_heads = query_width // head_dim

    kept = [
        shape((token_count, query_width), bf16),
        shape((token_count, kv_width), bf16),
        shape((token_count, kv_width), bf16),
        shape((token_count, query_width), f32),
        shape((token_count, kv_width), f32),
        shape((token_count, query_width), bf16),
        shape((q_heads, token_count), f32),
    ]
    vmem = [pltpu.VMEM(k.shape, k.dtype) for k in kept]
    outs = call(
        lambda *refs: attend_kernel(wide, chunks, *refs),
        1,
        [
            shape((chunks, 2, 2, quarter, width), bf16),
            shape((width, token_count), bf16),
            shape((width, token_count), bf16),
            shape((width, token_count), bf16),
            shape((chunks, quarter, width), f32),
            *kept,
        ],
        [in_vmem, any_space] + [in_vmem] * 11,
        [any_space] * 12,
        [
            *NarrowSum.sems(chunks),
            *NarrowSum.buffers(quarter, width),
            pltpu.VMEM((quarter, width), f32),
            *vmem[:3],
            pltpu.VMEM((kv_width, token_count), bf16),
            *vmem[3:],
            pltpu.VMEM((block, width), bf16),
            pltpu.VMEM((width, block), bf16),
            pltpu.VMEM((rows, width), bf16),
            pltpu.VMEM((width, rows), bf16),
            pltpu.VMEM((width, rows), bf16),
            dma((5,)),
            dma((7,)),
        ],
        (
            tokens, cotangent, w_query, key_weight, value_weight, w_output, attn_gain[None],
            mlp_gain[None], query_gain[None], key_norm_gain[None], cosine, sine, starts,
        ),
    )
    (mlp_in, mlp_in_t, cot_t, normed_t, hidden, q_low, k_low, v_low, q_raw, k_raw, context,
     lse) = outs[:12]

    cols = min(256 if line <= 4 else 128, hidden_units // 6)
    tiles = (3 * hidden_units + query_width + all_heads) // cols
    gain_width = 2 * width + 2 * head_dim
    outs = call(
        lambda *refs: main_kernel(wide, chunks, *refs),
        2,
        [
            shape((chunks, 2, 2, quarter, width), bf16),
            shape((chunks, 2, 2, quarter, width), bf16),
            shape((side_rows, query_width), f32),
            shape((side_rows, kv_width), f32),
            shape((side_rows, kv_width), f32),
            shape((query_width, side_rows), f32),
            shape((side_rows, hidden_units), f32),
            shape((side_rows, hidden_units), f32),
            shape((hidden_units, side_rows), f32),
            shape((1, gain_width), f32),
            shape((chunks, quarter, width), f32),
            *WideSum.lands(tiles, line, side_rows, cols),
        ],
        [any_space] * 23 + [in_vmem] * 5,
        [any_space] * 16,
        [
            *WideSum.sems(tiles),
            *NarrowSum.sems(3 * chunks),
            *WideSum.buffers(line, side_rows, cols),
            *NarrowSum.buffers(quarter, width),
            pltpu.VMEM((3, token_count, hidden_units), bf16),
            pltpu.VMEM((1, gain_width), f32),
            pltpu.VMEM((2 + line, 1, gain_width), f32),
            pltpu.VMEM((2, cols, side_rows), f32),
            dma((2 + line,)),
            dma((2 + line,)),
            dma((4,)),
            dma((2, 3)),
            dma((2,)),
            dma((2,)),
            dma((1,)),
        ],
        (
            mlp_in.reshape(token_count, width), mlp_in_t, cotangent, cot_t, normed_t, hidden,
            q_low, k_low, v_low, q_raw, k_raw, context, lse, tokens, w_gate, w_up, w_down,
            w_output, w_query, key_weight, value_weight, cosine, sine, starts, attn_gain[None],
            mlp_gain[None], query_gain[None], key_norm_gain[None],
        ),
    )
    (output, grad_tokens, shard_query, shard_key, shard_value, shard_output, shard_gate,
     shard_up, shard_down, gains) = outs[:10]
    gains = gains[0]
    at = lax.axis_index("wide")
    head_part = head_dim // wide

    def own(start, size):
        return lax.dynamic_slice_in_dim(gains, start + at * size, size)

    return (
        output.reshape(token_count, width),
        grad_tokens.reshape(token_count, width),
        own(0, side_rows),
        shard_query,
        shard_key,
        shard_value,
        own(2 * width, head_part),
        own(2 * width + head_dim, head_part),
        shard_output,
        own(width, side_rows),
        shard_gate,
        shard_up,
        shard_down,
    )


def solution(mesh):
    def run(*arrays):
        return per_device(mesh.shape["wide"], *arrays)

    return jax.shard_map(
        run,
        mesh=mesh,
        in_specs=(
            P("wide", None),
            P("wide", None),
            P(),
            P(None, "narrow"),
            P(None, "narrow"),
            P(None, "narrow"),
            P(),
            P(),
            P("narrow", None),
            P(),
            P(None, "narrow"),
            P(None, "narrow"),
            P("narrow", None),
            P("wide", None),
        ),
        out_specs=(
            P("wide", None),
            P("wide", None),
            P("wide"),
            P("wide", "narrow"),
            P("wide", "narrow"),
            P("wide", "narrow"),
            P("wide"),
            P("wide"),
            P("narrow", "wide"),
            P("wide"),
            P("wide", "narrow"),
            P("wide", "narrow"),
            P("narrow", "wide"),
        ),
        check_vma=False,
    )
```

```python
import functools

import jax
import jax.numpy as jnp
from jax import lax
from jax.experimental import pallas as pl
from jax.experimental.pallas import tpu as pltpu
from jax.sharding import PartitionSpec as P

norm_eps = 1e-06
rope_base = 1000000.0
masked_score = -1e30
bf16 = jnp.bfloat16
f32 = jnp.float32


def inverse_rms(values):
    return lax.rsqrt(jnp.mean(values * values, axis=-1, keepdims=True) + norm_eps)


def layout(seq_lengths, row_len):
    seq_ends = jnp.cumsum(seq_lengths, axis=-1)
    starts = seq_ends - seq_lengths
    places = jnp.arange(row_len, dtype=jnp.int32)
    segment_index = jnp.sum(
        (places[None, :, None] >= seq_ends[:, None, :]).astype(jnp.int32), axis=-1
    )
    belongs = (
        segment_index[:, :, None]
        == jnp.arange(seq_lengths.shape[-1], dtype=jnp.int32)[None, None, :]
    )
    seq_start = jnp.sum(jnp.where(belongs, starts[:, None, :], 0), axis=-1)
    return (segment_index, places[None, :] - seq_start)


def tables(token_positions, head_dim):
    half_width = head_dim // 2
    frequency = rope_base ** (-2.0 * jnp.arange(half_width, dtype=f32) / head_dim)
    angles = token_positions.astype(f32)[:, None] * frequency[None, :]
    angles = jnp.concatenate([angles, angles], axis=-1)
    return (jnp.cos(angles)[:, None, :], jnp.sin(angles)[:, None, :])


def forward_dot(left_side, right_side):
    return jnp.dot(left_side, right_side, preferred_element_type=f32)


MESH = pl.DeviceIdType.MESH
any_space = pl.BlockSpec(memory_space=pl.ANY)
in_vmem = pl.BlockSpec(memory_space=pltpu.VMEM)


def nt_dot(left_side, right_side):
    return lax.dot_general(
        left_side, right_side, (((1,), (1,)), ((), ())), preferred_element_type=f32
    )


def fetch(source, target, sem):
    copy = pltpu.make_async_copy(source, target, sem)
    copy.start()
    return copy


class Spot:
    def __init__(self, wide):
        self.line = wide // 2
        self.w = lax.axis_index("wide")
        self.n = lax.axis_index("narrow")
        self.spot = lax.div(self.w, 2)
        self.side = lax.rem(self.w, 2)
        self.core = lax.rem(self.n, 2)
        self.chip = lax.div(self.n, 2)
        self.to_core = {"narrow": self.n + 1 - 2 * self.core}
        self.to_chip = {"narrow": self.n + 2 - 4 * self.chip}
        self.to_side = {"wide": self.w + 1 - 2 * self.side}
        self.to_up = {"wide": self.w + 2}
        self.to_down = {"wide": self.w - 2}

    def along(self, distance):
        there = lax.rem(self.spot + distance, self.line)
        return {"wide": there * 2 + self.side}

    def greet(self, line_too):
        barrier = pltpu.get_barrier_semaphore()

        def tell(who):
            pl.semaphore_signal(barrier, inc=1, device_id=who, device_id_type=MESH)

        tell(self.to_core)
        tell(self.to_chip)
        tell(self.to_side)
        if line_too:
            for distance in range(1, self.line):
                tell(self.along(distance))
        pl.semaphore_wait(barrier, 2 + self.line if line_too else 3)


def remote(source, target, send, recv, who):
    return pltpu.make_async_remote_copy(
        src_ref=source, dst_ref=target, send_sem=send, recv_sem=recv,
        device_id=who, device_id_type=MESH,
    )


class WideSum:
    ahead = 3
    join_after = 5
    held_back = 0

    @staticmethod
    def lag(line):
        return 2 if line <= 4 else 1

    @staticmethod
    def numbers(counts):
        early, shared, late = counts
        firsts, pairs = early - 1 + late, 1 + shared
        return early + shared + late, firsts, pairs, firsts + 2 * pairs

    @classmethod
    def lands(cls, counts, line, rows, cols):
        tiles, firsts, pairs, items = cls.numbers(counts)
        return [
            jax.ShapeDtypeStruct((tiles, line, 2, rows, cols), f32),
            jax.ShapeDtypeStruct((firsts, line, rows, cols), f32),
            jax.ShapeDtypeStruct((items, line - 1, rows, cols), f32),
            jax.ShapeDtypeStruct((items, line - 1, rows, cols), f32),
            jax.ShapeDtypeStruct((pairs, rows, cols), f32),
            jax.ShapeDtypeStruct((counts[1], line, rows, cols), f32),
            jax.ShapeDtypeStruct((counts[1], line, rows, cols), f32),
        ]

    @classmethod
    def sems(cls, counts):
        dma = pltpu.SemaphoreType.DMA
        tiles, firsts, pairs, items = cls.numbers(counts)
        return [
            dma((firsts,)), dma((firsts,)), dma((2,)), dma((items,)), dma((2,)), dma((items,)),
            dma((pairs,)), dma((pairs,)), dma((counts[1],)), dma((counts[1],)), dma((7,)),
        ]

    @classmethod
    def buffers(cls, line, rows, cols):
        tile = (line, rows, cols)
        return [
            pltpu.VMEM(tile, f32),
            pltpu.VMEM((cls.lag(line) * (line - 1) + 1,) + tile, f32),
            pltpu.VMEM((2, line - 1, rows, cols), f32),
            pltpu.VMEM((2, line - 1, rows, cols), f32),
            pltpu.VMEM((line - 1, rows, cols), f32),
            pltpu.VMEM((line - 1, rows, cols), f32),
            pltpu.VMEM((4, rows, cols), f32),
            pltpu.VMEM((3, rows, cols), f32),
            pltpu.VMEM((3, rows, cols), f32),
        ]

    def __init__(self, me, counts, ready, lands, sems, buffers):
        self.me, self.line = me, me.line
        self.early, self.shared, self.late = counts
        (self.parts, self.y_land, self.up_land, self.down_land, self.last_land, self.give,
         self.give_land) = lands
        (self.y_send, self.y_recv, self.up_send, self.up_recv, self.down_send, self.down_recv,
         self.last_send, self.last_recv, self.give_send, self.give_recv, self.local) = sems
        (self.got, self.ring, self.up_buf, self.down_buf, self.up_load, self.down_load, self.last,
         self.leave, self.hold) = buffers
        self.tiles, self.firsts, self.pairs, self.items = self.numbers(counts)
        self.shared_from = self.early + 1
        before = self.shared - self.held_back
        self.late_from = self.shared_from + 2 * before
        self.rest_from = self.late_from + self.late
        used = [(2 + u, False, u) for u in range(self.early - 1)]
        used += [(self.shared_from + 2 * t, True, t) for t in range(before)]
        used += [(self.late_from + k, False, self.early - 1 + k) for k in range(self.late)]
        used += [(self.rest_from + 2 * k, True, before + k) for k in range(self.held_back)]
        self.sending = []
        for m in range(self.ahead, len(used)):
            slot, shared, number = used[m]
            late = number - (self.early - 1)
            made = 0 if shared or late < 0 else ready(late)
            at = max(used[m - self.ahead][0], made)
            assert at < slot
            self.sending.append((at, shared, number))

    def item(self, s):
        rest = s >= self.rest_from
        among = s - self.shared_from - jnp.where(rest, self.late, 0)
        start = s < 2
        paired = start | rest | ((among >= 0) & (s < self.late_from))
        pair = jnp.where(start, 0, 1 + lax.div(among, 2))
        half = jnp.where(start, s, lax.rem(among, 2))
        first = jnp.where(among < 0, s - 2, s - self.late_from + self.early - 1)
        return paired, pair, half, first

    def pair_tile(self, pair):
        return jnp.where(pair == 0, 0, self.early - 1 + pair)

    def first_tile(self, first):
        made = self.early - 1
        return jnp.where(first < made, first + 1, first + 1 + self.shared)

    def begin(self, tile):
        @pl.when((tile > 0) & (tile <= self.ahead))
        def _():
            self.y_copy(tile - 1).start()

    def y_copy(self, first):
        return remote(
            self.parts.at[self.first_tile(first), :, 1 - self.me.side], self.y_land.at[first],
            self.y_send.at[first], self.y_recv.at[first], self.me.to_side,
        )

    def give_copy(self, shared):
        return remote(
            self.give.at[shared], self.give_land.at[shared],
            self.give_send.at[shared], self.give_recv.at[shared], self.me.to_side,
        )

    def last_copy(self, pair):
        return remote(
            self.leave.at[lax.rem(pair, 3)], self.last_land.at[pair],
            self.last_send.at[pair], self.last_recv.at[pair], self.me.to_side,
        )

    def up_copy(self, item, count):
        slot = lax.rem(item, 2)
        return remote(
            self.up_buf.at[slot, 0:count], self.up_land.at[item, 0:count],
            self.up_send.at[slot], self.up_recv.at[item], self.me.to_up,
        )

    def down_copy(self, item, count):
        slot = lax.rem(item, 2)
        return remote(
            self.down_buf.at[slot, 0:count], self.down_land.at[item, 0:count],
            self.down_send.at[slot], self.down_recv.at[item], self.me.to_down,
        )

    def await_up(self, item, count):
        land = self.up_land.at[item, 0:count]
        remote(land, land, self.up_send.at[0], self.up_recv.at[item], self.me.to_up).wait_recv()

    def await_down(self, item, count):
        land = self.down_land.at[item, 0:count]
        remote(
            land, land, self.down_send.at[0], self.down_recv.at[item], self.me.to_down
        ).wait_recv()

    @property
    def slots(self):
        return self.items + self.lag(self.line) * (self.line - 1)

    def stages(self, s, first, up, down, last):
        me, line, items = self.me, self.line, self.items
        lag = self.lag(line)
        pl.when(s < items)(lambda: first(*self.item(s)))

        def at(item, found, body, *more):
            pl.when(found & (item >= 0) & (item < items))(lambda: body(item, *more))

        for k in range(line - 1):
            at(s - lag * k, me.spot == k, up, k, line - 1 - k)
        for k in range(1, line):
            at(s - lag * (line - 1 - k), me.spot == k, down, k, k)
        at(s - lag * (line - 1), s >= 0, last)

    @staticmethod
    def here(pair, half):
        return (pair > 0) & (half == 0)

    def joined(self, item):
        before = item - self.join_after
        paired, pair, half, _ = self.item(before)
        now_paired, now_pair, now_half, _ = self.item(item)
        soon = self.pairs - self.held_back
        late = now_paired & (now_half == 1) & (now_pair >= soon)
        joins = late | ((before >= 0) & paired & (half == 0) & (pair < soon))
        return joins, jnp.where(late, now_pair, pair)

    def fetches(self, s):
        me, line = self.me, self.line
        depth = self.ring.shape[0]
        for at, shared, number in self.sending:
            @pl.when(s == at)
            def _(shared=shared, number=number):
                (self.give_copy if shared else self.y_copy)(number).start()

        def first(paired, pair, half, number):
            held = self.ring.at[lax.rem(s, depth)]

            @pl.when(paired & jnp.logical_not(self.here(pair, half)))
            def _():
                side = jnp.where(half == 0, 1 - me.side, me.side)
                fetch(self.parts.at[self.pair_tile(pair), :, side], held, self.local.at[0])

            @pl.when(jnp.logical_not(paired))
            def _():
                fetch(self.parts.at[self.first_tile(number), :, me.side], held, self.local.at[0])
                self.y_copy(number).wait()
                fetch(self.y_land.at[number], self.got, self.local.at[1])

        def up(item, k, count):
            if k > 0:
                self.await_up(item, count + 1)
                fetch(
                    self.up_land.at[item, 1 : count + 1], self.up_load.at[0:count],
                    self.local.at[2],
                )

        def down(item, k, count):
            if k < line - 1:
                self.await_down(item, count + 1)
                fetch(
                    self.down_land.at[item, 0:count], self.down_load.at[0:count],
                    self.local.at[3],
                )

        def last(item):
            @pl.when(me.spot == line - 1)
            def _():
                self.await_up(item, 1)

            @pl.when(me.spot == 0)
            def _():
                self.await_down(item, 1)

            @pl.when(me.spot > 0)
            def _():
                fetch(self.up_land.at[item, 0], self.last.at[0], self.local.at[4])

            @pl.when(me.spot < line - 1)
            def _():
                fetch(self.down_land.at[item, me.spot], self.last.at[1], self.local.at[5])

            joins, pair = self.joined(item)

            @pl.when(joins)
            def _():
                self.last_copy(pair).wait()
                fetch(self.last_land.at[pair], self.last.at[3], self.local.at[6])

        self.stages(s, first, up, down, last)

    def loaded(self, target, at):
        pltpu.make_async_copy(target, target, self.local.at[at]).wait()

    def sums(self, s, emit, emit_shared):
        me, line = self.me, self.line
        depth = self.ring.shape[0]

        def first(paired, pair, half, number):
            held = lax.rem(s, depth)

            @pl.when(jnp.logical_not(paired & self.here(pair, half)))
            def _():
                self.loaded(self.ring.at[held], 0)

            @pl.when(jnp.logical_not(paired))
            def _():
                self.loaded(self.got, 1)
                self.ring[held] = self.ring[held] + self.got[...]

        def up(item, k, count):
            slot, held = lax.rem(item, 2), lax.rem(item, depth)

            @pl.when(item >= 2)
            def _():
                self.up_copy(item, count).wait_send()

            if k > 0:
                self.loaded(self.up_load.at[0:count], 2)
                self.up_buf[slot, 0:count] = self.ring[held, k + 1 : line] + self.up_load[0:count]
            else:
                self.up_buf[slot, 0:count] = self.ring[held, k + 1 : line]
            self.up_copy(item, count).start()

        def down(item, k, count):
            slot, held = lax.rem(item, 2), lax.rem(item, depth)

            @pl.when(item >= 2)
            def _():
                self.down_copy(item, count).wait_send()

            if k < line - 1:
                self.loaded(self.down_load.at[0:count], 3)
                self.down_buf[slot, 0:count] = self.ring[held, 0:count] + self.down_load[0:count]
            else:
                self.down_buf[slot, 0:count] = self.ring[held, 0:count]
            self.down_copy(item, count).start()

        def last(item):
            paired, pair, half, number = self.item(item)
            self.last[2] = self.ring[lax.rem(item, depth), me.spot]

            @pl.when(me.spot > 0)
            def _():
                self.loaded(self.last.at[0], 4)
                self.last[2] = self.last[2] + self.last[0]

            @pl.when(me.spot < line - 1)
            def _():
                self.loaded(self.last.at[1], 5)
                self.last[2] = self.last[2] + self.last[1]

            @pl.when(paired & (half == 0))
            def _():
                self.leave[lax.rem(pair, 3)] = self.last[2]
                self.last_copy(pair).start()

            @pl.when(paired & (half == 1))
            def _():
                self.hold[lax.rem(pair, 3)] = self.last[2]

            @pl.when(jnp.logical_not(paired))
            def _():
                emit(self.first_tile(number), self.last.at[2], 0)

            joins, pair = self.joined(item)

            @pl.when(joins)
            def _():
                self.loaded(self.last.at[3], 6)
                third = lax.rem(pair, 3)

                @pl.when(pair == 0)
                def _():
                    self.hold[third] = self.hold[third] + self.last[3]
                    emit(0, self.hold.at[third], 1)

                @pl.when(pair > 0)
                def _():
                    emit_shared(pair - 1, me.side, self.hold.at[third], 1)
                    emit_shared(pair - 1, 1 - me.side, self.last.at[3], 2)

        self.stages(s, first, up, down, last)

    def settle(self, s, emitted):
        def nothing(*_):
            pass

        def last(item):
            paired, _, _, _ = self.item(item)
            pl.when(jnp.logical_not(paired))(lambda: emitted(0))
            joins, pair = self.joined(item)
            pl.when(joins)(lambda: emitted(1))
            pl.when(joins & (pair > 0))(lambda: emitted(2))

        self.stages(s, nothing, nothing, nothing, last)

    def step(self, s, emit, emit_shared, emitted):
        self.fetches(s)
        self.sums(s, emit, emit_shared)
        self.settle(s, emitted)

    def finish(self):
        me, line = self.me, self.line
        for k in range(line - 1):
            @pl.when(me.spot == k)
            def _(k=k):
                for item in range(self.items - 2, self.items):
                    self.up_copy(item, line - 1 - k).wait_send()

        for k in range(1, line):
            @pl.when(me.spot == k)
            def _(k=k):
                for item in range(self.items - 2, self.items):
                    self.down_copy(item, k).wait_send()


class NarrowSum:
    @staticmethod
    def sems(chunks):
        dma = pltpu.SemaphoreType.DMA
        return [dma((chunks,)) for _ in range(8)]

    @staticmethod
    def buffers(quarter, width):
        return [
            pltpu.VMEM((2, 2, 2, quarter, width), f32),
            pltpu.VMEM((2, 2, quarter, width), f32),
            pltpu.VMEM((2, 2, quarter, width), f32),
            pltpu.VMEM((2, quarter, width), f32),
            pltpu.VMEM((3, 2, quarter, width), f32),
            pltpu.VMEM((2, 2, quarter, width), f32),
            pltpu.VMEM((2, 2, quarter, width), bf16),
        ]

    def __init__(self, me, sems, buffers):
        self.me = me
        (self.s0, self.r0, self.s1, self.r1, self.s2, self.r2, self.s3, self.r3) = sems
        (self.part, self.core_land, self.half, self.chip_land, self.pair, self.last_land,
         self.low) = buffers
        self.chunks = self.s0.shape[0]

    def copies(self, stage, c):
        me, slot, third = self.me, lax.rem(c, 2), lax.rem(c, 3)
        if stage == 0:
            return remote(self.part.at[slot, 1 - me.core], self.core_land.at[slot],
                          self.s0.at[c], self.r0.at[c], me.to_core)
        if stage == 1:
            return remote(self.half.at[slot, 1 - me.chip], self.chip_land.at[slot],
                          self.s1.at[c], self.r1.at[c], me.to_chip)
        if stage == 2:
            return remote(self.pair.at[third, me.chip], self.pair.at[third, me.chip],
                          self.s2.at[c], self.r2.at[c], me.to_chip)
        return remote(self.pair.at[third], self.last_land.at[slot],
                      self.s3.at[c], self.r3.at[c], me.to_core)

    @property
    def slots(self):
        return self.chunks + 4

    def at_stage(self, s, number, body):
        c = s - number
        pl.when((c >= 0) & (c < self.chunks))(lambda: body(c))

    def step(self, s, produce, work, lower, emit, beside=None):
        me = self.me

        def stage(number, body):
            def run(c):
                if number > 0:
                    self.copies(number - 1, c).wait()
                body(c, lax.rem(c, 2), lax.rem(c, 3))
                if number < 4:
                    self.copies(number, c).start()

            self.at_stage(s, number, run)

        def four(c, slot, third):
            self.low[me.core] = lower(self.pair[third])
            self.low[1 - me.core] = lower(self.last_land[slot])
            emit(c, self.low)

        def three(c, slot, third):
            if beside is not None:
                beside(c, self.pair.at[third])

        def two(c, slot, third):
            self.pair[third, me.chip] = work(c, self.half[slot, me.chip] + self.chip_land[slot])

        def one(c, slot, third):
            self.half[slot] = self.part[slot, me.core] + self.core_land[slot]

        def zero(c, slot, third):
            pl.when(slot == 0)(lambda: produce(c, self.part))

        stage(4, four)
        stage(3, three)
        stage(2, two)
        stage(1, one)
        stage(0, zero)


def take(refs, count):
    return refs[:count], refs[count:]


def store_part(part, value, columns):
    part[:, :, :, :, columns] = value.reshape(2, 2, 2, value.shape[0] // 8, value.shape[1])


def norm_back(pulled, unit, scale, gain):
    scaled = pulled * gain
    return scale * (scaled - unit * jnp.mean(scaled * unit, axis=-1, keepdims=True))


def half_turn(values):
    return pltpu.roll(values, values.shape[-1] // 2, values.ndim - 1)


def allowed_pairs(keys, rows, starts):
    count = rows.stop - rows.start
    key = lax.broadcasted_iota(jnp.int32, (keys, count), 0)
    query = lax.broadcasted_iota(jnp.int32, (keys, count), 1) + rows.start
    return (key <= query) & (key >= starts)


def attend_kernel(wide, chunks, *refs):
    (tokens, cot, w_query, w_key, w_value, w_output, attn_gain, mlp_gain, query_gain, key_gain,
     cosine, sine, starts), refs = take(refs, 13)
    (mlp_in, mlp_in_t, cot_t, normed_t, hidden_out, q_out, k_out, v_out, q_raw_out, k_raw_out,
     context_out, lse_out, other_out, rest_out), refs = take(refs, 14)
    sems, refs = take(refs, 8)
    buffers, refs = take(refs, 7)
    (hidden_buf, q_low, k_low, v_low, v_t, q_raw, k_raw, context, lse, normed, normed_turn,
     cot_load, cot_turn, low_turn, sem, out_sem, give_sem, take_sem) = refs
    me = Spot(wide)
    me.greet(False)
    summing = NarrowSum(me, sems, buffers)
    token_count, width = tokens.shape
    rows = token_count // chunks
    quarter = rows // 4
    block = normed.shape[0]
    per_block = block // rows
    head = query_gain.shape[1]
    q_heads = w_query.shape[1] // head
    group = q_heads // (w_key.shape[1] // head)
    scale = head ** (-0.5)
    step = min(512, width)
    kept = (
        (q_low, q_out), (k_low, k_out), (v_low, v_out), (q_raw, q_raw_out), (k_raw, k_raw_out),
        (context, context_out), (lse, lse_out),
    )

    def attend(i):
        own = slice(i * block, (i + 1) * block)
        keys = (i + 1) * block
        x = tokens[own, :].astype(f32)
        normed[...] = (x * inverse_rms(x) * attn_gain[...]).astype(bf16)
        cos, sin = cosine[own, :], sine[own, :]

        def heads_of(raw, low, gain):
            for h in range(raw.shape[1] // head):
                cut = slice(h * head, (h + 1) * head)
                u = raw[own, cut]
                y = u * inverse_rms(u) * gain[...]
                low[own, cut] = (y * cos + half_turn(y) * sin).astype(bf16)

        q_raw[own, :] = forward_dot(normed[...], w_query[...])
        k_raw[own, :] = forward_dot(normed[...], w_key[...])
        value = forward_dot(normed[...], w_value[...])
        v_low[own, :] = value.astype(bf16)
        v_t[:, own] = value.T.astype(bf16)
        heads_of(q_raw, q_low, query_gain)
        heads_of(k_raw, k_low, key_gain)
        allowed = allowed_pairs(keys, own, starts[:, own])
        for h in range(q_heads):
            cut, kv = slice(h * head, (h + 1) * head), h // group
            kv_cut = slice(kv * head, (kv + 1) * head)
            scores = nt_dot(k_low[0:keys, kv_cut], q_low[own, cut]) * scale
            scores = jnp.where(allowed, scores, masked_score)
            top = jnp.max(scores, axis=0, keepdims=True)
            expd = jnp.exp(scores - top)
            total = jnp.sum(expd, axis=0, keepdims=True)
            probs = (expd / total).astype(bf16)
            lse[h : h + 1, own] = top + jnp.log(total)
            mixed = forward_dot(v_t[kv_cut, 0:keys], probs)
            context[own, cut] = mixed.T.astype(bf16)

    def produce(c, part):
        for i in range(token_count // block):
            pl.when(c == i * per_block)(functools.partial(attend, i))
        left = context[pl.ds(pl.multiple_of(c * rows, 2 * rows), 2 * rows), :]
        for at in range(0, width, step):
            store_part(part, forward_dot(left, w_output[:, at : at + step]), slice(at, at + step))

    def work(c, total):
        at = pl.multiple_of(c * rows + me.core * 2 * quarter + me.chip * quarter, quarter)
        hidden = tokens[pl.ds(at, quarter), :].astype(f32) + total
        hidden_buf[...] = hidden
        fetch(hidden_buf, hidden_out.at[c], sem.at[2])
        return hidden * inverse_rms(hidden)

    def lower(value):
        return (value * mlp_gain[...]).astype(bf16)

    def emit(c, low):
        @pl.when(c < chunks - 1)
        def _():
            beside(c, summing.pair.at[lax.rem(c, 3)]).wait_send()

        @pl.when(c == chunks - 1)
        def _():
            pltpu.make_async_copy(summing.pair.at[lax.rem(c, 3)], rest_out, sem.at[5]).wait()

        fetch(low, mlp_in.at[c], sem.at[3])
        low_turn[...] = low[...].reshape(rows, width).T
        at = pl.ds(pl.multiple_of(c * rows, rows), rows)
        fetch(low_turn, mlp_in_t.at[:, at], sem.at[4])

    def settle(s):
        def two(c):
            pltpu.make_async_copy(hidden_buf, hidden_out.at[c], sem.at[2]).wait()

        def four(c):
            pltpu.make_async_copy(summing.low, mlp_in.at[c], sem.at[3]).wait()
            at = pl.ds(pl.multiple_of(c * rows, rows), rows)
            pltpu.make_async_copy(low_turn, mlp_in_t.at[:, at], sem.at[4]).wait()

        summing.at_stage(s, 2, two)
        summing.at_stage(s, 4, four)

    def beside(c, half):
        return remote(half, other_out.at[c], give_sem.at[c], take_sem.at[c], me.to_side)

    def begin_beside(c, half):
        @pl.when(c < chunks - 1)
        def _():
            beside(c, half).start()

        @pl.when(c == chunks - 1)
        def _():
            fetch(half, rest_out, sem.at[5])

    def turn_rows(s):
        at = pl.ds(pl.multiple_of(s * rows, rows), rows)
        fetch(cot.at[at, :], cot_load, sem.at[0]).wait()
        cot_turn[...] = cot_load[...].T
        a = fetch(cot_turn, cot_t.at[:, at], sem.at[1])

        @pl.when(lax.rem(s, per_block) == 0)
        def _():
            normed_turn[...] = normed[...].T
            wide_at = pl.ds(pl.multiple_of(s * rows, block), block)
            fetch(normed_turn, normed_t.at[:, wide_at], sem.at[0]).wait()

        a.wait()

    def body(s, carry):
        summing.step(s, produce, work, lower, emit, begin_beside)
        pl.when(s < chunks)(lambda: turn_rows(s))

        @pl.when(s == chunks - 1)
        def _():
            for at, (a, b) in enumerate(kept):
                fetch(a, b, out_sem.at[at])

        settle(s)
        return carry

    lax.fori_loop(0, summing.slots, body, 0)
    for at, (a, b) in enumerate(kept):
        pltpu.make_async_copy(a, b, out_sem.at[at]).wait()
    for c in range(chunks - 1):
        beside(c, summing.pair.at[c % 3]).wait_recv()


def outer_tile(left_t, right, stage):
    line, _, rows, _ = stage.shape
    group = max(1, 512 // (2 * rows))
    while line % group:
        group -= 1

    def body(m, carry):
        at = pl.multiple_of(m * group * 2 * rows, group * 2 * rows)
        value = forward_dot(left_t[pl.ds(at, group * 2 * rows), :], right)
        stage[pl.ds(m * group, group)] = value.reshape((group, 2, rows, value.shape[1]))
        return carry

    lax.fori_loop(0, line // group, body, 0)


class SmallSum:
    def __init__(self, me, value, lands, sends, recvs):
        self.me, self.value, self.lands, self.sends, self.recvs = me, value, lands, sends, recvs

    def copy(self, k):
        me = self.me
        who = (me.to_core, me.to_chip, me.to_side)[k] if k < 3 else me.along(k - 2)
        return remote(self.value, self.lands.at[k], self.sends.at[k], self.recvs.at[k], who)

    def step(self, at):
        last = 2 + self.me.line
        stages = [[0], [1], [2], list(range(3, last)), []]
        for number, copies in enumerate(stages):
            @pl.when(at == number)
            def _(number=number, copies=copies):
                if number > 0:
                    for k in stages[number - 1]:
                        self.copy(k).wait()
                    for k in stages[number - 1]:
                        self.value[...] = self.value[...] + self.lands[k]
                for k in copies:
                    self.copy(k).start()


def main_kernel(wide, chunks, counts, *refs):
    (mlp_in, mlp_in_t, cot, cot_t, normed_t, hidden, other, rest, q_in, k_in, v_in, q_raw, k_raw,
     context, lse_in, tokens, w_gate, w_up, w_down, w_output, w_query, w_key, w_value, cosine, sine,
     starts, attn_gain, mlp_gain, query_gain, key_gain), refs = take(refs, 30)
    (output, grad_tokens, grad_query, grad_key, grad_value, grad_output, grad_gate, grad_up,
     grad_down, gains_out, grad_hidden, inner_out, other_land, rest_land, rest_core,
     other_t), refs = take(refs, 16)
    wide_lands, refs = take(refs, 7)
    wide_sems, refs = take(refs, 11)
    sems, refs = take(refs, 8)
    wide_buffers, refs = take(refs, 9)
    buffers, refs = take(refs, 7)
    (acts, gains, gain_lands, turned, gain_send, gain_recv, sem, w_sem, store_sem, emit_sem,
     att_sem, give_sem, other_sem) = refs
    me = Spot(wide)
    me.greet(True)
    token_count, width = mlp_in.shape
    hidden_units = w_gate.shape[1]
    tiles, line, _, side_rows, cols = wide_lands[0].shape
    blocks = hidden_units // cols
    early_tiles, shared_tiles, late_tiles = counts
    late_from = early_tiles + shared_tiles
    query_width, kv_width = w_query.shape[1], w_key.shape[1]
    all_heads = query_width + 2 * kv_width
    head = query_gain.shape[1]
    q_heads = query_width // head
    group = q_heads // (kv_width // head)
    scale = head ** (-0.5)
    out_tiles = query_width // cols
    narrow_from, pace = 2, 6
    first_attend = chunks + 4
    heads_at_once = 2
    first_heads = first_attend + q_heads // heads_at_once

    def slot_at(r):
        return narrow_from + r - r // pace

    total = WideSum(
        me, counts, lambda late: slot_at(first_attend if late < out_tiles else first_heads),
        wide_lands, wide_sems, wide_buffers,
    )
    other_copy = remote(other, other_land, other_sem.at[0], other_sem.at[1], me.to_core)
    other_copy.start()
    rest_side = remote(rest, rest_land, other_sem.at[6], other_sem.at[7], me.to_side)
    rest_side.start()
    rest_pass = remote(rest_land, rest_core, other_sem.at[8], other_sem.at[9], me.to_core)
    half = token_count // 2
    rows = token_count // chunks
    quarter = rows // 4

    def block_of(t):
        return lax.rem(t, 2) * (blocks // 2) + lax.div(t, 2)

    def half_of(b):
        return lax.div(b, blocks // 2)

    def columns(at):
        return pl.ds(pl.multiple_of(at * cols, cols), cols)

    def emit_tile(tile, value, number):
        def part(first, count, target, turn, place):
            @pl.when((tile >= first) & (tile < first + count))
            def _():
                cut = columns(place(tile - first))
                if turn:
                    turned[number] = value[...].T
                    fetch(turned.at[number], target.at[cut, :], emit_sem.at[number])
                else:
                    fetch(value, target.at[:, cut], emit_sem.at[number])

        def same(at):
            return at

        part(0, early_tiles, grad_down, True, block_of)
        at = late_from
        part(at, out_tiles, grad_output, True, same)
        at += out_tiles
        part(at, query_width // cols, grad_query, False, same)
        at += query_width // cols
        part(at, kv_width // cols, grad_key, False, same)
        at += kv_width // cols
        part(at, kv_width // cols, grad_value, False, same)

    def emit_shared(t, side, value, number):
        cut = columns(side * (blocks // 2) + lax.div(t, 2))

        @pl.when(lax.rem(t, 2) == 0)
        def _():
            fetch(value, grad_gate.at[:, cut], emit_sem.at[number])

        @pl.when(lax.rem(t, 2) == 1)
        def _():
            fetch(value, grad_up.at[:, cut], emit_sem.at[number])

    def emitted(number):
        pltpu.make_async_copy(turned.at[0], turned.at[0], emit_sem.at[number]).wait()

    def compute(xs, cs, ct, gate_w, up_w, down_w, staged, inner, gives):
        pairs = ((mlp_in, xs), (cot, cs), (cot_t, ct))
        for at, (source, target) in enumerate(pairs[:2]):
            fetch(source, target, sem.at[at])

        def weights(t, slot):
            at = columns(block_of(t))
            return (
                pltpu.make_async_copy(w_gate.at[:, at], gate_w.at[slot], w_sem.at[slot, 0]),
                pltpu.make_async_copy(w_up.at[:, at], up_w.at[slot], w_sem.at[slot, 1]),
                pltpu.make_async_copy(w_down.at[at, :], down_w.at[slot], w_sem.at[slot, 2]),
            )

        for copy in weights(0, 0):
            copy.start()
        for at, (source, target) in enumerate(pairs[:2]):
            pltpu.make_async_copy(source, target, sem.at[at]).wait()
        fetch(cot_t, ct, sem.at[2])

        def store(tile):
            slot = lax.rem(tile, 2)
            return pltpu.make_async_copy(staged.at[slot], total.parts.at[tile], store_sem.at[slot])

        def store_inner(t):
            slot = lax.rem(t, 2)
            target = inner_out.at[:, columns(block_of(t))]
            return pltpu.make_async_copy(inner.at[slot], target, give_sem.at[2 + slot])

        def store_gives(t):
            return [
                pltpu.make_async_copy(
                    gives.at[j], total.give.at[2 * lax.div(t, 2) + j], give_sem.at[j]
                )
                for j in range(2)
            ]

        def leaves(t):
            return half_of(block_of(t)) != me.side

        def block(t, carry):
            slot = lax.rem(t, 2)
            for copy in weights(t, slot):
                copy.wait()

            @pl.when(t + 1 < blocks)
            def _():
                for copy in weights(t + 1, 1 - slot):
                    copy.start()

            @pl.when(t >= 2)
            def _():
                store_inner(t - 2).wait()

            at = columns(block_of(t))

            def some(m, carry):
                own = pl.ds(pl.multiple_of(m * half, half), half)
                gate = forward_dot(xs[own, :], gate_w[slot])
                up = forward_dot(xs[own, :], up_w[slot])
                back = nt_dot(cs[own, :], down_w[slot])
                sig = 1.0 / (1.0 + jnp.exp(-gate))
                silu = gate * sig
                inner[slot, own, :] = (silu * up).astype(bf16)
                grad_gate_low = (back * up * sig * (1.0 + gate * (1.0 - sig))).astype(bf16)
                grad_up_low = (back * silu).astype(bf16)
                acts[0, own, at] = grad_gate_low
                acts[1, own, at] = grad_up_low

                @pl.when(leaves(t))
                def _():
                    lines = line // 2
                    there = pl.ds(m * lines, lines)
                    shape = (lines, side_rows, cols)
                    gives[0, there] = grad_gate_low.astype(f32).reshape(shape)
                    gives[1, there] = grad_up_low.astype(f32).reshape(shape)

                return carry

            lax.fori_loop(0, 2, some, 0)
            store_inner(t).start()

            @pl.when(leaves(t))
            def _():
                for copy in store_gives(t):
                    copy.start()

            @pl.when(t == 0)
            def _():
                pltpu.make_async_copy(cot_t, ct, sem.at[2]).wait()

            outer_tile(ct, inner[slot], staged.at[slot])
            store(t).start()

            @pl.when(t == 0)
            def _():
                store(t).wait()

            @pl.when(t > 1)
            def _():
                store(t - 1).wait()
                total.begin(t - 1)

            @pl.when(leaves(t))
            def _():
                for copy in store_gives(t):
                    copy.wait()

            for number, after in enumerate((0, 2)):
                pl.when(t == after)(
                    lambda number=number: total.step(number, emit_tile, emit_shared, emitted)
                )
            return carry

        lax.fori_loop(0, blocks, block, 0)
        store(blocks - 1).wait()
        store_inner(blocks - 2).wait()
        store_inner(blocks - 1).wait()

    pl.run_scoped(
        compute,
        pltpu.VMEM(mlp_in.shape, bf16),
        pltpu.VMEM(mlp_in.shape, bf16),
        pltpu.VMEM(mlp_in_t.shape, bf16),
        pltpu.VMEM((2, width, cols), bf16),
        pltpu.VMEM((2, width, cols), bf16),
        pltpu.VMEM((2, cols, width), bf16),
        pltpu.VMEM((2, line, 2, side_rows, cols), f32),
        pltpu.VMEM((2, token_count, cols), bf16),
        pltpu.VMEM((2, line, side_rows, cols), f32),
    )

    def pass_on(*held):
        (gate_w, up_w, down_w, hidden_load, token_load, out_buf, out_w, left_t, staged, q_low,
         k_low, v_low, k_t, d_context, right, lse, cos, sin, raw, d_query, d_key, d_value,
         heads, inner_load, other_load, other_turn, left_cut) = held
        summing = NarrowSum(me, sems, buffers)
        small = SmallSum(me, gains, gain_lands, gain_send, gain_recv)
        gains[...] = jnp.zeros_like(gains)
        gain_at = (
            slice(0, width), slice(width, 2 * width), slice(2 * width, 2 * width + head),
            slice(2 * width + head, 2 * width + 2 * head),
        )
        loads = ((w_output, out_w), (q_in, q_low), (k_in, k_low), (v_in, v_low), (lse_in, lse),
                 (cosine, cos), (sine, sin))
        for a, b in loads:
            fetch(a, b, sem.at[0]).wait()
        k_t[...] = k_low[...].T
        step = gate_w.shape[1]

        def stream(copies, use):
            count = width // step
            for copy in copies(0, 0):
                copy.start()
            for at in range(count):
                if at + 1 < count:
                    for copy in copies(at + 1, (at + 1) % 2):
                        copy.start()
                for copy in copies(at, at % 2):
                    copy.wait()
                use(at % 2, slice(at * step, (at + 1) * step))

        def produce(c, part):
            chunk = lax.rem(c, chunks)
            own = pl.ds(pl.multiple_of(chunk * rows, 2 * rows), 2 * rows)
            kind = lax.div(c, chunks)

            @pl.when(kind == 0)
            def _():
                def copies(at, slot):
                    cut = pl.ds(at * step, step)
                    gate = gate_w.at[slot, :, 0:hidden_units]
                    return (
                        pltpu.make_async_copy(w_gate.at[cut, :], gate, w_sem.at[slot, 0]),
                        pltpu.make_async_copy(w_up.at[cut, :], up_w.at[slot], w_sem.at[slot, 1]),
                    )

                def use(slot, cut):
                    value = nt_dot(acts[0, own, :], gate_w[slot, :, 0:hidden_units])
                    store_part(part, value + nt_dot(acts[1, own, :], up_w[slot]), cut)

                stream(copies, use)

            @pl.when(kind == 1)
            def _():
                fetch(inner_out.at[own, :], inner_load, att_sem.at[0]).wait()

                def copies(at, slot):
                    cut = pl.ds(at * step, step)
                    return (
                        pltpu.make_async_copy(w_down.at[:, cut], down_w.at[slot], w_sem.at[slot, 2]),
                    )

                def use(slot, cut):
                    store_part(part, forward_dot(inner_load[...], down_w[slot]), cut)

                stream(copies, use)

            @pl.when(kind == 2)
            def _():
                def copies(at, slot):
                    cut, start, found = pl.ds(at * step, step), 0, []
                    for j, w in enumerate((w_query, w_key, w_value)):
                        there = gate_w.at[slot, :, start : start + w.shape[1]]
                        found.append(pltpu.make_async_copy(w.at[cut, :], there, w_sem.at[slot, j]))
                        start += w.shape[1]
                    return found

                def use(slot, cut):
                    store_part(part, nt_dot(heads[own, :], gate_w[slot, :, 0:all_heads]), cut)

                stream(copies, use)

        def preload(c):
            chunk, kind = lax.rem(c, chunks), lax.div(c, chunks)

            @pl.when(kind < 2)
            def _():
                fetch(hidden.at[chunk], hidden_load, sem.at[0])

            @pl.when(kind == 0)
            def _():
                fetch(cot.at[own_rows(chunk), :], token_load, sem.at[1])

            @pl.when(kind == 2)
            def _():
                fetch(grad_hidden.at[chunk], hidden_load, sem.at[0])
                fetch(tokens.at[own_rows(chunk), :], token_load, sem.at[1])

        def work(c, pulled):
            kind = lax.div(c, chunks)
            pltpu.make_async_copy(hidden_load, hidden_load, sem.at[0]).wait()

            @pl.when(kind != 1)
            def _():
                pltpu.make_async_copy(token_load, token_load, sem.at[1]).wait()

            @pl.when(kind == 0)
            def _():
                mid = hidden_load[...]
                inverse = inverse_rms(mid)
                unit = mid * inverse
                gains[:, gain_at[1]] += jnp.sum(pulled * unit, axis=0, keepdims=True)
                back = norm_back(pulled, unit, inverse, mlp_gain[...])
                out_buf[...] = token_load[...].astype(f32) + back
                fetch(out_buf, grad_hidden.at[lax.rem(c, chunks)], sem.at[2])

            @pl.when(kind == 1)
            def _():
                out_buf[...] = hidden_load[...] + pulled

            @pl.when(kind == 2)
            def _():
                mid = token_load[...].astype(f32)
                inverse = inverse_rms(mid)
                unit = mid * inverse
                gains[:, gain_at[0]] += jnp.sum(pulled * unit, axis=0, keepdims=True)
                out_buf[...] = hidden_load[...] + norm_back(pulled, unit, inverse, attn_gain[...])

            return out_buf[...]

        def settle(s):
            def two(c):
                @pl.when(lax.div(c, chunks) == 0)
                def _():
                    pltpu.make_async_copy(out_buf, out_buf, sem.at[2]).wait()

            def four(c):
                @pl.when(lax.div(c, chunks) > 0)
                def _():
                    pltpu.make_async_copy(summing.low, summing.low, sem.at[3]).wait()

            summing.at_stage(s, 2, two)
            summing.at_stage(s, 4, four)

        def own_rows(chunk):
            at = chunk * rows + me.core * 2 * quarter + me.chip * quarter
            return pl.ds(pl.multiple_of(at, quarter), quarter)

        def lower(value):
            return value.astype(bf16)

        def emit_rows(c, low):
            chunk = lax.rem(c, chunks)
            kind = lax.div(c, chunks)

            @pl.when(kind == 0)
            def _():
                own = pl.ds(pl.multiple_of(chunk * rows, rows), rows)
                value = low[...].reshape(rows, width)
                d_context[own, :] = nt_dot(value, out_w[...]).astype(bf16)
                left_t[:, own] = value.T

            @pl.when(kind == 1)
            def _():
                fetch(low, output.at[chunk], sem.at[3])

            @pl.when(kind == 2)
            def _():
                fetch(low, grad_tokens.at[chunk], sem.at[3])

        def take_other(c):
            mine, theirs = other_load.at[me.core], other_load.at[1 - me.core]

            @pl.when(c < chunks - 1)
            def _():
                a = fetch(other.at[c], mine, att_sem.at[0])
                fetch(other_land.at[c], theirs, give_sem.at[0]).wait()
                a.wait()

            @pl.when(c == chunks - 1)
            def _():
                rest_pass.wait()
                a = fetch(rest_land, mine, att_sem.at[0])
                fetch(rest_core, theirs, give_sem.at[0]).wait()
                a.wait()

            value = (other_load[...] * mlp_gain[...][None, None]).astype(bf16)
            other_turn[...] = value.reshape(rows, width).T
            at = pl.ds(pl.multiple_of(c * rows, rows), rows)
            fetch(other_turn, other_t.at[:, at], att_sem.at[0]).wait()

        def put_shared(t, s):
            total.give_copy(t).wait()
            load = fetch(total.give_land.at[t], total.got, att_sem.at[0])
            mine = acts[lax.rem(t, 2), :, columns(me.side * (blocks // 2) + lax.div(t, 2))]
            group = left_cut.shape[2]
            count = width // group

            def copies(m, slot):
                at = pl.ds(pl.multiple_of(m * group, group), group)
                return (
                    pltpu.make_async_copy(mlp_in_t.at[at, :], left_cut.at[slot, 0], other_sem.at[2 + slot]),
                    pltpu.make_async_copy(other_t.at[at, :], left_cut.at[slot, 1], other_sem.at[4 + slot]),
                )

            for copy in copies(0, 0):
                copy.start()
            load.wait()
            right[...] = total.got[...].reshape(token_count, cols).astype(bf16)

            def one(m, carry):
                slot = lax.rem(m, 2)
                for copy in copies(m, slot):
                    copy.wait()

                @pl.when(m + 1 < count)
                def _():
                    for copy in copies(m + 1, 1 - slot):
                        copy.start()

                value = forward_dot(left_cut[slot, 0], mine) + forward_dot(left_cut[slot, 1], right[...])
                lines = group // (2 * side_rows)
                staged[pl.ds(m * lines, lines)] = value.reshape((lines, 2, side_rows, cols))
                return carry

            lax.fori_loop(0, count, one, 0)
            fetch(staged, total.parts.at[early_tiles + t], store_sem.at[0])
            total.ring[lax.rem(s, total.ring.shape[0])] = staged[:, 1 - me.side]

        def shared_stored():
            pltpu.make_async_copy(staged, total.parts.at[0], store_sem.at[0]).wait()

        def put(tile, right_value):
            outer_tile(left_t, right_value, staged)
            fetch(staged, total.parts.at[tile], store_sem.at[0]).wait()

        def rope_norm_back(grad, raw_value, gain, at):
            scaled = grad * cos[...] - half_turn(grad) * sin[...]
            inverse = inverse_rms(raw_value)
            unit = raw_value * inverse
            gains[:, at] += jnp.sum(scaled * unit, axis=0, keepdims=True)
            return norm_back(scaled, unit, inverse, gain[...])

        def attend_back(h):
            kv = lax.div(h, group)
            cut = pl.ds(pl.multiple_of(h * head, head), head)
            kv_cut = pl.ds(pl.multiple_of(kv * head, head), head)

            @pl.when(lax.rem(h, group) == 0)
            def _():
                d_key[...] = jnp.zeros_like(d_key)
                d_value[...] = jnp.zeros_like(d_value)

            load = fetch(q_raw.at[:, cut], raw, att_sem.at[0])
            size = min(256, token_count)
            for i in range(token_count // size):
                own, keys = slice(i * size, (i + 1) * size), (i + 1) * size
                q, dc = q_low[own, cut], d_context[own, cut]
                scores = nt_dot(k_low[0:keys, kv_cut], q) * scale
                expd = jnp.exp(scores - lse[pl.ds(h, 1), own])
                probs = jnp.where(allowed_pairs(keys, own, starts[:, own]), expd, 0.0)
                d_value[0:keys, :] += forward_dot(probs.astype(bf16), dc)
                d_probs = nt_dot(v_low[0:keys, kv_cut], dc)
                mean = jnp.sum(probs * d_probs, axis=0, keepdims=True)
                d_scores = (probs * (d_probs - mean)).astype(bf16)
                d_key[0:keys, :] += forward_dot(d_scores, q)
                d_query[own, :] = forward_dot(k_t[kv_cut, 0:keys], d_scores).T
            load.wait()
            heads[:, cut] = rope_norm_back(
                d_query[...] * scale, raw[...], query_gain, gain_at[2]
            ).astype(bf16)

            @pl.when(lax.rem(h, group) == group - 1)
            def _():
                fetch(k_raw.at[:, kv_cut], raw, att_sem.at[0]).wait()
                there = pl.ds(pl.multiple_of(query_width + kv * head, head), head)
                heads[:, there] = rope_norm_back(
                    d_key[...] * scale, raw[...], key_gain, gain_at[3]
                ).astype(bf16)
                there = pl.ds(pl.multiple_of(query_width + kv_width + kv * head, head), head)
                heads[:, there] = d_value[...].astype(bf16)

        small_at = summing.slots - 1
        steps = small_at + 5
        while slot_at(steps) < total.slots:
            steps += 1

        def shared_at(s):
            paired, pair, second, _ = total.item(s)
            return paired & total.here(pair, second) & (s < total.items)

        def settle_all(r):
            s = narrow_from + r - lax.div(r, pace)

            @pl.when((r >= 0) & (lax.rem(r, pace) != pace - 1))
            def _():
                total.settle(s, emitted)
                pl.when(shared_at(s))(shared_stored)

            settle(r)

        def body(r, carry):
            s = narrow_from + r - lax.div(r, pace)
            wide_too = lax.rem(r, pace) != pace - 1
            settle_all(r - 1)

            @pl.when(r == first_attend)
            def _():
                for t in range(out_tiles):
                    cut = slice(t * cols, (t + 1) * cols)
                    fetch(context.at[:, cut], right, att_sem.at[0]).wait()
                    put(late_from + t, right[...])

            @pl.when((r >= first_attend) & (r < first_heads))
            def _():
                def one(h, carry):
                    attend_back((r - first_attend) * heads_at_once + h)
                    return carry

                lax.fori_loop(0, heads_at_once, one, 0)

            @pl.when(r == first_heads)
            def _():
                fetch(normed_t, left_t, att_sem.at[0]).wait()

                def one(t, carry):
                    put(late_from + out_tiles + t, heads[:, columns(t)])
                    return carry

                lax.fori_loop(0, all_heads // cols, one, 0)

            @pl.when(r == 0)
            def _():
                other_copy.wait()
                rest_side.wait()
                rest_pass.start()

            @pl.when(r < chunks // 2)
            def _():
                for each in range(2):
                    take_other(r * 2 + each)

            @pl.when(wide_too & shared_at(s))
            def _():
                put_shared(total.item(s)[1] - 1, s)

            summing.at_stage(r, 2, preload)
            pl.when(wide_too)(lambda: total.fetches(s))
            summing.step(r, produce, work, lower, emit_rows)

            @pl.when(wide_too)
            def _():
                total.sums(s, emit_tile, emit_shared)

            pl.when(r >= small_at)(lambda: small.step(r - small_at))
            return carry

        lax.fori_loop(0, steps, body, 0)
        settle_all(steps - 1)
        total.finish()

    step = min(256, width)
    pl.run_scoped(
        pass_on,
        pltpu.VMEM((2, step, max(hidden_units, all_heads)), bf16),
        pltpu.VMEM((2, step, hidden_units), bf16),
        pltpu.VMEM((2, hidden_units, step), bf16),
        pltpu.VMEM((quarter, width), f32),
        pltpu.VMEM((quarter, width), bf16),
        pltpu.VMEM((quarter, width), f32),
        pltpu.VMEM(w_output.shape, bf16),
        pltpu.VMEM(normed_t.shape, bf16),
        pltpu.VMEM((line, 2, side_rows, cols), f32),
        pltpu.VMEM(q_in.shape, bf16),
        pltpu.VMEM(k_in.shape, bf16),
        pltpu.VMEM(v_in.shape, bf16),
        pltpu.VMEM((kv_width, token_count), bf16),
        pltpu.VMEM(q_in.shape, bf16),
        pltpu.VMEM((token_count, cols), bf16),
        pltpu.VMEM(lse_in.shape, f32),
        pltpu.VMEM(cosine.shape, f32),
        pltpu.VMEM(sine.shape, f32),
        pltpu.VMEM((token_count, head), f32),
        pltpu.VMEM((token_count, head), f32),
        pltpu.VMEM((token_count, head), f32),
        pltpu.VMEM((token_count, head), f32),
        pltpu.VMEM((token_count, all_heads), bf16),
        pltpu.VMEM((2 * rows, hidden_units), bf16),
        pltpu.VMEM((2, 2, quarter, width), f32),
        pltpu.VMEM((width, rows), bf16),
        pltpu.VMEM((2, 2, max(512, 2 * side_rows), token_count), bf16),
    )
    fetch(gains, gains_out, sem.at[0]).wait()


def call(kernel, collective_id, out_shape, in_specs, out_specs, scratch, arrays):
    return pl.pallas_call(
        kernel,
        out_shape=out_shape,
        in_specs=in_specs,
        out_specs=out_specs,
        scratch_shapes=scratch,
        compiler_params=pltpu.CompilerParams(
            collective_id=collective_id,
            has_side_effects=True,
            vmem_limit_bytes=62 * 1024 * 1024,
        ),
    )(*arrays)


def per_device(
    wide,
    tokens,
    seq_lengths,
    attn_gain,
    w_query,
    key_weight,
    value_weight,
    query_gain,
    key_norm_gain,
    w_output,
    mlp_gain,
    w_gate,
    w_up,
    w_down,
    cotangent,
):
    token_count, width = tokens.shape
    head_dim = query_gain.shape[0]
    query_width, kv_width = w_query.shape[1], key_weight.shape[1]
    hidden_units = w_gate.shape[1]
    all_heads = query_width + 2 * kv_width
    line = wide // 2
    side_rows = width // wide
    chunks = 8
    rows = token_count // chunks
    quarter = rows // 4
    block = min(256, token_count)
    dma = pltpu.SemaphoreType.DMA
    shape = jax.ShapeDtypeStruct

    segment_index, token_positions = layout(seq_lengths, token_count)
    token_positions = token_positions.reshape(-1)
    starts = (jnp.arange(token_count, dtype=jnp.int32) - token_positions)[None]
    cosine, sine = tables(token_positions, head_dim)
    cosine = cosine.reshape(token_count, head_dim)
    sign = jnp.where(jnp.arange(head_dim) < head_dim // 2, -1.0, 1.0).astype(f32)
    sine = sine.reshape(token_count, head_dim) * sign
    q_heads = query_width // head_dim

    kept = [
        shape((token_count, query_width), bf16),
        shape((token_count, kv_width), bf16),
        shape((token_count, kv_width), bf16),
        shape((token_count, query_width), f32),
        shape((token_count, kv_width), f32),
        shape((token_count, query_width), bf16),
        shape((q_heads, token_count), f32),
    ]
    vmem = [pltpu.VMEM(k.shape, k.dtype) for k in kept]
    outs = call(
        lambda *refs: attend_kernel(wide, chunks, *refs),
        1,
        [
            shape((chunks, 2, 2, quarter, width), bf16),
            shape((width, token_count), bf16),
            shape((width, token_count), bf16),
            shape((width, token_count), bf16),
            shape((chunks, quarter, width), f32),
            *kept,
            shape((chunks - 1, 2, quarter, width), f32),
            shape((2, quarter, width), f32),
        ],
        [in_vmem, any_space] + [in_vmem] * 11,
        [any_space] * 14,
        [
            *NarrowSum.sems(chunks),
            *NarrowSum.buffers(quarter, width),
            pltpu.VMEM((quarter, width), f32),
            *vmem[:3],
            pltpu.VMEM((kv_width, token_count), bf16),
            *vmem[3:],
            pltpu.VMEM((block, width), bf16),
            pltpu.VMEM((width, block), bf16),
            pltpu.VMEM((rows, width), bf16),
            pltpu.VMEM((width, rows), bf16),
            pltpu.VMEM((width, rows), bf16),
            dma((6,)),
            dma((7,)),
            dma((chunks,)),
            dma((chunks,)),
        ],
        (
            tokens, cotangent, w_query, key_weight, value_weight, w_output, attn_gain[None],
            mlp_gain[None], query_gain[None], key_norm_gain[None], cosine, sine, starts,
        ),
    )
    (mlp_in, mlp_in_t, cot_t, normed_t, hidden, q_low, k_low, v_low, q_raw, k_raw, context,
     lse, other, rest) = outs[:14]

    cols = min(256 if line <= 4 else 128, hidden_units // 6)
    counts = (hidden_units // cols, hidden_units // cols, (query_width + all_heads) // cols)
    gain_width = 2 * width + 2 * head_dim
    outs = call(
        lambda *refs: main_kernel(wide, chunks, counts, *refs),
        2,
        [
            shape((chunks, 2, 2, quarter, width), bf16),
            shape((chunks, 2, 2, quarter, width), bf16),
            shape((side_rows, query_width), f32),
            shape((side_rows, kv_width), f32),
            shape((side_rows, kv_width), f32),
            shape((query_width, side_rows), f32),
            shape((side_rows, hidden_units), f32),
            shape((side_rows, hidden_units), f32),
            shape((hidden_units, side_rows), f32),
            shape((1, gain_width), f32),
            shape((chunks, quarter, width), f32),
            shape((token_count, hidden_units), bf16),
            shape((chunks - 1, 2, quarter, width), f32),
            shape((2, quarter, width), f32),
            shape((2, quarter, width), f32),
            shape((width, token_count), bf16),
            *WideSum.lands(counts, line, side_rows, cols),
        ],
        [any_space] * 25 + [in_vmem] * 5,
        [any_space] * 23,
        [
            *WideSum.sems(counts),
            *NarrowSum.sems(3 * chunks),
            *WideSum.buffers(line, side_rows, cols),
            *NarrowSum.buffers(quarter, width),
            pltpu.VMEM((2, token_count, hidden_units), bf16),
            pltpu.VMEM((1, gain_width), f32),
            pltpu.VMEM((2 + line, 1, gain_width), f32),
            pltpu.VMEM((2, cols, side_rows), f32),
            dma((2 + line,)),
            dma((2 + line,)),
            dma((4,)),
            dma((2, 3)),
            dma((2,)),
            dma((3,)),
            dma((1,)),
            dma((4,)),
            dma((10,)),
        ],
        (
            mlp_in.reshape(token_count, width), mlp_in_t, cotangent, cot_t, normed_t, hidden,
            other, rest, q_low, k_low, v_low, q_raw, k_raw, context, lse, tokens, w_gate, w_up, w_down,
            w_output, w_query, key_weight, value_weight, cosine, sine, starts, attn_gain[None],
            mlp_gain[None], query_gain[None], key_norm_gain[None],
        ),
    )
    (output, grad_tokens, shard_query, shard_key, shard_value, shard_output, shard_gate,
     shard_up, shard_down, gains) = outs[:10]
    gains = gains[0]
    at = lax.axis_index("wide")
    head_part = head_dim // wide

    def own(start, size):
        return lax.dynamic_slice_in_dim(gains, start + at * size, size)

    return (
        output.reshape(token_count, width),
        grad_tokens.reshape(token_count, width),
        own(0, side_rows),
        shard_query,
        shard_key,
        shard_value,
        own(2 * width, head_part),
        own(2 * width + head_dim, head_part),
        shard_output,
        own(width, side_rows),
        shard_gate,
        shard_up,
        shard_down,
    )


def solution(mesh):
    def run(*arrays):
        return per_device(mesh.shape["wide"], *arrays)

    return jax.shard_map(
        run,
        mesh=mesh,
        in_specs=(
            P("wide", None),
            P("wide", None),
            P(),
            P(None, "narrow"),
            P(None, "narrow"),
            P(None, "narrow"),
            P(),
            P(),
            P("narrow", None),
            P(),
            P(None, "narrow"),
            P(None, "narrow"),
            P("narrow", None),
            P("wide", None),
        ),
        out_specs=(
            P("wide", None),
            P("wide", None),
            P("wide"),
            P("wide", "narrow"),
            P("wide", "narrow"),
            P("wide", "narrow"),
            P("wide"),
            P("wide"),
            P("narrow", "wide"),
            P("wide"),
            P("wide", "narrow"),
            P("wide", "narrow"),
            P("narrow", "wide"),
        ),
        check_vma=False,
    )
```

```python
import functools

import jax
import jax.numpy as jnp
from jax import lax
from jax.experimental import pallas as pl
from jax.experimental.pallas import tpu as pltpu
from jax.sharding import PartitionSpec as P

norm_eps = 1e-06
rope_base = 1000000.0
masked_score = -1e30
bf16 = jnp.bfloat16
f32 = jnp.float32


def inverse_rms(values):
    return lax.rsqrt(jnp.mean(values * values, axis=-1, keepdims=True) + norm_eps)


def layout(seq_lengths, row_len):
    seq_ends = jnp.cumsum(seq_lengths, axis=-1)
    starts = seq_ends - seq_lengths
    places = jnp.arange(row_len, dtype=jnp.int32)
    segment_index = jnp.sum(
        (places[None, :, None] >= seq_ends[:, None, :]).astype(jnp.int32), axis=-1
    )
    belongs = (
        segment_index[:, :, None]
        == jnp.arange(seq_lengths.shape[-1], dtype=jnp.int32)[None, None, :]
    )
    seq_start = jnp.sum(jnp.where(belongs, starts[:, None, :], 0), axis=-1)
    return (segment_index, places[None, :] - seq_start)


def tables(token_positions, head_dim):
    half_width = head_dim // 2
    frequency = rope_base ** (-2.0 * jnp.arange(half_width, dtype=f32) / head_dim)
    angles = token_positions.astype(f32)[:, None] * frequency[None, :]
    angles = jnp.concatenate([angles, angles], axis=-1)
    return (jnp.cos(angles)[:, None, :], jnp.sin(angles)[:, None, :])


def forward_dot(left_side, right_side):
    return jnp.dot(left_side, right_side, preferred_element_type=f32)


MESH = pl.DeviceIdType.MESH
any_space = pl.BlockSpec(memory_space=pl.ANY)
in_vmem = pl.BlockSpec(memory_space=pltpu.VMEM)


def nt_dot(left_side, right_side):
    return lax.dot_general(
        left_side, right_side, (((1,), (1,)), ((), ())), preferred_element_type=f32
    )


def fetch(source, target, sem):
    copy = pltpu.make_async_copy(source, target, sem)
    copy.start()
    return copy


class Spot:
    def __init__(self, wide):
        self.line = wide // 2
        self.w = lax.axis_index("wide")
        self.n = lax.axis_index("narrow")
        self.spot = lax.div(self.w, 2)
        self.side = lax.rem(self.w, 2)
        self.core = lax.rem(self.n, 2)
        self.chip = lax.div(self.n, 2)
        self.to_core = {"narrow": self.n + 1 - 2 * self.core}
        self.to_chip = {"narrow": self.n + 2 - 4 * self.chip}
        self.to_side = {"wide": self.w + 1 - 2 * self.side}
        self.to_up = {"wide": self.w + 2}
        self.to_down = {"wide": self.w - 2}

    def along(self, distance):
        there = lax.rem(self.spot + distance, self.line)
        return {"wide": there * 2 + self.side}

    def greet(self, line_too):
        barrier = pltpu.get_barrier_semaphore()

        def tell(who):
            pl.semaphore_signal(barrier, inc=1, device_id=who, device_id_type=MESH)

        tell(self.to_core)
        tell(self.to_chip)
        tell(self.to_side)
        if line_too:
            for distance in range(1, self.line):
                tell(self.along(distance))
        pl.semaphore_wait(barrier, 2 + self.line if line_too else 3)


def remote(source, target, send, recv, who):
    return pltpu.make_async_remote_copy(
        src_ref=source, dst_ref=target, send_sem=send, recv_sem=recv,
        device_id=who, device_id_type=MESH,
    )


class WideSum:
    ahead = 3
    join_after = 5
    held_back = 0

    @staticmethod
    def lag(line):
        return 2 if line <= 4 else 1

    @staticmethod
    def numbers(counts):
        early, shared, late = counts
        firsts, pairs = early - 1 + late, 1 + shared
        return early + shared + late, firsts, pairs, firsts + 2 * pairs

    @classmethod
    def lands(cls, counts, line, rows, cols):
        tiles, firsts, pairs, items = cls.numbers(counts)
        return [
            jax.ShapeDtypeStruct((tiles, line, 2, rows, cols), f32),
            jax.ShapeDtypeStruct((firsts, line, rows, cols), f32),
            jax.ShapeDtypeStruct((items, line - 1, rows, cols), f32),
            jax.ShapeDtypeStruct((items, line - 1, rows, cols), f32),
            jax.ShapeDtypeStruct((pairs, rows, cols), f32),
            jax.ShapeDtypeStruct((counts[1], line, rows, cols), f32),
            jax.ShapeDtypeStruct((counts[1], line, rows, cols), f32),
        ]

    @classmethod
    def sems(cls, counts, line):
        dma, hops = pltpu.SemaphoreType.DMA, line - 1
        tiles, firsts, pairs, items = cls.numbers(counts)
        return [
            dma((firsts,)), dma((firsts,)), dma((2, hops)), dma((items, hops)), dma((2, hops)),
            dma((items, hops)),
            dma((pairs,)), dma((pairs,)), dma((counts[1],)), dma((counts[1],)), dma((7,)),
        ]

    @classmethod
    def buffers(cls, line, rows, cols):
        tile = (line, rows, cols)
        return [
            pltpu.VMEM(tile, f32),
            pltpu.VMEM((cls.lag(line) * (line - 1) + 1,) + tile, f32),
            pltpu.VMEM((2, line - 1, rows, cols), f32),
            pltpu.VMEM((2, line - 1, rows, cols), f32),
            pltpu.VMEM((line - 1, rows, cols), f32),
            pltpu.VMEM((line - 1, rows, cols), f32),
            pltpu.VMEM((4, rows, cols), f32),
            pltpu.VMEM((3, rows, cols), f32),
            pltpu.VMEM((3, rows, cols), f32),
        ]

    def __init__(self, me, counts, ready, lands, sems, buffers):
        self.me, self.line = me, me.line
        self.early, self.shared, self.late = counts
        (self.parts, self.y_land, self.up_land, self.down_land, self.last_land, self.give,
         self.give_land) = lands
        (self.y_send, self.y_recv, self.up_send, self.up_recv, self.down_send, self.down_recv,
         self.last_send, self.last_recv, self.give_send, self.give_recv, self.local) = sems
        (self.got, self.ring, self.up_buf, self.down_buf, self.up_load, self.down_load, self.last,
         self.leave, self.hold) = buffers
        self.tiles, self.firsts, self.pairs, self.items = self.numbers(counts)
        self.shared_from = self.early + 1
        before = self.shared - self.held_back
        self.late_from = self.shared_from + 2 * before
        self.rest_from = self.late_from + self.late
        used = [(2 + u, False, u) for u in range(self.early - 1)]
        used += [(self.shared_from + 2 * t, True, t) for t in range(before)]
        used += [(self.late_from + k, False, self.early - 1 + k) for k in range(self.late)]
        used += [(self.rest_from + 2 * k, True, before + k) for k in range(self.held_back)]
        self.sending = []
        for m in range(self.ahead, len(used)):
            slot, shared, number = used[m]
            late = number - (self.early - 1)
            made = 0 if shared or late < 0 else ready(late)
            at = max(used[m - self.ahead][0], made)
            assert at < slot
            self.sending.append((at, shared, number))

    def item(self, s):
        rest = s >= self.rest_from
        among = s - self.shared_from - jnp.where(rest, self.late, 0)
        start = s < 2
        paired = start | rest | ((among >= 0) & (s < self.late_from))
        pair = jnp.where(start, 0, 1 + lax.div(among, 2))
        half = jnp.where(start, s, lax.rem(among, 2))
        first = jnp.where(among < 0, s - 2, s - self.late_from + self.early - 1)
        return paired, pair, half, first

    def pair_tile(self, pair):
        return jnp.where(pair == 0, 0, self.early - 1 + pair)

    def first_tile(self, first):
        made = self.early - 1
        return jnp.where(first < made, first + 1, first + 1 + self.shared)

    def begin(self, tile):
        @pl.when((tile > 0) & (tile <= self.ahead))
        def _():
            self.y_copy(tile - 1).start()

    def y_copy(self, first):
        return remote(
            self.parts.at[self.first_tile(first), :, 1 - self.me.side], self.y_land.at[first],
            self.y_send.at[first], self.y_recv.at[first], self.me.to_side,
        )

    def give_copy(self, shared):
        return remote(
            self.give.at[shared], self.give_land.at[shared],
            self.give_send.at[shared], self.give_recv.at[shared], self.me.to_side,
        )

    def last_copy(self, pair):
        return remote(
            self.leave.at[lax.rem(pair, 3)], self.last_land.at[pair],
            self.last_send.at[pair], self.last_recv.at[pair], self.me.to_side,
        )

    def up_copy(self, item, at):
        slot = lax.rem(item, 2)
        return remote(
            self.up_buf.at[slot, at], self.up_land.at[item, at],
            self.up_send.at[slot, at], self.up_recv.at[item, at], self.me.to_up,
        )

    def down_copy(self, item, at):
        slot = lax.rem(item, 2)
        return remote(
            self.down_buf.at[slot, at], self.down_land.at[item, at],
            self.down_send.at[slot, at], self.down_recv.at[item, at], self.me.to_down,
        )

    def await_up(self, item, at):
        land = self.up_land.at[item, at]
        remote(
            land, land, self.up_send.at[0, 0], self.up_recv.at[item, at], self.me.to_up
        ).wait_recv()

    def await_down(self, item, at):
        land = self.down_land.at[item, at]
        remote(
            land, land, self.down_send.at[0, 0], self.down_recv.at[item, at], self.me.to_down
        ).wait_recv()

    @property
    def slots(self):
        return self.items + self.lag(self.line) * (self.line - 1)

    def stages(self, s, first, up, down, last):
        me, line, items = self.me, self.line, self.items
        lag = self.lag(line)
        pl.when(s < items)(lambda: first(*self.item(s)))

        def at(item, found, body, *more):
            pl.when(found & (item >= 0) & (item < items))(lambda: body(item, *more))

        for k in range(line - 1):
            at(s - lag * k, me.spot == k, up, k, line - 1 - k)
        for k in range(1, line):
            at(s - lag * (line - 1 - k), me.spot == k, down, k, k)
        at(s - lag * (line - 1), s >= 0, last)

    @staticmethod
    def here(pair, half):
        return (pair > 0) & (half == 0)

    def joined(self, item):
        before = item - self.join_after
        paired, pair, half, _ = self.item(before)
        now_paired, now_pair, now_half, _ = self.item(item)
        soon = self.pairs - self.held_back
        late = now_paired & (now_half == 1) & (now_pair >= soon)
        joins = late | ((before >= 0) & paired & (half == 0) & (pair < soon))
        return joins, jnp.where(late, now_pair, pair)

    def fetches(self, s):
        me, line = self.me, self.line
        depth = self.ring.shape[0]
        for at, shared, number in self.sending:
            @pl.when(s == at)
            def _(shared=shared, number=number):
                (self.give_copy if shared else self.y_copy)(number).start()

        def first(paired, pair, half, number):
            held = self.ring.at[lax.rem(s, depth)]

            @pl.when(paired & jnp.logical_not(self.here(pair, half)))
            def _():
                side = jnp.where(half == 0, 1 - me.side, me.side)
                fetch(self.parts.at[self.pair_tile(pair), :, side], held, self.local.at[0])

            @pl.when(jnp.logical_not(paired))
            def _():
                fetch(self.parts.at[self.first_tile(number), :, me.side], held, self.local.at[0])
                self.y_copy(number).wait()
                fetch(self.y_land.at[number], self.got, self.local.at[1])

        def up(item, k, count):
            if k == 0:
                return

            @pl.when(item < self.items - 1)
            def _():
                for at in range(count + 1):
                    self.await_up(item, at)
                fetch(
                    self.up_land.at[item, 1 : count + 1], self.up_load.at[0:count],
                    self.local.at[2],
                )

        def down(item, k, count):
            if k == line - 1:
                return

            @pl.when(item < self.items - 1)
            def _():
                for at in range(count + 1):
                    self.await_down(item, at)
                fetch(
                    self.down_land.at[item, 0:count], self.down_load.at[0:count],
                    self.local.at[3],
                )

        def last(item):
            final = item == self.items - 1

            @pl.when((me.spot == line - 1) | (final & (me.spot > 0)))
            def _():
                self.await_up(item, 0)

            @pl.when((me.spot == 0) | (final & (me.spot < line - 1)))
            def _():
                self.await_down(item, me.spot)

            @pl.when(me.spot > 0)
            def _():
                fetch(self.up_land.at[item, 0], self.last.at[0], self.local.at[4])

            @pl.when(me.spot < line - 1)
            def _():
                fetch(self.down_land.at[item, me.spot], self.last.at[1], self.local.at[5])

            joins, pair = self.joined(item)

            @pl.when(joins)
            def _():
                self.last_copy(pair).wait()
                fetch(self.last_land.at[pair], self.last.at[3], self.local.at[6])

        self.stages(s, first, up, down, last)

    def loaded(self, target, at):
        pltpu.make_async_copy(target, target, self.local.at[at]).wait()

    def sums(self, s, emit, emit_shared):
        me, line = self.me, self.line
        depth = self.ring.shape[0]

        def first(paired, pair, half, number):
            held = lax.rem(s, depth)

            @pl.when(jnp.logical_not(paired & self.here(pair, half)))
            def _():
                self.loaded(self.ring.at[held], 0)

            @pl.when(jnp.logical_not(paired))
            def _():
                self.loaded(self.got, 1)
                self.ring[held] = self.ring[held] + self.got[...]

        def up(item, k, count):
            slot, held = lax.rem(item, 2), lax.rem(item, depth)
            order = range(count - 1, -1, -1)

            @pl.when(item >= 2)
            def _():
                for at in order:
                    self.up_copy(item, at).wait_send()

            if k == 0:
                self.up_buf[slot, 0:count] = self.ring[held, 1:line]
                for at in order:
                    self.up_copy(item, at).start()
                return

            @pl.when(item < self.items - 1)
            def _():
                self.loaded(self.up_load.at[0:count], 2)
                self.up_buf[slot, 0:count] = self.ring[held, k + 1 : line] + self.up_load[0:count]
                for at in order:
                    self.up_copy(item, at).start()

            @pl.when(item == self.items - 1)
            def _():
                for at in order:
                    self.await_up(item, at + 1)
                    fetch(
                        self.up_land.at[item, at + 1], self.up_load.at[at], self.local.at[2]
                    ).wait()
                    self.up_buf[slot, at] = self.ring[held, k + 1 + at] + self.up_load[at]
                    self.up_copy(item, at).start()

        def down(item, k, count):
            slot, held = lax.rem(item, 2), lax.rem(item, depth)
            order = range(count)

            @pl.when(item >= 2)
            def _():
                for at in order:
                    self.down_copy(item, at).wait_send()

            if k == line - 1:
                self.down_buf[slot, 0:count] = self.ring[held, 0:count]
                for at in order:
                    self.down_copy(item, at).start()
                return

            @pl.when(item < self.items - 1)
            def _():
                self.loaded(self.down_load.at[0:count], 3)
                self.down_buf[slot, 0:count] = self.ring[held, 0:count] + self.down_load[0:count]
                for at in order:
                    self.down_copy(item, at).start()

            @pl.when(item == self.items - 1)
            def _():
                for at in order:
                    self.await_down(item, at)
                    fetch(
                        self.down_land.at[item, at], self.down_load.at[at], self.local.at[3]
                    ).wait()
                    self.down_buf[slot, at] = self.ring[held, at] + self.down_load[at]
                    self.down_copy(item, at).start()

        def last(item):
            paired, pair, half, number = self.item(item)
            self.last[2] = self.ring[lax.rem(item, depth), me.spot]

            @pl.when(me.spot > 0)
            def _():
                self.loaded(self.last.at[0], 4)
                self.last[2] = self.last[2] + self.last[0]

            @pl.when(me.spot < line - 1)
            def _():
                self.loaded(self.last.at[1], 5)
                self.last[2] = self.last[2] + self.last[1]

            @pl.when(paired & (half == 0))
            def _():
                self.leave[lax.rem(pair, 3)] = self.last[2]
                self.last_copy(pair).start()

            @pl.when(paired & (half == 1))
            def _():
                self.hold[lax.rem(pair, 3)] = self.last[2]

            @pl.when(jnp.logical_not(paired))
            def _():
                emit(self.first_tile(number), self.last.at[2], 0)

            joins, pair = self.joined(item)

            @pl.when(joins)
            def _():
                self.loaded(self.last.at[3], 6)
                third = lax.rem(pair, 3)

                @pl.when(pair == 0)
                def _():
                    self.hold[third] = self.hold[third] + self.last[3]
                    emit(0, self.hold.at[third], 1)

                @pl.when(pair > 0)
                def _():
                    emit_shared(pair - 1, me.side, self.hold.at[third], 1)
                    emit_shared(pair - 1, 1 - me.side, self.last.at[3], 2)

        self.stages(s, first, up, down, last)

    def settle(self, s, emitted):
        def nothing(*_):
            pass

        def last(item):
            paired, _, _, _ = self.item(item)
            pl.when(jnp.logical_not(paired))(lambda: emitted(0))
            joins, pair = self.joined(item)
            pl.when(joins)(lambda: emitted(1))
            pl.when(joins & (pair > 0))(lambda: emitted(2))

        self.stages(s, nothing, nothing, nothing, last)

    def step(self, s, emit, emit_shared, emitted):
        self.fetches(s)
        self.sums(s, emit, emit_shared)
        self.settle(s, emitted)

    def finish(self):
        me, line = self.me, self.line
        for k in range(line - 1):
            @pl.when(me.spot == k)
            def _(k=k):
                for item in range(self.items - 2, self.items):
                    for at in range(line - 1 - k):
                        self.up_copy(item, at).wait_send()

        for k in range(1, line):
            @pl.when(me.spot == k)
            def _(k=k):
                for item in range(self.items - 2, self.items):
                    for at in range(k):
                        self.down_copy(item, at).wait_send()


class NarrowSum:
    @staticmethod
    def sems(chunks):
        dma = pltpu.SemaphoreType.DMA
        return [dma((chunks,)) for _ in range(8)]

    @staticmethod
    def buffers(quarter, width):
        return [
            pltpu.VMEM((2, 2, 2, quarter, width), f32),
            pltpu.VMEM((2, 2, quarter, width), f32),
            pltpu.VMEM((2, 2, quarter, width), f32),
            pltpu.VMEM((2, quarter, width), f32),
            pltpu.VMEM((3, 2, quarter, width), f32),
            pltpu.VMEM((2, 2, quarter, width), f32),
            pltpu.VMEM((2, 2, quarter, width), bf16),
        ]

    def __init__(self, me, sems, buffers):
        self.me = me
        (self.s0, self.r0, self.s1, self.r1, self.s2, self.r2, self.s3, self.r3) = sems
        (self.part, self.core_land, self.half, self.chip_land, self.pair, self.last_land,
         self.low) = buffers
        self.chunks = self.s0.shape[0]

    def copies(self, stage, c):
        me, slot, third = self.me, lax.rem(c, 2), lax.rem(c, 3)
        if stage == 0:
            return remote(self.part.at[slot, 1 - me.core], self.core_land.at[slot],
                          self.s0.at[c], self.r0.at[c], me.to_core)
        if stage == 1:
            return remote(self.half.at[slot, 1 - me.chip], self.chip_land.at[slot],
                          self.s1.at[c], self.r1.at[c], me.to_chip)
        if stage == 2:
            return remote(self.pair.at[third, me.chip], self.pair.at[third, me.chip],
                          self.s2.at[c], self.r2.at[c], me.to_chip)
        return remote(self.pair.at[third], self.last_land.at[slot],
                      self.s3.at[c], self.r3.at[c], me.to_core)

    @property
    def slots(self):
        return self.chunks + 4

    def at_stage(self, s, number, body):
        c = s - number
        pl.when((c >= 0) & (c < self.chunks))(lambda: body(c))

    def step(self, s, produce, work, lower, emit, beside=None):
        me = self.me

        def stage(number, body):
            def run(c):
                if number > 0:
                    self.copies(number - 1, c).wait()
                body(c, lax.rem(c, 2), lax.rem(c, 3))
                if number < 4:
                    self.copies(number, c).start()

            self.at_stage(s, number, run)

        def four(c, slot, third):
            self.low[me.core] = lower(self.pair[third])
            self.low[1 - me.core] = lower(self.last_land[slot])
            emit(c, self.low)

        def three(c, slot, third):
            if beside is not None:
                beside(c, self.pair.at[third])

        def two(c, slot, third):
            self.pair[third, me.chip] = work(c, self.half[slot, me.chip] + self.chip_land[slot])

        def one(c, slot, third):
            self.half[slot] = self.part[slot, me.core] + self.core_land[slot]

        def zero(c, slot, third):
            pl.when(slot == 0)(lambda: produce(c, self.part))

        stage(4, four)
        stage(3, three)
        stage(2, two)
        stage(1, one)
        stage(0, zero)


def take(refs, count):
    return refs[:count], refs[count:]


def store_part(part, value, columns):
    part[:, :, :, :, columns] = value.reshape(2, 2, 2, value.shape[0] // 8, value.shape[1])


def norm_back(pulled, unit, scale, gain):
    scaled = pulled * gain
    return scale * (scaled - unit * jnp.mean(scaled * unit, axis=-1, keepdims=True))


def half_turn(values):
    return pltpu.roll(values, values.shape[-1] // 2, values.ndim - 1)


def allowed_pairs(keys, rows, starts):
    count = rows.stop - rows.start
    key = lax.broadcasted_iota(jnp.int32, (keys, count), 0)
    query = lax.broadcasted_iota(jnp.int32, (keys, count), 1) + rows.start
    return (key <= query) & (key >= starts)


def attend_kernel(wide, chunks, *refs):
    (tokens, cot, w_query, w_key, w_value, w_output, attn_gain, mlp_gain, query_gain, key_gain,
     cosine, sine, starts), refs = take(refs, 13)
    (mlp_in, mlp_in_t, cot_t, normed_t, hidden_out, q_out, k_out, v_out, q_raw_out, k_raw_out,
     context_out, lse_out, other_out, rest_out), refs = take(refs, 14)
    sems, refs = take(refs, 8)
    buffers, refs = take(refs, 7)
    (hidden_buf, q_low, k_low, v_low, v_t, q_raw, k_raw, context, lse, normed, normed_turn,
     cot_load, cot_turn, low_turn, sem, out_sem, give_sem, take_sem) = refs
    me = Spot(wide)
    me.greet(False)
    summing = NarrowSum(me, sems, buffers)
    token_count, width = tokens.shape
    rows = token_count // chunks
    quarter = rows // 4
    block = normed.shape[0]
    per_block = block // rows
    head = query_gain.shape[1]
    q_heads = w_query.shape[1] // head
    group = q_heads // (w_key.shape[1] // head)
    scale = head ** (-0.5)
    step = min(512, width)
    kept = (
        (q_low, q_out), (k_low, k_out), (v_low, v_out), (q_raw, q_raw_out), (k_raw, k_raw_out),
        (context, context_out), (lse, lse_out),
    )

    def attend(i):
        own = slice(i * block, (i + 1) * block)
        keys = (i + 1) * block
        x = tokens[own, :].astype(f32)
        normed[...] = (x * inverse_rms(x) * attn_gain[...]).astype(bf16)
        cos, sin = cosine[own, :], sine[own, :]

        def heads_of(raw, low, gain):
            for h in range(raw.shape[1] // head):
                cut = slice(h * head, (h + 1) * head)
                u = raw[own, cut]
                y = u * inverse_rms(u) * gain[...]
                low[own, cut] = (y * cos + half_turn(y) * sin).astype(bf16)

        q_raw[own, :] = forward_dot(normed[...], w_query[...])
        k_raw[own, :] = forward_dot(normed[...], w_key[...])
        value = forward_dot(normed[...], w_value[...])
        v_low[own, :] = value.astype(bf16)
        v_t[:, own] = value.T.astype(bf16)
        heads_of(q_raw, q_low, query_gain)
        heads_of(k_raw, k_low, key_gain)
        allowed = allowed_pairs(keys, own, starts[:, own])
        for h in range(q_heads):
            cut, kv = slice(h * head, (h + 1) * head), h // group
            kv_cut = slice(kv * head, (kv + 1) * head)
            scores = nt_dot(k_low[0:keys, kv_cut], q_low[own, cut]) * scale
            scores = jnp.where(allowed, scores, masked_score)
            top = jnp.max(scores, axis=0, keepdims=True)
            expd = jnp.exp(scores - top)
            total = jnp.sum(expd, axis=0, keepdims=True)
            probs = (expd / total).astype(bf16)
            lse[h : h + 1, own] = top + jnp.log(total)
            mixed = forward_dot(v_t[kv_cut, 0:keys], probs)
            context[own, cut] = mixed.T.astype(bf16)

    def produce(c, part):
        for i in range(token_count // block):
            pl.when(c == i * per_block)(functools.partial(attend, i))
        left = context[pl.ds(pl.multiple_of(c * rows, 2 * rows), 2 * rows), :]
        for at in range(0, width, step):
            store_part(part, forward_dot(left, w_output[:, at : at + step]), slice(at, at + step))

    def work(c, total):
        at = pl.multiple_of(c * rows + me.core * 2 * quarter + me.chip * quarter, quarter)
        hidden = tokens[pl.ds(at, quarter), :].astype(f32) + total
        hidden_buf[...] = hidden
        fetch(hidden_buf, hidden_out.at[c], sem.at[2])
        return hidden * inverse_rms(hidden)

    def lower(value):
        return (value * mlp_gain[...]).astype(bf16)

    def emit(c, low):
        @pl.when(c < chunks - 1)
        def _():
            beside(c, summing.pair.at[lax.rem(c, 3)]).wait_send()

        @pl.when(c == chunks - 1)
        def _():
            pltpu.make_async_copy(summing.pair.at[lax.rem(c, 3)], rest_out, sem.at[5]).wait()

        fetch(low, mlp_in.at[c], sem.at[3])
        low_turn[...] = low[...].reshape(rows, width).T
        at = pl.ds(pl.multiple_of(c * rows, rows), rows)
        fetch(low_turn, mlp_in_t.at[:, at], sem.at[4])

    def settle(s):
        def two(c):
            pltpu.make_async_copy(hidden_buf, hidden_out.at[c], sem.at[2]).wait()

        def four(c):
            pltpu.make_async_copy(summing.low, mlp_in.at[c], sem.at[3]).wait()
            at = pl.ds(pl.multiple_of(c * rows, rows), rows)
            pltpu.make_async_copy(low_turn, mlp_in_t.at[:, at], sem.at[4]).wait()

        summing.at_stage(s, 2, two)
        summing.at_stage(s, 4, four)

    def beside(c, half):
        return remote(half, other_out.at[c], give_sem.at[c], take_sem.at[c], me.to_side)

    def begin_beside(c, half):
        @pl.when(c < chunks - 1)
        def _():
            beside(c, half).start()

        @pl.when(c == chunks - 1)
        def _():
            fetch(half, rest_out, sem.at[5])

    def turn_rows(s):
        at = pl.ds(pl.multiple_of(s * rows, rows), rows)
        fetch(cot.at[at, :], cot_load, sem.at[0]).wait()
        cot_turn[...] = cot_load[...].T
        a = fetch(cot_turn, cot_t.at[:, at], sem.at[1])

        @pl.when(lax.rem(s, per_block) == 0)
        def _():
            normed_turn[...] = normed[...].T
            wide_at = pl.ds(pl.multiple_of(s * rows, block), block)
            fetch(normed_turn, normed_t.at[:, wide_at], sem.at[0]).wait()

        a.wait()

    def body(s, carry):
        summing.step(s, produce, work, lower, emit, begin_beside)
        pl.when(s < chunks)(lambda: turn_rows(s))

        @pl.when(s == chunks - 1)
        def _():
            for at, (a, b) in enumerate(kept):
                fetch(a, b, out_sem.at[at])

        settle(s)
        return carry

    lax.fori_loop(0, summing.slots, body, 0)
    for at, (a, b) in enumerate(kept):
        pltpu.make_async_copy(a, b, out_sem.at[at]).wait()
    for c in range(chunks - 1):
        beside(c, summing.pair.at[c % 3]).wait_recv()


def outer_tile(left_t, right, stage):
    line, _, rows, _ = stage.shape
    group = max(1, 512 // (2 * rows))
    while line % group:
        group -= 1

    def body(m, carry):
        at = pl.multiple_of(m * group * 2 * rows, group * 2 * rows)
        value = forward_dot(left_t[pl.ds(at, group * 2 * rows), :], right)
        stage[pl.ds(m * group, group)] = value.reshape((group, 2, rows, value.shape[1]))
        return carry

    lax.fori_loop(0, line // group, body, 0)


class SmallSum:
    def __init__(self, me, value, lands, sends, recvs):
        self.me, self.value, self.lands, self.sends, self.recvs = me, value, lands, sends, recvs

    def copy(self, k):
        me = self.me
        who = (me.to_core, me.to_chip, me.to_side)[k] if k < 3 else me.along(k - 2)
        return remote(self.value, self.lands.at[k], self.sends.at[k], self.recvs.at[k], who)

    def step(self, at):
        last = 2 + self.me.line
        stages = [[0], [1], [2], list(range(3, last)), []]
        for number, copies in enumerate(stages):
            @pl.when(at == number)
            def _(number=number, copies=copies):
                if number > 0:
                    for k in stages[number - 1]:
                        self.copy(k).wait()
                    for k in stages[number - 1]:
                        self.value[...] = self.value[...] + self.lands[k]
                for k in copies:
                    self.copy(k).start()


def main_kernel(wide, chunks, counts, *refs):
    (mlp_in, mlp_in_t, cot, cot_t, normed_t, hidden, other, rest, q_in, k_in, v_in, q_raw, k_raw,
     context, lse_in, tokens, w_gate, w_up, w_down, w_output, w_query, w_key, w_value, cosine, sine,
     starts, attn_gain, mlp_gain, query_gain, key_gain), refs = take(refs, 30)
    (output, grad_tokens, grad_query, grad_key, grad_value, grad_output, grad_gate, grad_up,
     grad_down, gains_out, grad_hidden, inner_out, other_land, rest_land, rest_core,
     other_t), refs = take(refs, 16)
    wide_lands, refs = take(refs, 7)
    wide_sems, refs = take(refs, 11)
    sems, refs = take(refs, 8)
    wide_buffers, refs = take(refs, 9)
    buffers, refs = take(refs, 7)
    (acts, gains, gain_lands, turned, gain_send, gain_recv, sem, w_sem, store_sem, emit_sem,
     att_sem, give_sem, other_sem) = refs
    me = Spot(wide)
    me.greet(True)
    token_count, width = mlp_in.shape
    hidden_units = w_gate.shape[1]
    tiles, line, _, side_rows, cols = wide_lands[0].shape
    blocks = hidden_units // cols
    early_tiles, shared_tiles, late_tiles = counts
    late_from = early_tiles + shared_tiles
    query_width, kv_width = w_query.shape[1], w_key.shape[1]
    all_heads = query_width + 2 * kv_width
    head = query_gain.shape[1]
    q_heads = query_width // head
    group = q_heads // (kv_width // head)
    scale = head ** (-0.5)
    out_tiles = query_width // cols
    narrow_from, pace = 2, 6
    first_attend = chunks + 4
    heads_at_once = 2
    first_heads = first_attend + q_heads // heads_at_once

    def slot_at(r):
        return narrow_from + r - r // pace

    total = WideSum(
        me, counts, lambda late: slot_at(first_attend if late < out_tiles else first_heads),
        wide_lands, wide_sems, wide_buffers,
    )
    other_copy = remote(other, other_land, other_sem.at[0], other_sem.at[1], me.to_core)
    other_copy.start()
    rest_side = remote(rest, rest_land, other_sem.at[6], other_sem.at[7], me.to_side)
    rest_side.start()
    rest_pass = remote(rest_land, rest_core, other_sem.at[8], other_sem.at[9], me.to_core)
    half = token_count // 2
    rows = token_count // chunks
    quarter = rows // 4

    def block_of(t):
        return lax.rem(t, 2) * (blocks // 2) + lax.div(t, 2)

    def half_of(b):
        return lax.div(b, blocks // 2)

    def columns(at):
        return pl.ds(pl.multiple_of(at * cols, cols), cols)

    def emit_tile(tile, value, number):
        def part(first, count, target, turn, place):
            @pl.when((tile >= first) & (tile < first + count))
            def _():
                cut = columns(place(tile - first))
                if turn:
                    turned[number] = value[...].T
                    fetch(turned.at[number], target.at[cut, :], emit_sem.at[number])
                else:
                    fetch(value, target.at[:, cut], emit_sem.at[number])

        def same(at):
            return at

        part(0, early_tiles, grad_down, True, block_of)
        at = late_from
        part(at, out_tiles, grad_output, True, same)
        at += out_tiles
        part(at, query_width // cols, grad_query, False, same)
        at += query_width // cols
        part(at, kv_width // cols, grad_key, False, same)
        at += kv_width // cols
        part(at, kv_width // cols, grad_value, False, same)

    def emit_shared(t, side, value, number):
        cut = columns(side * (blocks // 2) + lax.div(t, 2))

        @pl.when(lax.rem(t, 2) == 0)
        def _():
            fetch(value, grad_gate.at[:, cut], emit_sem.at[number])

        @pl.when(lax.rem(t, 2) == 1)
        def _():
            fetch(value, grad_up.at[:, cut], emit_sem.at[number])

    def emitted(number):
        pltpu.make_async_copy(turned.at[0], turned.at[0], emit_sem.at[number]).wait()

    def compute(xs, cs, ct, gate_w, up_w, down_w, staged, inner, gives):
        pairs = ((mlp_in, xs), (cot, cs), (cot_t, ct))
        for at, (source, target) in enumerate(pairs[:2]):
            fetch(source, target, sem.at[at])

        def weights(t, slot):
            at = columns(block_of(t))
            return (
                pltpu.make_async_copy(w_gate.at[:, at], gate_w.at[slot], w_sem.at[slot, 0]),
                pltpu.make_async_copy(w_up.at[:, at], up_w.at[slot], w_sem.at[slot, 1]),
                pltpu.make_async_copy(w_down.at[at, :], down_w.at[slot], w_sem.at[slot, 2]),
            )

        for copy in weights(0, 0):
            copy.start()
        for at, (source, target) in enumerate(pairs[:2]):
            pltpu.make_async_copy(source, target, sem.at[at]).wait()
        fetch(cot_t, ct, sem.at[2])

        def store(tile):
            slot = lax.rem(tile, 2)
            return pltpu.make_async_copy(staged.at[slot], total.parts.at[tile], store_sem.at[slot])

        def store_inner(t):
            slot = lax.rem(t, 2)
            target = inner_out.at[:, columns(block_of(t))]
            return pltpu.make_async_copy(inner.at[slot], target, give_sem.at[2 + slot])

        def store_gives(t):
            return [
                pltpu.make_async_copy(
                    gives.at[j], total.give.at[2 * lax.div(t, 2) + j], give_sem.at[j]
                )
                for j in range(2)
            ]

        def leaves(t):
            return half_of(block_of(t)) != me.side

        def block(t, carry):
            slot = lax.rem(t, 2)
            for copy in weights(t, slot):
                copy.wait()

            @pl.when(t + 1 < blocks)
            def _():
                for copy in weights(t + 1, 1 - slot):
                    copy.start()

            @pl.when(t >= 2)
            def _():
                store_inner(t - 2).wait()

            at = columns(block_of(t))

            def some(m, carry):
                own = pl.ds(pl.multiple_of(m * half, half), half)
                gate = forward_dot(xs[own, :], gate_w[slot])
                up = forward_dot(xs[own, :], up_w[slot])
                back = nt_dot(cs[own, :], down_w[slot])
                sig = 1.0 / (1.0 + jnp.exp(-gate))
                silu = gate * sig
                inner[slot, own, :] = (silu * up).astype(bf16)
                grad_gate_low = (back * up * sig * (1.0 + gate * (1.0 - sig))).astype(bf16)
                grad_up_low = (back * silu).astype(bf16)
                acts[0, own, at] = grad_gate_low
                acts[1, own, at] = grad_up_low

                @pl.when(leaves(t))
                def _():
                    lines = line // 2
                    there = pl.ds(m * lines, lines)
                    shape = (lines, side_rows, cols)
                    gives[0, there] = grad_gate_low.astype(f32).reshape(shape)
                    gives[1, there] = grad_up_low.astype(f32).reshape(shape)

                return carry

            lax.fori_loop(0, 2, some, 0)
            store_inner(t).start()

            @pl.when(leaves(t))
            def _():
                for copy in store_gives(t):
                    copy.start()

            @pl.when(t == 0)
            def _():
                pltpu.make_async_copy(cot_t, ct, sem.at[2]).wait()

            outer_tile(ct, inner[slot], staged.at[slot])
            store(t).start()

            @pl.when(t == 0)
            def _():
                store(t).wait()

            @pl.when(t > 1)
            def _():
                store(t - 1).wait()
                total.begin(t - 1)

            @pl.when(leaves(t))
            def _():
                for copy in store_gives(t):
                    copy.wait()

            for number, after in enumerate((0, 2)):
                pl.when(t == after)(
                    lambda number=number: total.step(number, emit_tile, emit_shared, emitted)
                )
            return carry

        lax.fori_loop(0, blocks, block, 0)
        store(blocks - 1).wait()
        store_inner(blocks - 2).wait()
        store_inner(blocks - 1).wait()

    pl.run_scoped(
        compute,
        pltpu.VMEM(mlp_in.shape, bf16),
        pltpu.VMEM(mlp_in.shape, bf16),
        pltpu.VMEM(mlp_in_t.shape, bf16),
        pltpu.VMEM((2, width, cols), bf16),
        pltpu.VMEM((2, width, cols), bf16),
        pltpu.VMEM((2, cols, width), bf16),
        pltpu.VMEM((2, line, 2, side_rows, cols), f32),
        pltpu.VMEM((2, token_count, cols), bf16),
        pltpu.VMEM((2, line, side_rows, cols), f32),
    )

    def pass_on(*held):
        (gate_w, up_w, down_w, hidden_load, token_load, out_buf, out_w, left_t, staged, q_low,
         k_low, v_low, k_t, d_context, right, lse, cos, sin, raw, d_query, d_key, d_value,
         heads, inner_load, other_load, other_turn, left_cut) = held
        summing = NarrowSum(me, sems, buffers)
        small = SmallSum(me, gains, gain_lands, gain_send, gain_recv)
        gains[...] = jnp.zeros_like(gains)
        gain_at = (
            slice(0, width), slice(width, 2 * width), slice(2 * width, 2 * width + head),
            slice(2 * width + head, 2 * width + 2 * head),
        )
        loads = ((w_output, out_w), (q_in, q_low), (k_in, k_low), (v_in, v_low), (lse_in, lse),
                 (cosine, cos), (sine, sin))
        for a, b in loads:
            fetch(a, b, sem.at[0]).wait()
        k_t[...] = k_low[...].T
        step = gate_w.shape[1]

        def weights_of(kind, at, slot):
            cut = pl.ds(at * step, step)
            if kind == 0:
                gate = gate_w.at[slot, :, 0:hidden_units]
                return [
                    pltpu.make_async_copy(w_gate.at[cut, :], gate, w_sem.at[slot, 0]),
                    pltpu.make_async_copy(w_up.at[cut, :], up_w.at[slot], w_sem.at[slot, 1]),
                ]
            if kind == 1:
                return [
                    pltpu.make_async_copy(w_down.at[:, cut], down_w.at[slot], w_sem.at[slot, 2])
                ]
            start, found = 0, []
            for j, w in enumerate((w_query, w_key, w_value)):
                there = gate_w.at[slot, :, start : start + w.shape[1]]
                found.append(pltpu.make_async_copy(w.at[cut, :], there, w_sem.at[slot, j]))
                start += w.shape[1]
            return found

        def of_kind(c, body):
            kind = lax.div(c, chunks)
            for number in range(3):
                pl.when(kind == number)(functools.partial(body, number))

        def chunk_rows(c):
            at = lax.rem(c, chunks) * rows
            return pl.ds(pl.multiple_of(at, 2 * rows), 2 * rows)

        def inner_copy(c):
            return pltpu.make_async_copy(inner_out.at[chunk_rows(c), :], inner_load, sem.at[4])

        def ahead_of_produce(c):
            def start(kind):
                if kind == 1:
                    inner_copy(c).start()
                for at in range(2):
                    for copy in weights_of(kind, at, at):
                        copy.start()

            pl.when(lax.rem(c, 2) == 0)(lambda: of_kind(c, start))

        def produce(c, part):
            own = chunk_rows(c)
            count = width // step

            def make(kind):
                if kind == 1:
                    inner_copy(c).wait()
                for at in range(count):
                    slot = at % 2
                    if 1 <= at < count - 1:
                        for copy in weights_of(kind, at + 1, 1 - slot):
                            copy.start()
                    for copy in weights_of(kind, at, slot):
                        copy.wait()
                    if kind == 0:
                        value = nt_dot(acts[0, own, :], gate_w[slot, :, 0:hidden_units])
                        value = value + nt_dot(acts[1, own, :], up_w[slot])
                    elif kind == 1:
                        value = forward_dot(inner_load[...], down_w[slot])
                    else:
                        value = nt_dot(heads[own, :], gate_w[slot, :, 0:all_heads])
                    store_part(part, value, slice(at * step, (at + 1) * step))

            of_kind(c, make)

        def preload(c):
            chunk, kind = lax.rem(c, chunks), lax.div(c, chunks)

            @pl.when(kind < 2)
            def _():
                fetch(hidden.at[chunk], hidden_load, sem.at[0])

            @pl.when(kind == 0)
            def _():
                fetch(cot.at[own_rows(chunk), :], token_load, sem.at[1])

            @pl.when(kind == 2)
            def _():
                fetch(grad_hidden.at[chunk], hidden_load, sem.at[0])
                fetch(tokens.at[own_rows(chunk), :], token_load, sem.at[1])

        def work(c, pulled):
            kind = lax.div(c, chunks)
            pltpu.make_async_copy(hidden_load, hidden_load, sem.at[0]).wait()

            @pl.when(kind != 1)
            def _():
                pltpu.make_async_copy(token_load, token_load, sem.at[1]).wait()

            @pl.when(kind == 0)
            def _():
                mid = hidden_load[...]
                inverse = inverse_rms(mid)
                unit = mid * inverse
                gains[:, gain_at[1]] += jnp.sum(pulled * unit, axis=0, keepdims=True)
                back = norm_back(pulled, unit, inverse, mlp_gain[...])
                out_buf[...] = token_load[...].astype(f32) + back
                fetch(out_buf, grad_hidden.at[lax.rem(c, chunks)], sem.at[2])

            @pl.when(kind == 1)
            def _():
                out_buf[...] = hidden_load[...] + pulled

            @pl.when(kind == 2)
            def _():
                mid = token_load[...].astype(f32)
                inverse = inverse_rms(mid)
                unit = mid * inverse
                gains[:, gain_at[0]] += jnp.sum(pulled * unit, axis=0, keepdims=True)
                out_buf[...] = hidden_load[...] + norm_back(pulled, unit, inverse, attn_gain[...])

            return out_buf[...]

        def settle(s):
            def two(c):
                @pl.when(lax.div(c, chunks) == 0)
                def _():
                    pltpu.make_async_copy(out_buf, out_buf, sem.at[2]).wait()

            def four(c):
                @pl.when(lax.div(c, chunks) > 0)
                def _():
                    pltpu.make_async_copy(summing.low, summing.low, sem.at[3]).wait()

            summing.at_stage(s, 2, two)
            summing.at_stage(s, 4, four)

        def own_rows(chunk):
            at = chunk * rows + me.core * 2 * quarter + me.chip * quarter
            return pl.ds(pl.multiple_of(at, quarter), quarter)

        def lower(value):
            return value.astype(bf16)

        def emit_rows(c, low):
            chunk = lax.rem(c, chunks)
            kind = lax.div(c, chunks)

            @pl.when(kind == 0)
            def _():
                own = pl.ds(pl.multiple_of(chunk * rows, rows), rows)
                value = low[...].reshape(rows, width)
                d_context[own, :] = nt_dot(value, out_w[...]).astype(bf16)
                left_t[:, own] = value.T

            @pl.when(kind == 1)
            def _():
                fetch(low, output.at[chunk], sem.at[3])

            @pl.when(kind == 2)
            def _():
                fetch(low, grad_tokens.at[chunk], sem.at[3])

        def take_other(c):
            mine, theirs = other_load.at[me.core], other_load.at[1 - me.core]

            @pl.when(c < chunks - 1)
            def _():
                a = fetch(other.at[c], mine, att_sem.at[0])
                fetch(other_land.at[c], theirs, give_sem.at[0]).wait()
                a.wait()

            @pl.when(c == chunks - 1)
            def _():
                rest_pass.wait()
                a = fetch(rest_land, mine, att_sem.at[0])
                fetch(rest_core, theirs, give_sem.at[0]).wait()
                a.wait()

            value = (other_load[...] * mlp_gain[...][None, None]).astype(bf16)
            other_turn[...] = value.reshape(rows, width).T
            at = pl.ds(pl.multiple_of(c * rows, rows), rows)
            fetch(other_turn, other_t.at[:, at], att_sem.at[0]).wait()

        def put_shared(t, s):
            total.give_copy(t).wait()
            load = fetch(total.give_land.at[t], total.got, att_sem.at[0])
            mine = acts[lax.rem(t, 2), :, columns(me.side * (blocks // 2) + lax.div(t, 2))]
            group = left_cut.shape[2]
            count = width // group

            def copies(m, slot):
                at = pl.ds(pl.multiple_of(m * group, group), group)
                return (
                    pltpu.make_async_copy(mlp_in_t.at[at, :], left_cut.at[slot, 0], other_sem.at[2 + slot]),
                    pltpu.make_async_copy(other_t.at[at, :], left_cut.at[slot, 1], other_sem.at[4 + slot]),
                )

            for copy in copies(0, 0):
                copy.start()
            load.wait()
            right[...] = total.got[...].reshape(token_count, cols).astype(bf16)

            def one(m, carry):
                slot = lax.rem(m, 2)
                for copy in copies(m, slot):
                    copy.wait()

                @pl.when(m + 1 < count)
                def _():
                    for copy in copies(m + 1, 1 - slot):
                        copy.start()

                value = forward_dot(left_cut[slot, 0], mine) + forward_dot(left_cut[slot, 1], right[...])
                lines = group // (2 * side_rows)
                staged[pl.ds(m * lines, lines)] = value.reshape((lines, 2, side_rows, cols))
                return carry

            lax.fori_loop(0, count, one, 0)
            fetch(staged, total.parts.at[early_tiles + t], store_sem.at[0])
            total.ring[lax.rem(s, total.ring.shape[0])] = staged[:, 1 - me.side]

        def shared_stored():
            pltpu.make_async_copy(staged, total.parts.at[0], store_sem.at[0]).wait()

        def put(tile, right_value):
            outer_tile(left_t, right_value, staged)
            fetch(staged, total.parts.at[tile], store_sem.at[0]).wait()

        def rope_norm_back(grad, raw_value, gain, at):
            scaled = grad * cos[...] - half_turn(grad) * sin[...]
            inverse = inverse_rms(raw_value)
            unit = raw_value * inverse
            gains[:, at] += jnp.sum(scaled * unit, axis=0, keepdims=True)
            return norm_back(scaled, unit, inverse, gain[...])

        def attend_back(h):
            kv = lax.div(h, group)
            cut = pl.ds(pl.multiple_of(h * head, head), head)
            kv_cut = pl.ds(pl.multiple_of(kv * head, head), head)

            @pl.when(lax.rem(h, group) == 0)
            def _():
                d_key[...] = jnp.zeros_like(d_key)
                d_value[...] = jnp.zeros_like(d_value)

            load = fetch(q_raw.at[:, cut], raw, att_sem.at[0])
            size = min(256, token_count)
            for i in range(token_count // size):
                own, keys = slice(i * size, (i + 1) * size), (i + 1) * size
                q, dc = q_low[own, cut], d_context[own, cut]
                scores = nt_dot(k_low[0:keys, kv_cut], q) * scale
                expd = jnp.exp(scores - lse[pl.ds(h, 1), own])
                probs = jnp.where(allowed_pairs(keys, own, starts[:, own]), expd, 0.0)
                d_value[0:keys, :] += forward_dot(probs.astype(bf16), dc)
                d_probs = nt_dot(v_low[0:keys, kv_cut], dc)
                mean = jnp.sum(probs * d_probs, axis=0, keepdims=True)
                d_scores = (probs * (d_probs - mean)).astype(bf16)
                d_key[0:keys, :] += forward_dot(d_scores, q)
                d_query[own, :] = forward_dot(k_t[kv_cut, 0:keys], d_scores).T
            load.wait()
            heads[:, cut] = rope_norm_back(
                d_query[...] * scale, raw[...], query_gain, gain_at[2]
            ).astype(bf16)

            @pl.when(lax.rem(h, group) == group - 1)
            def _():
                fetch(k_raw.at[:, kv_cut], raw, att_sem.at[0]).wait()
                there = pl.ds(pl.multiple_of(query_width + kv * head, head), head)
                heads[:, there] = rope_norm_back(
                    d_key[...] * scale, raw[...], key_gain, gain_at[3]
                ).astype(bf16)
                there = pl.ds(pl.multiple_of(query_width + kv_width + kv * head, head), head)
                heads[:, there] = d_value[...].astype(bf16)

        small_at = summing.slots - 3
        steps = small_at + 5
        while slot_at(steps) < total.slots:
            steps += 1

        def shared_at(s):
            paired, pair, second, _ = total.item(s)
            return paired & total.here(pair, second) & (s < total.items)

        def settle_all(r):
            s = narrow_from + r - lax.div(r, pace)

            @pl.when((r >= 0) & (lax.rem(r, pace) != pace - 1))
            def _():
                total.settle(s, emitted)
                pl.when(shared_at(s))(shared_stored)

            settle(r)

        def body(r, carry):
            s = narrow_from + r - lax.div(r, pace)
            wide_too = lax.rem(r, pace) != pace - 1
            settle_all(r - 1)
            summing.at_stage(r, 0, ahead_of_produce)

            @pl.when(r == first_attend)
            def _():
                for t in range(out_tiles):
                    cut = slice(t * cols, (t + 1) * cols)
                    fetch(context.at[:, cut], right, att_sem.at[0]).wait()
                    put(late_from + t, right[...])

            @pl.when((r >= first_attend) & (r < first_heads))
            def _():
                def one(h, carry):
                    attend_back((r - first_attend) * heads_at_once + h)
                    return carry

                lax.fori_loop(0, heads_at_once, one, 0)

            @pl.when(r == first_heads)
            def _():
                fetch(normed_t, left_t, att_sem.at[0]).wait()

                def one(t, carry):
                    put(late_from + out_tiles + t, heads[:, columns(t)])
                    return carry

                lax.fori_loop(0, all_heads // cols, one, 0)

            @pl.when(r == 0)
            def _():
                other_copy.wait()
                rest_side.wait()
                rest_pass.start()

            @pl.when(r < chunks // 2)
            def _():
                for each in range(2):
                    take_other(r * 2 + each)

            @pl.when(wide_too & shared_at(s))
            def _():
                put_shared(total.item(s)[1] - 1, s)

            summing.at_stage(r, 2, preload)
            pl.when(wide_too)(lambda: total.fetches(s))
            summing.step(r, produce, work, lower, emit_rows)

            @pl.when(wide_too)
            def _():
                total.sums(s, emit_tile, emit_shared)

            pl.when(r >= small_at)(lambda: small.step(r - small_at))
            return carry

        lax.fori_loop(0, steps, body, 0)
        settle_all(steps - 1)
        total.finish()

    step = min(256, width)
    pl.run_scoped(
        pass_on,
        pltpu.VMEM((2, step, max(hidden_units, all_heads)), bf16),
        pltpu.VMEM((2, step, hidden_units), bf16),
        pltpu.VMEM((2, hidden_units, step), bf16),
        pltpu.VMEM((quarter, width), f32),
        pltpu.VMEM((quarter, width), bf16),
        pltpu.VMEM((quarter, width), f32),
        pltpu.VMEM(w_output.shape, bf16),
        pltpu.VMEM(normed_t.shape, bf16),
        pltpu.VMEM((line, 2, side_rows, cols), f32),
        pltpu.VMEM(q_in.shape, bf16),
        pltpu.VMEM(k_in.shape, bf16),
        pltpu.VMEM(v_in.shape, bf16),
        pltpu.VMEM((kv_width, token_count), bf16),
        pltpu.VMEM(q_in.shape, bf16),
        pltpu.VMEM((token_count, cols), bf16),
        pltpu.VMEM(lse_in.shape, f32),
        pltpu.VMEM(cosine.shape, f32),
        pltpu.VMEM(sine.shape, f32),
        pltpu.VMEM((token_count, head), f32),
        pltpu.VMEM((token_count, head), f32),
        pltpu.VMEM((token_count, head), f32),
        pltpu.VMEM((token_count, head), f32),
        pltpu.VMEM((token_count, all_heads), bf16),
        pltpu.VMEM((2 * rows, hidden_units), bf16),
        pltpu.VMEM((2, 2, quarter, width), f32),
        pltpu.VMEM((width, rows), bf16),
        pltpu.VMEM((2, 2, max(512, 2 * side_rows), token_count), bf16),
    )
    fetch(gains, gains_out, sem.at[0]).wait()


def call(kernel, collective_id, out_shape, in_specs, out_specs, scratch, arrays):
    return pl.pallas_call(
        kernel,
        out_shape=out_shape,
        in_specs=in_specs,
        out_specs=out_specs,
        scratch_shapes=scratch,
        compiler_params=pltpu.CompilerParams(
            collective_id=collective_id,
            has_side_effects=True,
            vmem_limit_bytes=62 * 1024 * 1024,
        ),
    )(*arrays)


def per_device(
    wide,
    tokens,
    seq_lengths,
    attn_gain,
    w_query,
    key_weight,
    value_weight,
    query_gain,
    key_norm_gain,
    w_output,
    mlp_gain,
    w_gate,
    w_up,
    w_down,
    cotangent,
):
    token_count, width = tokens.shape
    head_dim = query_gain.shape[0]
    query_width, kv_width = w_query.shape[1], key_weight.shape[1]
    hidden_units = w_gate.shape[1]
    all_heads = query_width + 2 * kv_width
    line = wide // 2
    side_rows = width // wide
    chunks = 8
    rows = token_count // chunks
    quarter = rows // 4
    block = min(256, token_count)
    dma = pltpu.SemaphoreType.DMA
    shape = jax.ShapeDtypeStruct

    segment_index, token_positions = layout(seq_lengths, token_count)
    token_positions = token_positions.reshape(-1)
    starts = (jnp.arange(token_count, dtype=jnp.int32) - token_positions)[None]
    cosine, sine = tables(token_positions, head_dim)
    cosine = cosine.reshape(token_count, head_dim)
    sign = jnp.where(jnp.arange(head_dim) < head_dim // 2, -1.0, 1.0).astype(f32)
    sine = sine.reshape(token_count, head_dim) * sign
    q_heads = query_width // head_dim

    kept = [
        shape((token_count, query_width), bf16),
        shape((token_count, kv_width), bf16),
        shape((token_count, kv_width), bf16),
        shape((token_count, query_width), f32),
        shape((token_count, kv_width), f32),
        shape((token_count, query_width), bf16),
        shape((q_heads, token_count), f32),
    ]
    vmem = [pltpu.VMEM(k.shape, k.dtype) for k in kept]
    outs = call(
        lambda *refs: attend_kernel(wide, chunks, *refs),
        1,
        [
            shape((chunks, 2, 2, quarter, width), bf16),
            shape((width, token_count), bf16),
            shape((width, token_count), bf16),
            shape((width, token_count), bf16),
            shape((chunks, quarter, width), f32),
            *kept,
            shape((chunks - 1, 2, quarter, width), f32),
            shape((2, quarter, width), f32),
        ],
        [in_vmem, any_space] + [in_vmem] * 11,
        [any_space] * 14,
        [
            *NarrowSum.sems(chunks),
            *NarrowSum.buffers(quarter, width),
            pltpu.VMEM((quarter, width), f32),
            *vmem[:3],
            pltpu.VMEM((kv_width, token_count), bf16),
            *vmem[3:],
            pltpu.VMEM((block, width), bf16),
            pltpu.VMEM((width, block), bf16),
            pltpu.VMEM((rows, width), bf16),
            pltpu.VMEM((width, rows), bf16),
            pltpu.VMEM((width, rows), bf16),
            dma((6,)),
            dma((7,)),
            dma((chunks,)),
            dma((chunks,)),
        ],
        (
            tokens, cotangent, w_query, key_weight, value_weight, w_output, attn_gain[None],
            mlp_gain[None], query_gain[None], key_norm_gain[None], cosine, sine, starts,
        ),
    )
    (mlp_in, mlp_in_t, cot_t, normed_t, hidden, q_low, k_low, v_low, q_raw, k_raw, context,
     lse, other, rest) = outs[:14]

    cols = min(256 if line <= 4 else 128, hidden_units // 6)
    counts = (hidden_units // cols, hidden_units // cols, (query_width + all_heads) // cols)
    gain_width = 2 * width + 2 * head_dim
    outs = call(
        lambda *refs: main_kernel(wide, chunks, counts, *refs),
        2,
        [
            shape((chunks, 2, 2, quarter, width), bf16),
            shape((chunks, 2, 2, quarter, width), bf16),
            shape((side_rows, query_width), f32),
            shape((side_rows, kv_width), f32),
            shape((side_rows, kv_width), f32),
            shape((query_width, side_rows), f32),
            shape((side_rows, hidden_units), f32),
            shape((side_rows, hidden_units), f32),
            shape((hidden_units, side_rows), f32),
            shape((1, gain_width), f32),
            shape((chunks, quarter, width), f32),
            shape((token_count, hidden_units), bf16),
            shape((chunks - 1, 2, quarter, width), f32),
            shape((2, quarter, width), f32),
            shape((2, quarter, width), f32),
            shape((width, token_count), bf16),
            *WideSum.lands(counts, line, side_rows, cols),
        ],
        [any_space] * 25 + [in_vmem] * 5,
        [any_space] * 23,
        [
            *WideSum.sems(counts, line),
            *NarrowSum.sems(3 * chunks),
            *WideSum.buffers(line, side_rows, cols),
            *NarrowSum.buffers(quarter, width),
            pltpu.VMEM((2, token_count, hidden_units), bf16),
            pltpu.VMEM((1, gain_width), f32),
            pltpu.VMEM((2 + line, 1, gain_width), f32),
            pltpu.VMEM((2, cols, side_rows), f32),
            dma((2 + line,)),
            dma((2 + line,)),
            dma((5,)),
            dma((2, 3)),
            dma((2,)),
            dma((3,)),
            dma((1,)),
            dma((4,)),
            dma((10,)),
        ],
        (
            mlp_in.reshape(token_count, width), mlp_in_t, cotangent, cot_t, normed_t, hidden,
            other, rest, q_low, k_low, v_low, q_raw, k_raw, context, lse, tokens, w_gate, w_up, w_down,
            w_output, w_query, key_weight, value_weight, cosine, sine, starts, attn_gain[None],
            mlp_gain[None], query_gain[None], key_norm_gain[None],
        ),
    )
    (output, grad_tokens, shard_query, shard_key, shard_value, shard_output, shard_gate,
     shard_up, shard_down, gains) = outs[:10]
    gains = gains[0]
    at = lax.axis_index("wide")
    head_part = head_dim // wide

    def own(start, size):
        return lax.dynamic_slice_in_dim(gains, start + at * size, size)

    return (
        output.reshape(token_count, width),
        grad_tokens.reshape(token_count, width),
        own(0, side_rows),
        shard_query,
        shard_key,
        shard_value,
        own(2 * width, head_part),
        own(2 * width + head_dim, head_part),
        shard_output,
        own(width, side_rows),
        shard_gate,
        shard_up,
        shard_down,
    )


def solution(mesh):
    def run(*arrays):
        return per_device(mesh.shape["wide"], *arrays)

    return jax.shard_map(
        run,
        mesh=mesh,
        in_specs=(
            P("wide", None),
            P("wide", None),
            P(),
            P(None, "narrow"),
            P(None, "narrow"),
            P(None, "narrow"),
            P(),
            P(),
            P("narrow", None),
            P(),
            P(None, "narrow"),
            P(None, "narrow"),
            P("narrow", None),
            P("wide", None),
        ),
        out_specs=(
            P("wide", None),
            P("wide", None),
            P("wide"),
            P("wide", "narrow"),
            P("wide", "narrow"),
            P("wide", "narrow"),
            P("wide"),
            P("wide"),
            P("narrow", "wide"),
            P("wide"),
            P("wide", "narrow"),
            P("wide", "narrow"),
            P("narrow", "wide"),
        ),
        check_vma=False,
    )
```

```python
import functools

import jax
import jax.numpy as jnp
from jax import lax
from jax.experimental import pallas as pl
from jax.experimental.pallas import tpu as pltpu
from jax.sharding import PartitionSpec as P

norm_eps = 1e-06
rope_base = 1000000.0
masked_score = -1e30
bf16 = jnp.bfloat16
f32 = jnp.float32


def inverse_rms(values):
    return lax.rsqrt(jnp.mean(values * values, axis=-1, keepdims=True) + norm_eps)


def layout(seq_lengths, row_len):
    seq_ends = jnp.cumsum(seq_lengths, axis=-1)
    starts = seq_ends - seq_lengths
    places = jnp.arange(row_len, dtype=jnp.int32)
    segment_index = jnp.sum(
        (places[None, :, None] >= seq_ends[:, None, :]).astype(jnp.int32), axis=-1
    )
    belongs = (
        segment_index[:, :, None]
        == jnp.arange(seq_lengths.shape[-1], dtype=jnp.int32)[None, None, :]
    )
    seq_start = jnp.sum(jnp.where(belongs, starts[:, None, :], 0), axis=-1)
    return (segment_index, places[None, :] - seq_start)


def tables(token_positions, head_dim):
    half_width = head_dim // 2
    frequency = rope_base ** (-2.0 * jnp.arange(half_width, dtype=f32) / head_dim)
    angles = token_positions.astype(f32)[:, None] * frequency[None, :]
    angles = jnp.concatenate([angles, angles], axis=-1)
    return (jnp.cos(angles)[:, None, :], jnp.sin(angles)[:, None, :])


def forward_dot(left_side, right_side):
    return jnp.dot(left_side, right_side, preferred_element_type=f32)


MESH = pl.DeviceIdType.MESH
any_space = pl.BlockSpec(memory_space=pl.ANY)
in_vmem = pl.BlockSpec(memory_space=pltpu.VMEM)


def nt_dot(left_side, right_side):
    return lax.dot_general(
        left_side, right_side, (((1,), (1,)), ((), ())), preferred_element_type=f32
    )


def fetch(source, target, sem):
    copy = pltpu.make_async_copy(source, target, sem)
    copy.start()
    return copy


class Spot:
    def __init__(self, wide):
        self.line = wide // 2
        self.w = lax.axis_index("wide")
        self.n = lax.axis_index("narrow")
        self.spot = lax.div(self.w, 2)
        self.side = lax.rem(self.w, 2)
        self.core = lax.rem(self.n, 2)
        self.chip = lax.div(self.n, 2)
        self.to_core = {"narrow": self.n + 1 - 2 * self.core}
        self.to_chip = {"narrow": self.n + 2 - 4 * self.chip}
        self.to_side = {"wide": self.w + 1 - 2 * self.side}
        self.to_up = {"wide": self.w + 2}
        self.to_down = {"wide": self.w - 2}

    def along(self, distance):
        there = lax.rem(self.spot + distance, self.line)
        return {"wide": there * 2 + self.side}

    def greet(self, line_too):
        barrier = pltpu.get_barrier_semaphore()

        def tell(who):
            pl.semaphore_signal(barrier, inc=1, device_id=who, device_id_type=MESH)

        tell(self.to_core)
        tell(self.to_chip)
        tell(self.to_side)
        if line_too:
            for distance in range(1, self.line):
                tell(self.along(distance))
        pl.semaphore_wait(barrier, 2 + self.line if line_too else 3)


def remote(source, target, send, recv, who):
    return pltpu.make_async_remote_copy(
        src_ref=source, dst_ref=target, send_sem=send, recv_sem=recv,
        device_id=who, device_id_type=MESH,
    )


class WideSum:
    ahead = 3
    join_after = 5
    held_back = 0

    @staticmethod
    def lag(line):
        return 2 if line <= 4 else 1

    @staticmethod
    def numbers(counts):
        early, shared, late = counts
        firsts, pairs = early - 1 + late, 1 + shared
        return early + shared + late, firsts, pairs, firsts + 2 * pairs

    @classmethod
    def lands(cls, counts, line, rows, cols):
        tiles, firsts, pairs, items = cls.numbers(counts)
        return [
            jax.ShapeDtypeStruct((tiles, line, 2, rows, cols), f32),
            jax.ShapeDtypeStruct((firsts, line, rows, cols), f32),
            jax.ShapeDtypeStruct((items, line - 1, rows, cols), f32),
            jax.ShapeDtypeStruct((items, line - 1, rows, cols), f32),
            jax.ShapeDtypeStruct((pairs, rows, cols), f32),
            jax.ShapeDtypeStruct((counts[1], line, rows, cols), f32),
            jax.ShapeDtypeStruct((counts[1], line, rows, cols), f32),
        ]

    @classmethod
    def sems(cls, counts, line):
        dma, hops = pltpu.SemaphoreType.DMA, line - 1
        tiles, firsts, pairs, items = cls.numbers(counts)
        return [
            dma((firsts,)), dma((firsts,)), dma((2, hops)), dma((items, hops)), dma((2, hops)),
            dma((items, hops)),
            dma((pairs,)), dma((pairs,)), dma((counts[1],)), dma((counts[1],)), dma((7,)),
        ]

    @classmethod
    def buffers(cls, line, rows, cols):
        tile = (line, rows, cols)
        return [
            pltpu.VMEM(tile, f32),
            pltpu.VMEM((cls.lag(line) * (line - 1) + 1,) + tile, f32),
            pltpu.VMEM((2, line - 1, rows, cols), f32),
            pltpu.VMEM((2, line - 1, rows, cols), f32),
            pltpu.VMEM((line - 1, rows, cols), f32),
            pltpu.VMEM((line - 1, rows, cols), f32),
            pltpu.VMEM((4, rows, cols), f32),
            pltpu.VMEM((3, rows, cols), f32),
            pltpu.VMEM((3, rows, cols), f32),
        ]

    def __init__(self, me, counts, ready, lands, sems, buffers):
        self.me, self.line = me, me.line
        self.early, self.shared, self.late = counts
        (self.parts, self.y_land, self.up_land, self.down_land, self.last_land, self.give,
         self.give_land) = lands
        (self.y_send, self.y_recv, self.up_send, self.up_recv, self.down_send, self.down_recv,
         self.last_send, self.last_recv, self.give_send, self.give_recv, self.local) = sems
        (self.got, self.ring, self.up_buf, self.down_buf, self.up_load, self.down_load, self.last,
         self.leave, self.hold) = buffers
        self.tiles, self.firsts, self.pairs, self.items = self.numbers(counts)
        self.shared_from = self.early + 1
        before = self.shared - self.held_back
        self.late_from = self.shared_from + 2 * before
        self.rest_from = self.late_from + self.late
        used = [(2 + u, False, u) for u in range(self.early - 1)]
        used += [(self.shared_from + 2 * t, True, t) for t in range(before)]
        used += [(self.late_from + k, False, self.early - 1 + k) for k in range(self.late)]
        used += [(self.rest_from + 2 * k, True, before + k) for k in range(self.held_back)]
        self.sending = []
        for m in range(self.ahead, len(used)):
            slot, shared, number = used[m]
            late = number - (self.early - 1)
            made = 0 if shared or late < 0 else ready(late)
            at = max(used[m - self.ahead][0], made)
            assert at < slot
            self.sending.append((at, shared, number))

    def item(self, s):
        rest = s >= self.rest_from
        among = s - self.shared_from - jnp.where(rest, self.late, 0)
        start = s < 2
        paired = start | rest | ((among >= 0) & (s < self.late_from))
        pair = jnp.where(start, 0, 1 + lax.div(among, 2))
        half = jnp.where(start, s, lax.rem(among, 2))
        first = jnp.where(among < 0, s - 2, s - self.late_from + self.early - 1)
        return paired, pair, half, first

    def pair_tile(self, pair):
        return jnp.where(pair == 0, 0, self.early - 1 + pair)

    def first_tile(self, first):
        made = self.early - 1
        return jnp.where(first < made, first + 1, first + 1 + self.shared)

    def begin(self, tile):
        @pl.when((tile > 0) & (tile <= self.ahead))
        def _():
            self.y_copy(tile - 1).start()

    def y_copy(self, first):
        return remote(
            self.parts.at[self.first_tile(first), :, 1 - self.me.side], self.y_land.at[first],
            self.y_send.at[first], self.y_recv.at[first], self.me.to_side,
        )

    def give_copy(self, shared):
        return remote(
            self.give.at[shared], self.give_land.at[shared],
            self.give_send.at[shared], self.give_recv.at[shared], self.me.to_side,
        )

    def last_copy(self, pair):
        return remote(
            self.leave.at[lax.rem(pair, 3)], self.last_land.at[pair],
            self.last_send.at[pair], self.last_recv.at[pair], self.me.to_side,
        )

    def up_copy(self, item, at):
        slot = lax.rem(item, 2)
        return remote(
            self.up_buf.at[slot, at], self.up_land.at[item, at],
            self.up_send.at[slot, at], self.up_recv.at[item, at], self.me.to_up,
        )

    def down_copy(self, item, at):
        slot = lax.rem(item, 2)
        return remote(
            self.down_buf.at[slot, at], self.down_land.at[item, at],
            self.down_send.at[slot, at], self.down_recv.at[item, at], self.me.to_down,
        )

    def await_up(self, item, at):
        land = self.up_land.at[item, at]
        remote(
            land, land, self.up_send.at[0, 0], self.up_recv.at[item, at], self.me.to_up
        ).wait_recv()

    def await_down(self, item, at):
        land = self.down_land.at[item, at]
        remote(
            land, land, self.down_send.at[0, 0], self.down_recv.at[item, at], self.me.to_down
        ).wait_recv()

    @property
    def slots(self):
        return self.items + self.lag(self.line) * (self.line - 1)

    def stages(self, s, first, up, down, last):
        me, line, items = self.me, self.line, self.items
        lag = self.lag(line)
        pl.when(s < items)(lambda: first(*self.item(s)))

        def at(item, found, body, *more):
            pl.when(found & (item >= 0) & (item < items))(lambda: body(item, *more))

        for k in range(line - 1):
            at(s - lag * k, me.spot == k, up, k, line - 1 - k)
        for k in range(1, line):
            at(s - lag * (line - 1 - k), me.spot == k, down, k, k)
        at(s - lag * (line - 1), s >= 0, last)

    @staticmethod
    def here(pair, half):
        return (pair > 0) & (half == 0)

    def joined(self, item):
        before = item - self.join_after
        paired, pair, half, _ = self.item(before)
        now_paired, now_pair, now_half, _ = self.item(item)
        soon = self.pairs - self.held_back
        late = now_paired & (now_half == 1) & (now_pair >= soon)
        joins = late | ((before >= 0) & paired & (half == 0) & (pair < soon))
        return joins, jnp.where(late, now_pair, pair)

    def fetches(self, s):
        me, line = self.me, self.line
        depth = self.ring.shape[0]
        for at, shared, number in self.sending:
            @pl.when(s == at)
            def _(shared=shared, number=number):
                (self.give_copy if shared else self.y_copy)(number).start()

        def first(paired, pair, half, number):
            held = self.ring.at[lax.rem(s, depth)]

            @pl.when(paired & jnp.logical_not(self.here(pair, half)))
            def _():
                side = jnp.where(half == 0, 1 - me.side, me.side)
                fetch(self.parts.at[self.pair_tile(pair), :, side], held, self.local.at[0])

            @pl.when(jnp.logical_not(paired))
            def _():
                fetch(self.parts.at[self.first_tile(number), :, me.side], held, self.local.at[0])
                self.y_copy(number).wait()
                fetch(self.y_land.at[number], self.got, self.local.at[1])

        def up(item, k, count):
            if k == 0:
                return

            @pl.when(item < self.items - 1)
            def _():
                for at in range(count + 1):
                    self.await_up(item, at)
                fetch(
                    self.up_land.at[item, 1 : count + 1], self.up_load.at[0:count],
                    self.local.at[2],
                )

        def down(item, k, count):
            if k == line - 1:
                return

            @pl.when(item < self.items - 1)
            def _():
                for at in range(count + 1):
                    self.await_down(item, at)
                fetch(
                    self.down_land.at[item, 0:count], self.down_load.at[0:count],
                    self.local.at[3],
                )

        def last(item):
            final = item == self.items - 1

            @pl.when((me.spot == line - 1) | (final & (me.spot > 0)))
            def _():
                self.await_up(item, 0)

            @pl.when((me.spot == 0) | (final & (me.spot < line - 1)))
            def _():
                self.await_down(item, me.spot)

            @pl.when(me.spot > 0)
            def _():
                fetch(self.up_land.at[item, 0], self.last.at[0], self.local.at[4])

            @pl.when(me.spot < line - 1)
            def _():
                fetch(self.down_land.at[item, me.spot], self.last.at[1], self.local.at[5])

            joins, pair = self.joined(item)

            @pl.when(joins)
            def _():
                self.last_copy(pair).wait()
                fetch(self.last_land.at[pair], self.last.at[3], self.local.at[6])

        self.stages(s, first, up, down, last)

    def loaded(self, target, at):
        pltpu.make_async_copy(target, target, self.local.at[at]).wait()

    def sums(self, s, emit, emit_shared):
        me, line = self.me, self.line
        depth = self.ring.shape[0]

        def first(paired, pair, half, number):
            held = lax.rem(s, depth)

            @pl.when(jnp.logical_not(paired & self.here(pair, half)))
            def _():
                self.loaded(self.ring.at[held], 0)

            @pl.when(jnp.logical_not(paired))
            def _():
                self.loaded(self.got, 1)
                self.ring[held] = self.ring[held] + self.got[...]

        def up(item, k, count):
            slot, held = lax.rem(item, 2), lax.rem(item, depth)
            order = range(count - 1, -1, -1)

            @pl.when(item >= 2)
            def _():
                for at in order:
                    self.up_copy(item, at).wait_send()

            if k == 0:
                self.up_buf[slot, 0:count] = self.ring[held, 1:line]
                for at in order:
                    self.up_copy(item, at).start()
                return

            @pl.when(item < self.items - 1)
            def _():
                self.loaded(self.up_load.at[0:count], 2)
                self.up_buf[slot, 0:count] = self.ring[held, k + 1 : line] + self.up_load[0:count]
                for at in order:
                    self.up_copy(item, at).start()

            @pl.when(item == self.items - 1)
            def _():
                for at in order:
                    self.await_up(item, at + 1)
                    fetch(
                        self.up_land.at[item, at + 1], self.up_load.at[at], self.local.at[2]
                    ).wait()
                    self.up_buf[slot, at] = self.ring[held, k + 1 + at] + self.up_load[at]
                    self.up_copy(item, at).start()

        def down(item, k, count):
            slot, held = lax.rem(item, 2), lax.rem(item, depth)
            order = range(count)

            @pl.when(item >= 2)
            def _():
                for at in order:
                    self.down_copy(item, at).wait_send()

            if k == line - 1:
                self.down_buf[slot, 0:count] = self.ring[held, 0:count]
                for at in order:
                    self.down_copy(item, at).start()
                return

            @pl.when(item < self.items - 1)
            def _():
                self.loaded(self.down_load.at[0:count], 3)
                self.down_buf[slot, 0:count] = self.ring[held, 0:count] + self.down_load[0:count]
                for at in order:
                    self.down_copy(item, at).start()

            @pl.when(item == self.items - 1)
            def _():
                for at in order:
                    self.await_down(item, at)
                    fetch(
                        self.down_land.at[item, at], self.down_load.at[at], self.local.at[3]
                    ).wait()
                    self.down_buf[slot, at] = self.ring[held, at] + self.down_load[at]
                    self.down_copy(item, at).start()

        def last(item):
            paired, pair, half, number = self.item(item)
            self.last[2] = self.ring[lax.rem(item, depth), me.spot]

            @pl.when(me.spot > 0)
            def _():
                self.loaded(self.last.at[0], 4)
                self.last[2] = self.last[2] + self.last[0]

            @pl.when(me.spot < line - 1)
            def _():
                self.loaded(self.last.at[1], 5)
                self.last[2] = self.last[2] + self.last[1]

            @pl.when(paired & (half == 0))
            def _():
                self.leave[lax.rem(pair, 3)] = self.last[2]
                self.last_copy(pair).start()

            @pl.when(paired & (half == 1))
            def _():
                self.hold[lax.rem(pair, 3)] = self.last[2]

            @pl.when(jnp.logical_not(paired))
            def _():
                emit(self.first_tile(number), self.last.at[2], 0)

            joins, pair = self.joined(item)

            @pl.when(joins)
            def _():
                self.loaded(self.last.at[3], 6)
                third = lax.rem(pair, 3)

                @pl.when(pair == 0)
                def _():
                    self.hold[third] = self.hold[third] + self.last[3]
                    emit(0, self.hold.at[third], 1)

                @pl.when(pair > 0)
                def _():
                    emit_shared(pair - 1, me.side, self.hold.at[third], 1)
                    emit_shared(pair - 1, 1 - me.side, self.last.at[3], 2)

        self.stages(s, first, up, down, last)

    def settle(self, s, emitted):
        def nothing(*_):
            pass

        def last(item):
            paired, _, _, _ = self.item(item)
            pl.when(jnp.logical_not(paired))(lambda: emitted(0))
            joins, pair = self.joined(item)
            pl.when(joins)(lambda: emitted(1))
            pl.when(joins & (pair > 0))(lambda: emitted(2))

        self.stages(s, nothing, nothing, nothing, last)

    def step(self, s, emit, emit_shared, emitted):
        self.fetches(s)
        self.sums(s, emit, emit_shared)
        self.settle(s, emitted)

    def finish(self):
        me, line = self.me, self.line
        for k in range(line - 1):
            @pl.when(me.spot == k)
            def _(k=k):
                for item in range(self.items - 2, self.items):
                    for at in range(line - 1 - k):
                        self.up_copy(item, at).wait_send()

        for k in range(1, line):
            @pl.when(me.spot == k)
            def _(k=k):
                for item in range(self.items - 2, self.items):
                    for at in range(k):
                        self.down_copy(item, at).wait_send()


class NarrowSum:
    @staticmethod
    def sems(chunks):
        dma = pltpu.SemaphoreType.DMA
        return [dma((chunks,)) for _ in range(8)]

    @staticmethod
    def buffers(quarter, width):
        return [
            pltpu.VMEM((2, 2, 2, quarter, width), f32),
            pltpu.VMEM((2, 2, quarter, width), f32),
            pltpu.VMEM((2, 2, quarter, width), f32),
            pltpu.VMEM((2, quarter, width), f32),
            pltpu.VMEM((3, 2, quarter, width), f32),
            pltpu.VMEM((2, 2, quarter, width), f32),
            pltpu.VMEM((2, 2, quarter, width), bf16),
        ]

    def __init__(self, me, sems, buffers):
        self.me = me
        (self.s0, self.r0, self.s1, self.r1, self.s2, self.r2, self.s3, self.r3) = sems
        (self.part, self.core_land, self.half, self.chip_land, self.pair, self.last_land,
         self.low) = buffers
        self.chunks = self.s0.shape[0]

    def copies(self, stage, c):
        me, slot, third = self.me, lax.rem(c, 2), lax.rem(c, 3)
        if stage == 0:
            return remote(self.part.at[slot, 1 - me.core], self.core_land.at[slot],
                          self.s0.at[c], self.r0.at[c], me.to_core)
        if stage == 1:
            return remote(self.half.at[slot, 1 - me.chip], self.chip_land.at[slot],
                          self.s1.at[c], self.r1.at[c], me.to_chip)
        if stage == 2:
            return remote(self.pair.at[third, me.chip], self.pair.at[third, me.chip],
                          self.s2.at[c], self.r2.at[c], me.to_chip)
        return remote(self.pair.at[third], self.last_land.at[slot],
                      self.s3.at[c], self.r3.at[c], me.to_core)

    @property
    def slots(self):
        return self.chunks + 4

    def at_stage(self, s, number, body):
        c = s - number
        pl.when((c >= 0) & (c < self.chunks))(lambda: body(c))

    def step(self, s, produce, work, lower, emit, beside=None):
        me = self.me

        def stage(number, body):
            def run(c):
                if number > 0:
                    self.copies(number - 1, c).wait()
                body(c, lax.rem(c, 2), lax.rem(c, 3))
                if number < 4:
                    self.copies(number, c).start()

            self.at_stage(s, number, run)

        def four(c, slot, third):
            self.low[me.core] = lower(self.pair[third])
            self.low[1 - me.core] = lower(self.last_land[slot])
            emit(c, self.low)

        def three(c, slot, third):
            if beside is not None:
                beside(c, self.pair.at[third])

        def two(c, slot, third):
            self.pair[third, me.chip] = work(c, self.half[slot, me.chip] + self.chip_land[slot])

        def one(c, slot, third):
            self.half[slot] = self.part[slot, me.core] + self.core_land[slot]

        def zero(c, slot, third):
            pl.when(slot == 0)(lambda: produce(c, self.part))

        stage(4, four)
        stage(3, three)
        stage(2, two)
        stage(1, one)
        stage(0, zero)


def take(refs, count):
    return refs[:count], refs[count:]


def store_part(part, value, columns):
    part[:, :, :, :, columns] = value.reshape(2, 2, 2, value.shape[0] // 8, value.shape[1])


def norm_back(pulled, unit, scale, gain):
    scaled = pulled * gain
    return scale * (scaled - unit * jnp.mean(scaled * unit, axis=-1, keepdims=True))


def half_turn(values):
    return pltpu.roll(values, values.shape[-1] // 2, values.ndim - 1)


def allowed_pairs(keys, rows, starts):
    count = rows.stop - rows.start
    key = lax.broadcasted_iota(jnp.int32, (keys, count), 0)
    query = lax.broadcasted_iota(jnp.int32, (keys, count), 1) + rows.start
    return (key <= query) & (key >= starts)


def attend_kernel(wide, chunks, *refs):
    (tokens, cot, w_query, w_key, w_value, w_output, attn_gain, mlp_gain, query_gain, key_gain,
     cosine, sine, starts), refs = take(refs, 13)
    (mlp_in, mlp_in_t, cot_t, normed_t, hidden_out, q_out, k_out, v_out, q_raw_out, k_raw_out,
     context_out, lse_out, other_out, rest_out), refs = take(refs, 14)
    sems, refs = take(refs, 8)
    buffers, refs = take(refs, 7)
    (hidden_buf, q_low, k_low, v_low, v_t, q_raw, k_raw, context, lse, normed, normed_turn,
     cot_load, cot_turn, low_turn, sem, out_sem, give_sem, take_sem) = refs
    me = Spot(wide)
    me.greet(False)
    summing = NarrowSum(me, sems, buffers)
    token_count, width = tokens.shape
    rows = token_count // chunks
    quarter = rows // 4
    block = normed.shape[0]
    per_block = block // rows
    head = query_gain.shape[1]
    q_heads = w_query.shape[1] // head
    group = q_heads // (w_key.shape[1] // head)
    scale = head ** (-0.5)
    step = min(512, width)
    kept = (
        (q_low, q_out), (k_low, k_out), (v_low, v_out), (q_raw, q_raw_out), (k_raw, k_raw_out),
        (context, context_out), (lse, lse_out),
    )

    def attend(i):
        own = slice(i * block, (i + 1) * block)
        keys = (i + 1) * block
        x = tokens[own, :].astype(f32)
        normed[...] = (x * inverse_rms(x) * attn_gain[...]).astype(bf16)
        cos, sin = cosine[own, :], sine[own, :]

        def heads_of(raw, low, gain):
            for h in range(raw.shape[1] // head):
                cut = slice(h * head, (h + 1) * head)
                u = raw[own, cut]
                y = u * inverse_rms(u) * gain[...]
                low[own, cut] = (y * cos + half_turn(y) * sin).astype(bf16)

        q_raw[own, :] = forward_dot(normed[...], w_query[...])
        k_raw[own, :] = forward_dot(normed[...], w_key[...])
        value = forward_dot(normed[...], w_value[...])
        v_low[own, :] = value.astype(bf16)
        v_t[:, own] = value.T.astype(bf16)
        heads_of(q_raw, q_low, query_gain)
        heads_of(k_raw, k_low, key_gain)
        allowed = allowed_pairs(keys, own, starts[:, own])
        for h in range(q_heads):
            cut, kv = slice(h * head, (h + 1) * head), h // group
            kv_cut = slice(kv * head, (kv + 1) * head)
            scores = nt_dot(k_low[0:keys, kv_cut], q_low[own, cut]) * scale
            scores = jnp.where(allowed, scores, masked_score)
            top = jnp.max(scores, axis=0, keepdims=True)
            expd = jnp.exp(scores - top)
            total = jnp.sum(expd, axis=0, keepdims=True)
            probs = (expd / total).astype(bf16)
            lse[h : h + 1, own] = top + jnp.log(total)
            mixed = forward_dot(v_t[kv_cut, 0:keys], probs)
            context[own, cut] = mixed.T.astype(bf16)

    def produce(c, part):
        for i in range(token_count // block):
            pl.when(c == i * per_block)(functools.partial(attend, i))
        left = context[pl.ds(pl.multiple_of(c * rows, 2 * rows), 2 * rows), :]
        for at in range(0, width, step):
            store_part(part, forward_dot(left, w_output[:, at : at + step]), slice(at, at + step))

    def work(c, total):
        at = pl.multiple_of(c * rows + me.core * 2 * quarter + me.chip * quarter, quarter)
        hidden = tokens[pl.ds(at, quarter), :].astype(f32) + total
        hidden_buf[...] = hidden
        fetch(hidden_buf, hidden_out.at[c], sem.at[2])
        return hidden * inverse_rms(hidden)

    def lower(value):
        return (value * mlp_gain[...]).astype(bf16)

    def emit(c, low):
        @pl.when(c < chunks - 1)
        def _():
            beside(c, summing.pair.at[lax.rem(c, 3)]).wait_send()

        @pl.when(c == chunks - 1)
        def _():
            pltpu.make_async_copy(summing.pair.at[lax.rem(c, 3)], rest_out, sem.at[5]).wait()

        fetch(low, mlp_in.at[c], sem.at[3])
        low_turn[...] = low[...].reshape(rows, width).T
        at = pl.ds(pl.multiple_of(c * rows, rows), rows)
        fetch(low_turn, mlp_in_t.at[:, at], sem.at[4])

    def settle(s):
        def two(c):
            pltpu.make_async_copy(hidden_buf, hidden_out.at[c], sem.at[2]).wait()

        def four(c):
            pltpu.make_async_copy(summing.low, mlp_in.at[c], sem.at[3]).wait()
            at = pl.ds(pl.multiple_of(c * rows, rows), rows)
            pltpu.make_async_copy(low_turn, mlp_in_t.at[:, at], sem.at[4]).wait()

        summing.at_stage(s, 2, two)
        summing.at_stage(s, 4, four)

    def beside(c, half):
        return remote(half, other_out.at[c], give_sem.at[c], take_sem.at[c], me.to_side)

    def begin_beside(c, half):
        @pl.when(c < chunks - 1)
        def _():
            beside(c, half).start()

        @pl.when(c == chunks - 1)
        def _():
            fetch(half, rest_out, sem.at[5])

    def turn_rows(s):
        at = pl.ds(pl.multiple_of(s * rows, rows), rows)
        fetch(cot.at[at, :], cot_load, sem.at[0]).wait()
        cot_turn[...] = cot_load[...].T
        a = fetch(cot_turn, cot_t.at[:, at], sem.at[1])

        @pl.when(lax.rem(s, per_block) == 0)
        def _():
            normed_turn[...] = normed[...].T
            wide_at = pl.ds(pl.multiple_of(s * rows, block), block)
            fetch(normed_turn, normed_t.at[:, wide_at], sem.at[0]).wait()

        a.wait()

    def body(s, carry):
        summing.step(s, produce, work, lower, emit, begin_beside)
        pl.when(s < chunks)(lambda: turn_rows(s))

        @pl.when(s == chunks - 1)
        def _():
            for at, (a, b) in enumerate(kept):
                fetch(a, b, out_sem.at[at])

        settle(s)
        return carry

    lax.fori_loop(0, summing.slots, body, 0)
    for at, (a, b) in enumerate(kept):
        pltpu.make_async_copy(a, b, out_sem.at[at]).wait()
    for c in range(chunks - 1):
        beside(c, summing.pair.at[c % 3]).wait_recv()


def outer_tile(left_t, right, stage):
    line, _, rows, _ = stage.shape
    group = max(1, 512 // (2 * rows))
    while line % group:
        group -= 1

    def body(m, carry):
        at = pl.multiple_of(m * group * 2 * rows, group * 2 * rows)
        value = forward_dot(left_t[pl.ds(at, group * 2 * rows), :], right)
        stage[pl.ds(m * group, group)] = value.reshape((group, 2, rows, value.shape[1]))
        return carry

    lax.fori_loop(0, line // group, body, 0)


class SmallSum:
    def __init__(self, me, value, lands, sends, recvs):
        self.me, self.value, self.lands, self.sends, self.recvs = me, value, lands, sends, recvs

    def copy(self, k):
        me = self.me
        who = (me.to_core, me.to_chip, me.to_side)[k] if k < 3 else me.along(k - 2)
        return remote(self.value, self.lands.at[k], self.sends.at[k], self.recvs.at[k], who)

    def step(self, at):
        last = 2 + self.me.line
        stages = [[0], [1], [2], list(range(3, last)), []]
        for number, copies in enumerate(stages):
            @pl.when(at == number)
            def _(number=number, copies=copies):
                if number > 0:
                    for k in stages[number - 1]:
                        self.copy(k).wait()
                    for k in stages[number - 1]:
                        self.value[...] = self.value[...] + self.lands[k]
                for k in copies:
                    self.copy(k).start()


def main_kernel(wide, chunks, counts, *refs):
    (mlp_in, mlp_in_t, cot, cot_t, normed_t, hidden, other, rest, q_in, k_in, v_in, q_raw, k_raw,
     context, lse_in, tokens, w_gate, w_up, w_down, w_output, w_query, w_key, w_value, cosine, sine,
     starts, attn_gain, mlp_gain, query_gain, key_gain), refs = take(refs, 30)
    (output, grad_tokens, grad_query, grad_key, grad_value, grad_output, grad_gate, grad_up,
     grad_down, gains_out, grad_hidden, inner_out, other_land, rest_land, rest_core,
     other_t), refs = take(refs, 16)
    wide_lands, refs = take(refs, 7)
    wide_sems, refs = take(refs, 11)
    sems, refs = take(refs, 8)
    wide_buffers, refs = take(refs, 9)
    buffers, refs = take(refs, 7)
    (acts, gains, gain_lands, turned, gain_send, gain_recv, sem, w_sem, store_sem, emit_sem,
     att_sem, give_sem, other_sem, late_sem) = refs
    me = Spot(wide)
    me.greet(True)
    token_count, width = mlp_in.shape
    hidden_units = w_gate.shape[1]
    tiles, line, _, side_rows, cols = wide_lands[0].shape
    blocks = hidden_units // cols
    early_tiles, shared_tiles, late_tiles = counts
    late_from = early_tiles + shared_tiles
    query_width, kv_width = w_query.shape[1], w_key.shape[1]
    all_heads = query_width + 2 * kv_width
    head = query_gain.shape[1]
    q_heads = query_width // head
    group = q_heads // (kv_width // head)
    scale = head ** (-0.5)
    out_tiles = query_width // cols
    narrow_from, pace = 2, 10
    first_attend = chunks + 4
    heads_at_once = 2
    first_heads = first_attend + q_heads // heads_at_once

    def slot_at(r):
        return narrow_from + r - r // pace

    total = WideSum(
        me, counts, lambda late: slot_at(first_attend if late < out_tiles else first_heads),
        wide_lands, wide_sems, wide_buffers,
    )
    other_copy = remote(other, other_land, other_sem.at[0], other_sem.at[1], me.to_core)
    other_copy.start()
    rest_side = remote(rest, rest_land, other_sem.at[6], other_sem.at[7], me.to_side)
    rest_side.start()
    rest_pass = remote(rest_land, rest_core, other_sem.at[8], other_sem.at[9], me.to_core)
    half = token_count // 2
    rows = token_count // chunks
    quarter = rows // 4

    def block_of(t):
        return lax.rem(t, 2) * (blocks // 2) + lax.div(t, 2)

    def half_of(b):
        return lax.div(b, blocks // 2)

    def columns(at):
        return pl.ds(pl.multiple_of(at * cols, cols), cols)

    def emit_tile(tile, value, number):
        def part(first, count, target, turn, place):
            @pl.when((tile >= first) & (tile < first + count))
            def _():
                cut = columns(place(tile - first))
                if turn:
                    turned[number] = value[...].T
                    fetch(turned.at[number], target.at[cut, :], emit_sem.at[number])
                else:
                    fetch(value, target.at[:, cut], emit_sem.at[number])

        def same(at):
            return at

        part(0, early_tiles, grad_down, True, block_of)
        at = late_from
        part(at, out_tiles, grad_output, True, same)
        at += out_tiles
        part(at, query_width // cols, grad_query, False, same)
        at += query_width // cols
        part(at, kv_width // cols, grad_key, False, same)
        at += kv_width // cols
        part(at, kv_width // cols, grad_value, False, same)

    def emit_shared(t, side, value, number):
        cut = columns(side * (blocks // 2) + lax.div(t, 2))

        @pl.when(lax.rem(t, 2) == 0)
        def _():
            fetch(value, grad_gate.at[:, cut], emit_sem.at[number])

        @pl.when(lax.rem(t, 2) == 1)
        def _():
            fetch(value, grad_up.at[:, cut], emit_sem.at[number])

    def emitted(number):
        pltpu.make_async_copy(turned.at[0], turned.at[0], emit_sem.at[number]).wait()

    def compute(xs, cs, ct, gate_w, up_w, down_w, staged, inner, gives):
        pairs = ((mlp_in, xs), (cot, cs), (cot_t, ct))
        for at, (source, target) in enumerate(pairs[:2]):
            fetch(source, target, sem.at[at])

        def weights(t, slot):
            at = columns(block_of(t))
            return (
                pltpu.make_async_copy(w_gate.at[:, at], gate_w.at[slot], w_sem.at[slot, 0]),
                pltpu.make_async_copy(w_up.at[:, at], up_w.at[slot], w_sem.at[slot, 1]),
                pltpu.make_async_copy(w_down.at[at, :], down_w.at[slot], w_sem.at[slot, 2]),
            )

        for copy in weights(0, 0):
            copy.start()
        for at, (source, target) in enumerate(pairs[:2]):
            pltpu.make_async_copy(source, target, sem.at[at]).wait()
        fetch(cot_t, ct, sem.at[2])

        def store(tile):
            slot = lax.rem(tile, 2)
            return pltpu.make_async_copy(staged.at[slot], total.parts.at[tile], store_sem.at[slot])

        def store_inner(t):
            slot = lax.rem(t, 2)
            target = inner_out.at[:, columns(block_of(t))]
            return pltpu.make_async_copy(inner.at[slot], target, give_sem.at[2 + slot])

        def store_gives(t):
            return [
                pltpu.make_async_copy(
                    gives.at[j], total.give.at[2 * lax.div(t, 2) + j], give_sem.at[j]
                )
                for j in range(2)
            ]

        def leaves(t):
            return half_of(block_of(t)) != me.side

        def block(t, carry):
            slot = lax.rem(t, 2)
            for copy in weights(t, slot):
                copy.wait()

            @pl.when(t + 1 < blocks)
            def _():
                for copy in weights(t + 1, 1 - slot):
                    copy.start()

            @pl.when(t >= 2)
            def _():
                store_inner(t - 2).wait()

            at = columns(block_of(t))

            def some(m, carry):
                own = pl.ds(pl.multiple_of(m * half, half), half)
                gate = forward_dot(xs[own, :], gate_w[slot])
                up = forward_dot(xs[own, :], up_w[slot])
                back = nt_dot(cs[own, :], down_w[slot])
                sig = 1.0 / (1.0 + jnp.exp(-gate))
                silu = gate * sig
                inner[slot, own, :] = (silu * up).astype(bf16)
                grad_gate_low = (back * up * sig * (1.0 + gate * (1.0 - sig))).astype(bf16)
                grad_up_low = (back * silu).astype(bf16)
                acts[0, own, at] = grad_gate_low
                acts[1, own, at] = grad_up_low

                @pl.when(leaves(t))
                def _():
                    lines = line // 2
                    there = pl.ds(m * lines, lines)
                    shape = (lines, side_rows, cols)
                    gives[0, there] = grad_gate_low.astype(f32).reshape(shape)
                    gives[1, there] = grad_up_low.astype(f32).reshape(shape)

                return carry

            lax.fori_loop(0, 2, some, 0)
            store_inner(t).start()

            @pl.when(leaves(t))
            def _():
                for copy in store_gives(t):
                    copy.start()

            @pl.when(t == 0)
            def _():
                pltpu.make_async_copy(cot_t, ct, sem.at[2]).wait()

            outer_tile(ct, inner[slot], staged.at[slot])
            store(t).start()

            @pl.when(t == 0)
            def _():
                store(t).wait()

            @pl.when(t > 1)
            def _():
                store(t - 1).wait()
                total.begin(t - 1)

            @pl.when(leaves(t))
            def _():
                for copy in store_gives(t):
                    copy.wait()

            for number, after in enumerate((0, 2)):
                pl.when(t == after)(
                    lambda number=number: total.step(number, emit_tile, emit_shared, emitted)
                )
            return carry

        lax.fori_loop(0, blocks, block, 0)
        store(blocks - 1).wait()
        store_inner(blocks - 2).wait()
        store_inner(blocks - 1).wait()

    pl.run_scoped(
        compute,
        pltpu.VMEM(mlp_in.shape, bf16),
        pltpu.VMEM(mlp_in.shape, bf16),
        pltpu.VMEM(mlp_in_t.shape, bf16),
        pltpu.VMEM((2, width, cols), bf16),
        pltpu.VMEM((2, width, cols), bf16),
        pltpu.VMEM((2, cols, width), bf16),
        pltpu.VMEM((2, line, 2, side_rows, cols), f32),
        pltpu.VMEM((2, token_count, cols), bf16),
        pltpu.VMEM((2, line, side_rows, cols), f32),
    )

    def pass_on(*held):
        (gate_w, up_w, down_w, hidden_load, token_load, out_buf, out_w, left_t, staged, q_low,
         k_low, v_low, k_t, d_context, right, lse, cos, sin, raw, d_query, d_key, d_value,
         heads, inner_load, other_load, other_turn, left_cut) = held
        summing = NarrowSum(me, sems, buffers)
        small = SmallSum(me, gains, gain_lands, gain_send, gain_recv)
        gains[...] = jnp.zeros_like(gains)
        gain_at = (
            slice(0, width), slice(width, 2 * width), slice(2 * width, 2 * width + head),
            slice(2 * width + head, 2 * width + 2 * head),
        )
        loads = ((w_output, out_w), (q_in, q_low), (k_in, k_low), (v_in, v_low), (lse_in, lse),
                 (cosine, cos), (sine, sin))
        for a, b in loads:
            fetch(a, b, sem.at[0]).wait()
        k_t[...] = k_low[...].T
        step = gate_w.shape[1]

        def weights_of(kind, at, slot):
            cut = pl.ds(at * step, step)
            if kind == 0:
                gate = gate_w.at[slot, :, 0:hidden_units]
                return [
                    pltpu.make_async_copy(w_gate.at[cut, :], gate, w_sem.at[slot, 0]),
                    pltpu.make_async_copy(w_up.at[cut, :], up_w.at[slot], w_sem.at[slot, 1]),
                ]
            if kind == 1:
                return [
                    pltpu.make_async_copy(w_down.at[:, cut], down_w.at[slot], w_sem.at[slot, 2])
                ]
            start, found = 0, []
            for j, w in enumerate((w_query, w_key, w_value)):
                there = gate_w.at[slot, :, start : start + w.shape[1]]
                found.append(pltpu.make_async_copy(w.at[cut, :], there, w_sem.at[slot, j]))
                start += w.shape[1]
            return found

        def of_kind(c, body):
            kind = lax.div(c, chunks)
            for number in range(3):
                pl.when(kind == number)(functools.partial(body, number))

        def chunk_rows(c):
            at = lax.rem(c, chunks) * rows
            return pl.ds(pl.multiple_of(at, 2 * rows), 2 * rows)

        def inner_copy(c):
            return pltpu.make_async_copy(inner_out.at[chunk_rows(c), :], inner_load, sem.at[4])

        def ahead_of_produce(c):
            def start(kind):
                if kind == 1:
                    inner_copy(c).start()
                for at in range(2):
                    for copy in weights_of(kind, at, at):
                        copy.start()

            pl.when(lax.rem(c, 2) == 0)(lambda: of_kind(c, start))

        def produce(c, part):
            own = chunk_rows(c)
            count = width // step

            def make(kind):
                if kind == 1:
                    inner_copy(c).wait()
                for at in range(count):
                    slot = at % 2
                    if 1 <= at < count - 1:
                        for copy in weights_of(kind, at + 1, 1 - slot):
                            copy.start()
                    for copy in weights_of(kind, at, slot):
                        copy.wait()
                    if kind == 0:
                        value = nt_dot(acts[0, own, :], gate_w[slot, :, 0:hidden_units])
                        value = value + nt_dot(acts[1, own, :], up_w[slot])
                    elif kind == 1:
                        value = forward_dot(inner_load[...], down_w[slot])
                    else:
                        value = nt_dot(heads[own, :], gate_w[slot, :, 0:all_heads])
                    store_part(part, value, slice(at * step, (at + 1) * step))

            of_kind(c, make)

        def preload(c):
            chunk, kind = lax.rem(c, chunks), lax.div(c, chunks)

            @pl.when(kind < 2)
            def _():
                fetch(hidden.at[chunk], hidden_load, sem.at[0])

            @pl.when(kind == 0)
            def _():
                fetch(cot.at[own_rows(chunk), :], token_load, sem.at[1])

            @pl.when(kind == 2)
            def _():
                fetch(grad_hidden.at[chunk], hidden_load, sem.at[0])
                fetch(tokens.at[own_rows(chunk), :], token_load, sem.at[1])

        def work(c, pulled):
            kind = lax.div(c, chunks)
            pltpu.make_async_copy(hidden_load, hidden_load, sem.at[0]).wait()

            @pl.when(kind != 1)
            def _():
                pltpu.make_async_copy(token_load, token_load, sem.at[1]).wait()

            @pl.when(kind == 0)
            def _():
                mid = hidden_load[...]
                inverse = inverse_rms(mid)
                unit = mid * inverse
                gains[:, gain_at[1]] += jnp.sum(pulled * unit, axis=0, keepdims=True)
                back = norm_back(pulled, unit, inverse, mlp_gain[...])
                out_buf[...] = token_load[...].astype(f32) + back
                fetch(out_buf, grad_hidden.at[lax.rem(c, chunks)], sem.at[2])

            @pl.when(kind == 1)
            def _():
                out_buf[...] = hidden_load[...] + pulled

            @pl.when(kind == 2)
            def _():
                mid = token_load[...].astype(f32)
                inverse = inverse_rms(mid)
                unit = mid * inverse
                gains[:, gain_at[0]] += jnp.sum(pulled * unit, axis=0, keepdims=True)
                out_buf[...] = hidden_load[...] + norm_back(pulled, unit, inverse, attn_gain[...])

            return out_buf[...]

        def settle(s):
            def two(c):
                @pl.when(lax.div(c, chunks) == 0)
                def _():
                    pltpu.make_async_copy(out_buf, out_buf, sem.at[2]).wait()

            def four(c):
                @pl.when(lax.div(c, chunks) > 0)
                def _():
                    pltpu.make_async_copy(summing.low, summing.low, sem.at[3]).wait()

            summing.at_stage(s, 2, two)
            summing.at_stage(s, 4, four)

        def own_rows(chunk):
            at = chunk * rows + me.core * 2 * quarter + me.chip * quarter
            return pl.ds(pl.multiple_of(at, quarter), quarter)

        def lower(value):
            return value.astype(bf16)

        def emit_rows(c, low):
            chunk = lax.rem(c, chunks)
            kind = lax.div(c, chunks)

            @pl.when(kind == 0)
            def _():
                own = pl.ds(pl.multiple_of(chunk * rows, rows), rows)
                value = low[...].reshape(rows, width)
                d_context[own, :] = nt_dot(value, out_w[...]).astype(bf16)
                left_t[:, own] = value.T

            @pl.when(kind == 1)
            def _():
                fetch(low, output.at[chunk], sem.at[3])

            @pl.when(kind == 2)
            def _():
                fetch(low, grad_tokens.at[chunk], sem.at[3])

        def take_other(c):
            mine, theirs = other_load.at[me.core], other_load.at[1 - me.core]

            @pl.when(c < chunks - 1)
            def _():
                a = fetch(other.at[c], mine, att_sem.at[0])
                fetch(other_land.at[c], theirs, give_sem.at[0]).wait()
                a.wait()

            @pl.when(c == chunks - 1)
            def _():
                rest_pass.wait()
                a = fetch(rest_land, mine, att_sem.at[0])
                fetch(rest_core, theirs, give_sem.at[0]).wait()
                a.wait()

            value = (other_load[...] * mlp_gain[...][None, None]).astype(bf16)
            other_turn[...] = value.reshape(rows, width).T
            at = pl.ds(pl.multiple_of(c * rows, rows), rows)
            fetch(other_turn, other_t.at[:, at], att_sem.at[0]).wait()

        def left_copies(m, slot):
            group = left_cut.shape[2]
            at = pl.ds(pl.multiple_of(m * group, group), group)
            return (
                pltpu.make_async_copy(mlp_in_t.at[at, :], left_cut.at[slot, 0], other_sem.at[2 + slot]),
                pltpu.make_async_copy(other_t.at[at, :], left_cut.at[slot, 1], other_sem.at[4 + slot]),
            )

        def load_shared(t):
            for copy in left_copies(0, 0):
                copy.start()
            total.give_copy(t).wait()
            fetch(total.give_land.at[t], total.got, att_sem.at[0])

        def put_shared(t, s):
            pltpu.make_async_copy(total.got, total.got, att_sem.at[0]).wait()
            right[...] = total.got[...].reshape(token_count, cols).astype(bf16)
            mine = acts[lax.rem(t, 2), :, columns(me.side * (blocks // 2) + lax.div(t, 2))]
            group = left_cut.shape[2]
            count = width // group

            def one(m, carry):
                slot = lax.rem(m, 2)
                for copy in left_copies(m, slot):
                    copy.wait()

                @pl.when(m + 1 < count)
                def _():
                    for copy in left_copies(m + 1, 1 - slot):
                        copy.start()

                value = forward_dot(left_cut[slot, 0], mine) + forward_dot(left_cut[slot, 1], right[...])
                lines = group // (2 * side_rows)
                staged[pl.ds(m * lines, lines)] = value.reshape((lines, 2, side_rows, cols))
                return carry

            lax.fori_loop(0, count, one, 0)
            fetch(staged, total.parts.at[early_tiles + t], store_sem.at[0])
            total.ring[lax.rem(s, total.ring.shape[0])] = staged[:, 1 - me.side]

        def shared_stored():
            pltpu.make_async_copy(staged, total.parts.at[0], store_sem.at[0]).wait()

        def put(tile, right_value):
            outer_tile(left_t, right_value, staged)
            fetch(staged, total.parts.at[tile], store_sem.at[0]).wait()

        def rope_norm_back(grad, raw_value, gain, at):
            scaled = grad * cos[...] - half_turn(grad) * sin[...]
            inverse = inverse_rms(raw_value)
            unit = raw_value * inverse
            gains[:, at] += jnp.sum(scaled * unit, axis=0, keepdims=True)
            return norm_back(scaled, unit, inverse, gain[...])

        def attend_back(h):
            kv = lax.div(h, group)
            cut = pl.ds(pl.multiple_of(h * head, head), head)
            kv_cut = pl.ds(pl.multiple_of(kv * head, head), head)

            @pl.when(lax.rem(h, group) == 0)
            def _():
                d_key[...] = jnp.zeros_like(d_key)
                d_value[...] = jnp.zeros_like(d_value)

            load = fetch(q_raw.at[:, cut], raw, att_sem.at[0])
            size = min(256, token_count)
            for i in range(token_count // size):
                own, keys = slice(i * size, (i + 1) * size), (i + 1) * size
                q, dc = q_low[own, cut], d_context[own, cut]
                scores = nt_dot(k_low[0:keys, kv_cut], q) * scale
                expd = jnp.exp(scores - lse[pl.ds(h, 1), own])
                probs = jnp.where(allowed_pairs(keys, own, starts[:, own]), expd, 0.0)
                d_value[0:keys, :] += forward_dot(probs.astype(bf16), dc)
                d_probs = nt_dot(v_low[0:keys, kv_cut], dc)
                mean = jnp.sum(probs * d_probs, axis=0, keepdims=True)
                d_scores = (probs * (d_probs - mean)).astype(bf16)
                d_key[0:keys, :] += forward_dot(d_scores, q)
                d_query[own, :] = forward_dot(k_t[kv_cut, 0:keys], d_scores).T
            load.wait()
            heads[:, cut] = rope_norm_back(
                d_query[...] * scale, raw[...], query_gain, gain_at[2]
            ).astype(bf16)

            @pl.when(lax.rem(h, group) == group - 1)
            def _():
                fetch(k_raw.at[:, kv_cut], raw, att_sem.at[0]).wait()
                there = pl.ds(pl.multiple_of(query_width + kv * head, head), head)
                heads[:, there] = rope_norm_back(
                    d_key[...] * scale, raw[...], key_gain, gain_at[3]
                ).astype(bf16)
                there = pl.ds(pl.multiple_of(query_width + kv_width + kv * head, head), head)
                heads[:, there] = d_value[...].astype(bf16)

        small_at = summing.slots - 3
        steps = small_at + 5
        while slot_at(steps) < total.slots:
            steps += 1

        def shared_at(s):
            paired, pair, second, _ = total.item(s)
            return paired & total.here(pair, second) & (s < total.items)

        def settle_all(r):
            s = narrow_from + r - lax.div(r, pace)

            @pl.when((r >= 0) & (lax.rem(r, pace) != pace - 1))
            def _():
                total.settle(s, emitted)
                pl.when(shared_at(s))(shared_stored)

            settle(r)

        def body(r, carry):
            s = narrow_from + r - lax.div(r, pace)
            wide_too = lax.rem(r, pace) != pace - 1
            settle_all(r - 1)
            summing.at_stage(r, 0, ahead_of_produce)

            @pl.when(r == first_attend - 1)
            def _():
                fetch(context, heads.at[:, 0:query_width], late_sem.at[0])

            @pl.when(r == first_attend)
            def _():
                held = heads.at[:, 0:query_width]
                pltpu.make_async_copy(context, held, late_sem.at[0]).wait()
                for t in range(out_tiles):
                    put(late_from + t, heads[:, t * cols : (t + 1) * cols])
                fetch(normed_t, left_t, late_sem.at[0])

            @pl.when((r >= first_attend) & (r < first_heads))
            def _():
                def one(h, carry):
                    attend_back((r - first_attend) * heads_at_once + h)
                    return carry

                lax.fori_loop(0, heads_at_once, one, 0)

            @pl.when(r == first_heads)
            def _():
                pltpu.make_async_copy(normed_t, left_t, late_sem.at[0]).wait()

                def one(t, carry):
                    put(late_from + out_tiles + t, heads[:, columns(t)])
                    return carry

                lax.fori_loop(0, all_heads // cols, one, 0)

            @pl.when(r == 0)
            def _():
                other_copy.wait()
                rest_side.wait()
                rest_pass.start()

            @pl.when(r < chunks // 2)
            def _():
                for each in range(2):
                    take_other(r * 2 + each)

            pl.when(wide_too & shared_at(s))(lambda: load_shared(total.item(s)[1] - 1))
            summing.at_stage(r, 2, preload)
            pl.when(wide_too)(lambda: total.fetches(s))
            summing.step(r, produce, work, lower, emit_rows)
            pl.when(wide_too & shared_at(s))(lambda: put_shared(total.item(s)[1] - 1, s))

            @pl.when(wide_too)
            def _():
                total.sums(s, emit_tile, emit_shared)

            pl.when(r >= small_at)(lambda: small.step(r - small_at))
            return carry

        lax.fori_loop(0, steps, body, 0)
        settle_all(steps - 1)
        total.finish()

    step = min(256, width)
    pl.run_scoped(
        pass_on,
        pltpu.VMEM((2, step, max(hidden_units, all_heads)), bf16),
        pltpu.VMEM((2, step, hidden_units), bf16),
        pltpu.VMEM((2, hidden_units, step), bf16),
        pltpu.VMEM((quarter, width), f32),
        pltpu.VMEM((quarter, width), bf16),
        pltpu.VMEM((quarter, width), f32),
        pltpu.VMEM(w_output.shape, bf16),
        pltpu.VMEM(normed_t.shape, bf16),
        pltpu.VMEM((line, 2, side_rows, cols), f32),
        pltpu.VMEM(q_in.shape, bf16),
        pltpu.VMEM(k_in.shape, bf16),
        pltpu.VMEM(v_in.shape, bf16),
        pltpu.VMEM((kv_width, token_count), bf16),
        pltpu.VMEM(q_in.shape, bf16),
        pltpu.VMEM((token_count, cols), bf16),
        pltpu.VMEM(lse_in.shape, f32),
        pltpu.VMEM(cosine.shape, f32),
        pltpu.VMEM(sine.shape, f32),
        pltpu.VMEM((token_count, head), f32),
        pltpu.VMEM((token_count, head), f32),
        pltpu.VMEM((token_count, head), f32),
        pltpu.VMEM((token_count, head), f32),
        pltpu.VMEM((token_count, all_heads), bf16),
        pltpu.VMEM((2 * rows, hidden_units), bf16),
        pltpu.VMEM((2, 2, quarter, width), f32),
        pltpu.VMEM((width, rows), bf16),
        pltpu.VMEM((2, 2, max(512, 2 * side_rows), token_count), bf16),
    )
    fetch(gains, gains_out, sem.at[0]).wait()


def call(kernel, collective_id, out_shape, in_specs, out_specs, scratch, arrays):
    return pl.pallas_call(
        kernel,
        out_shape=out_shape,
        in_specs=in_specs,
        out_specs=out_specs,
        scratch_shapes=scratch,
        compiler_params=pltpu.CompilerParams(
            collective_id=collective_id,
            has_side_effects=True,
            vmem_limit_bytes=62 * 1024 * 1024,
        ),
    )(*arrays)


def per_device(
    wide,
    tokens,
    seq_lengths,
    attn_gain,
    w_query,
    key_weight,
    value_weight,
    query_gain,
    key_norm_gain,
    w_output,
    mlp_gain,
    w_gate,
    w_up,
    w_down,
    cotangent,
):
    token_count, width = tokens.shape
    head_dim = query_gain.shape[0]
    query_width, kv_width = w_query.shape[1], key_weight.shape[1]
    hidden_units = w_gate.shape[1]
    all_heads = query_width + 2 * kv_width
    line = wide // 2
    side_rows = width // wide
    chunks = 8
    rows = token_count // chunks
    quarter = rows // 4
    block = min(256, token_count)
    dma = pltpu.SemaphoreType.DMA
    shape = jax.ShapeDtypeStruct

    segment_index, token_positions = layout(seq_lengths, token_count)
    token_positions = token_positions.reshape(-1)
    starts = (jnp.arange(token_count, dtype=jnp.int32) - token_positions)[None]
    cosine, sine = tables(token_positions, head_dim)
    cosine = cosine.reshape(token_count, head_dim)
    sign = jnp.where(jnp.arange(head_dim) < head_dim // 2, -1.0, 1.0).astype(f32)
    sine = sine.reshape(token_count, head_dim) * sign
    q_heads = query_width // head_dim

    kept = [
        shape((token_count, query_width), bf16),
        shape((token_count, kv_width), bf16),
        shape((token_count, kv_width), bf16),
        shape((token_count, query_width), f32),
        shape((token_count, kv_width), f32),
        shape((token_count, query_width), bf16),
        shape((q_heads, token_count), f32),
    ]
    vmem = [pltpu.VMEM(k.shape, k.dtype) for k in kept]
    outs = call(
        lambda *refs: attend_kernel(wide, chunks, *refs),
        1,
        [
            shape((chunks, 2, 2, quarter, width), bf16),
            shape((width, token_count), bf16),
            shape((width, token_count), bf16),
            shape((width, token_count), bf16),
            shape((chunks, quarter, width), f32),
            *kept,
            shape((chunks - 1, 2, quarter, width), f32),
            shape((2, quarter, width), f32),
        ],
        [in_vmem, any_space] + [in_vmem] * 11,
        [any_space] * 14,
        [
            *NarrowSum.sems(chunks),
            *NarrowSum.buffers(quarter, width),
            pltpu.VMEM((quarter, width), f32),
            *vmem[:3],
            pltpu.VMEM((kv_width, token_count), bf16),
            *vmem[3:],
            pltpu.VMEM((block, width), bf16),
            pltpu.VMEM((width, block), bf16),
            pltpu.VMEM((rows, width), bf16),
            pltpu.VMEM((width, rows), bf16),
            pltpu.VMEM((width, rows), bf16),
            dma((6,)),
            dma((7,)),
            dma((chunks,)),
            dma((chunks,)),
        ],
        (
            tokens, cotangent, w_query, key_weight, value_weight, w_output, attn_gain[None],
            mlp_gain[None], query_gain[None], key_norm_gain[None], cosine, sine, starts,
        ),
    )
    (mlp_in, mlp_in_t, cot_t, normed_t, hidden, q_low, k_low, v_low, q_raw, k_raw, context,
     lse, other, rest) = outs[:14]

    cols = min(256 if line <= 4 else 128, hidden_units // 6)
    counts = (hidden_units // cols, hidden_units // cols, (query_width + all_heads) // cols)
    gain_width = 2 * width + 2 * head_dim
    outs = call(
        lambda *refs: main_kernel(wide, chunks, counts, *refs),
        2,
        [
            shape((chunks, 2, 2, quarter, width), bf16),
            shape((chunks, 2, 2, quarter, width), bf16),
            shape((side_rows, query_width), f32),
            shape((side_rows, kv_width), f32),
            shape((side_rows, kv_width), f32),
            shape((query_width, side_rows), f32),
            shape((side_rows, hidden_units), f32),
            shape((side_rows, hidden_units), f32),
            shape((hidden_units, side_rows), f32),
            shape((1, gain_width), f32),
            shape((chunks, quarter, width), f32),
            shape((token_count, hidden_units), bf16),
            shape((chunks - 1, 2, quarter, width), f32),
            shape((2, quarter, width), f32),
            shape((2, quarter, width), f32),
            shape((width, token_count), bf16),
            *WideSum.lands(counts, line, side_rows, cols),
        ],
        [any_space] * 25 + [in_vmem] * 5,
        [any_space] * 23,
        [
            *WideSum.sems(counts, line),
            *NarrowSum.sems(3 * chunks),
            *WideSum.buffers(line, side_rows, cols),
            *NarrowSum.buffers(quarter, width),
            pltpu.VMEM((2, token_count, hidden_units), bf16),
            pltpu.VMEM((1, gain_width), f32),
            pltpu.VMEM((2 + line, 1, gain_width), f32),
            pltpu.VMEM((2, cols, side_rows), f32),
            dma((2 + line,)),
            dma((2 + line,)),
            dma((5,)),
            dma((2, 3)),
            dma((2,)),
            dma((3,)),
            dma((1,)),
            dma((4,)),
            dma((10,)),
            dma((1,)),
        ],
        (
            mlp_in.reshape(token_count, width), mlp_in_t, cotangent, cot_t, normed_t, hidden,
            other, rest, q_low, k_low, v_low, q_raw, k_raw, context, lse, tokens, w_gate, w_up, w_down,
            w_output, w_query, key_weight, value_weight, cosine, sine, starts, attn_gain[None],
            mlp_gain[None], query_gain[None], key_norm_gain[None],
        ),
    )
    (output, grad_tokens, shard_query, shard_key, shard_value, shard_output, shard_gate,
     shard_up, shard_down, gains) = outs[:10]
    gains = gains[0]
    at = lax.axis_index("wide")
    head_part = head_dim // wide

    def own(start, size):
        return lax.dynamic_slice_in_dim(gains, start + at * size, size)

    return (
        output.reshape(token_count, width),
        grad_tokens.reshape(token_count, width),
        own(0, side_rows),
        shard_query,
        shard_key,
        shard_value,
        own(2 * width, head_part),
        own(2 * width + head_dim, head_part),
        shard_output,
        own(width, side_rows),
        shard_gate,
        shard_up,
        shard_down,
    )


def solution(mesh):
    def run(*arrays):
        return per_device(mesh.shape["wide"], *arrays)

    return jax.shard_map(
        run,
        mesh=mesh,
        in_specs=(
            P("wide", None),
            P("wide", None),
            P(),
            P(None, "narrow"),
            P(None, "narrow"),
            P(None, "narrow"),
            P(),
            P(),
            P("narrow", None),
            P(),
            P(None, "narrow"),
            P(None, "narrow"),
            P("narrow", None),
            P("wide", None),
        ),
        out_specs=(
            P("wide", None),
            P("wide", None),
            P("wide"),
            P("wide", "narrow"),
            P("wide", "narrow"),
            P("wide", "narrow"),
            P("wide"),
            P("wide"),
            P("narrow", "wide"),
            P("wide"),
            P("wide", "narrow"),
            P("wide", "narrow"),
            P("narrow", "wide"),
        ),
        check_vma=False,
    )
```

```python
import functools

import jax
import jax.numpy as jnp
from jax import lax
from jax.experimental import pallas as pl
from jax.experimental.pallas import tpu as pltpu
from jax.sharding import PartitionSpec as P

norm_eps = 1e-06
rope_base = 1000000.0
masked_score = -1e30
bf16 = jnp.bfloat16
f32 = jnp.float32


def inverse_rms(values):
    return lax.rsqrt(jnp.mean(values * values, axis=-1, keepdims=True) + norm_eps)


def layout(seq_lengths, row_len):
    seq_ends = jnp.cumsum(seq_lengths, axis=-1)
    starts = seq_ends - seq_lengths
    places = jnp.arange(row_len, dtype=jnp.int32)
    segment_index = jnp.sum(
        (places[None, :, None] >= seq_ends[:, None, :]).astype(jnp.int32), axis=-1
    )
    belongs = (
        segment_index[:, :, None]
        == jnp.arange(seq_lengths.shape[-1], dtype=jnp.int32)[None, None, :]
    )
    seq_start = jnp.sum(jnp.where(belongs, starts[:, None, :], 0), axis=-1)
    return (segment_index, places[None, :] - seq_start)


def tables(token_positions, head_dim):
    half_width = head_dim // 2
    frequency = rope_base ** (-2.0 * jnp.arange(half_width, dtype=f32) / head_dim)
    angles = token_positions.astype(f32)[:, None] * frequency[None, :]
    angles = jnp.concatenate([angles, angles], axis=-1)
    return (jnp.cos(angles)[:, None, :], jnp.sin(angles)[:, None, :])


def forward_dot(left_side, right_side):
    return jnp.dot(left_side, right_side, preferred_element_type=f32)


MESH = pl.DeviceIdType.MESH
any_space = pl.BlockSpec(memory_space=pl.ANY)
in_vmem = pl.BlockSpec(memory_space=pltpu.VMEM)


def nt_dot(left_side, right_side):
    return lax.dot_general(
        left_side, right_side, (((1,), (1,)), ((), ())), preferred_element_type=f32
    )


def fetch(source, target, sem):
    copy = pltpu.make_async_copy(source, target, sem)
    copy.start()
    return copy


class Spot:
    def __init__(self, wide):
        self.line = wide // 2
        self.w = lax.axis_index("wide")
        self.n = lax.axis_index("narrow")
        self.spot = lax.div(self.w, 2)
        self.side = lax.rem(self.w, 2)
        self.core = lax.rem(self.n, 2)
        self.chip = lax.div(self.n, 2)
        self.to_core = {"narrow": self.n + 1 - 2 * self.core}
        self.to_chip = {"narrow": self.n + 2 - 4 * self.chip}
        self.to_side = {"wide": self.w + 1 - 2 * self.side}
        self.to_up = {"wide": self.w + 2}
        self.to_down = {"wide": self.w - 2}

    def along(self, distance):
        there = lax.rem(self.spot + distance, self.line)
        return {"wide": there * 2 + self.side}

    def greet(self, line_too):
        barrier = pltpu.get_barrier_semaphore()

        def tell(who):
            pl.semaphore_signal(barrier, inc=1, device_id=who, device_id_type=MESH)

        tell(self.to_core)
        tell(self.to_chip)
        tell(self.to_side)
        if line_too:
            for distance in range(1, self.line):
                tell(self.along(distance))
        pl.semaphore_wait(barrier, 2 + self.line if line_too else 3)


def remote(source, target, send, recv, who):
    return pltpu.make_async_remote_copy(
        src_ref=source, dst_ref=target, send_sem=send, recv_sem=recv,
        device_id=who, device_id_type=MESH,
    )


class WideSum:
    ahead = 3
    join_after = 5
    held_back = 0

    @staticmethod
    def lag(line):
        return 2 if line <= 4 else 1

    @staticmethod
    def numbers(counts):
        early, shared, late = counts
        firsts, pairs = early - 1 + late, 1 + shared
        return early + shared + late, firsts, pairs, firsts + 2 * pairs

    @classmethod
    def lands(cls, counts, line, rows, cols):
        tiles, firsts, pairs, items = cls.numbers(counts)
        return [
            jax.ShapeDtypeStruct((tiles, line, 2, rows, cols), f32),
            jax.ShapeDtypeStruct((firsts, line, rows, cols), f32),
            jax.ShapeDtypeStruct((items, line - 1, rows, cols), f32),
            jax.ShapeDtypeStruct((items, line - 1, rows, cols), f32),
            jax.ShapeDtypeStruct((pairs, rows, cols), f32),
            jax.ShapeDtypeStruct((counts[1], line, rows, cols), f32),
            jax.ShapeDtypeStruct((counts[1], line, rows, cols), f32),
        ]

    @classmethod
    def sems(cls, counts, line):
        dma, hops = pltpu.SemaphoreType.DMA, line - 1
        tiles, firsts, pairs, items = cls.numbers(counts)
        return [
            dma((firsts,)), dma((firsts,)), dma((2, hops)), dma((items, hops)), dma((2, hops)),
            dma((items, hops)),
            dma((pairs,)), dma((pairs,)), dma((counts[1],)), dma((counts[1],)), dma((7,)),
        ]

    @classmethod
    def buffers(cls, line, rows, cols):
        tile = (line, rows, cols)
        return [
            pltpu.VMEM(tile, f32),
            pltpu.VMEM((cls.lag(line) * (line - 1) + 1,) + tile, f32),
            pltpu.VMEM((2, line - 1, rows, cols), f32),
            pltpu.VMEM((2, line - 1, rows, cols), f32),
            pltpu.VMEM((line - 1, rows, cols), f32),
            pltpu.VMEM((line - 1, rows, cols), f32),
            pltpu.VMEM((4, rows, cols), f32),
            pltpu.VMEM((3, rows, cols), f32),
            pltpu.VMEM((3, rows, cols), f32),
        ]

    def __init__(self, me, counts, ready, lands, sems, buffers):
        self.me, self.line = me, me.line
        self.early, self.shared, self.late = counts
        (self.parts, self.y_land, self.up_land, self.down_land, self.last_land, self.give,
         self.give_land) = lands
        (self.y_send, self.y_recv, self.up_send, self.up_recv, self.down_send, self.down_recv,
         self.last_send, self.last_recv, self.give_send, self.give_recv, self.local) = sems
        (self.got, self.ring, self.up_buf, self.down_buf, self.up_load, self.down_load, self.last,
         self.leave, self.hold) = buffers
        self.tiles, self.firsts, self.pairs, self.items = self.numbers(counts)
        self.shared_from = self.early + 1
        before = self.shared - self.held_back
        self.late_from = self.shared_from + 2 * before
        self.rest_from = self.late_from + self.late
        used = [(2 + u, False, u) for u in range(self.early - 1)]
        used += [(self.shared_from + 2 * t, True, t) for t in range(before)]
        used += [(self.late_from + k, False, self.early - 1 + k) for k in range(self.late)]
        used += [(self.rest_from + 2 * k, True, before + k) for k in range(self.held_back)]
        self.sending = []
        for m in range(self.ahead, len(used)):
            slot, shared, number = used[m]
            late = number - (self.early - 1)
            made = 0 if shared or late < 0 else ready(late)
            at = max(used[m - self.ahead][0], made)
            assert at < slot
            self.sending.append((at, shared, number))

    def item(self, s):
        rest = s >= self.rest_from
        among = s - self.shared_from - jnp.where(rest, self.late, 0)
        start = s < 2
        paired = start | rest | ((among >= 0) & (s < self.late_from))
        pair = jnp.where(start, 0, 1 + lax.div(among, 2))
        half = jnp.where(start, s, lax.rem(among, 2))
        first = jnp.where(among < 0, s - 2, s - self.late_from + self.early - 1)
        return paired, pair, half, first

    def pair_tile(self, pair):
        return jnp.where(pair == 0, 0, self.early - 1 + pair)

    def first_tile(self, first):
        made = self.early - 1
        return jnp.where(first < made, first + 1, first + 1 + self.shared)

    def begin(self, tile):
        @pl.when((tile > 0) & (tile <= self.ahead))
        def _():
            self.y_copy(tile - 1).start()

    def y_copy(self, first):
        return remote(
            self.parts.at[self.first_tile(first), :, 1 - self.me.side], self.y_land.at[first],
            self.y_send.at[first], self.y_recv.at[first], self.me.to_side,
        )

    def give_copy(self, shared):
        return remote(
            self.give.at[shared], self.give_land.at[shared],
            self.give_send.at[shared], self.give_recv.at[shared], self.me.to_side,
        )

    def last_copy(self, pair):
        return remote(
            self.leave.at[lax.rem(pair, 3)], self.last_land.at[pair],
            self.last_send.at[pair], self.last_recv.at[pair], self.me.to_side,
        )

    def up_copy(self, item, at):
        slot = lax.rem(item, 2)
        return remote(
            self.up_buf.at[slot, at], self.up_land.at[item, at],
            self.up_send.at[slot, at], self.up_recv.at[item, at], self.me.to_up,
        )

    def down_copy(self, item, at):
        slot = lax.rem(item, 2)
        return remote(
            self.down_buf.at[slot, at], self.down_land.at[item, at],
            self.down_send.at[slot, at], self.down_recv.at[item, at], self.me.to_down,
        )

    def await_up(self, item, at):
        land = self.up_land.at[item, at]
        remote(
            land, land, self.up_send.at[0, 0], self.up_recv.at[item, at], self.me.to_up
        ).wait_recv()

    def await_down(self, item, at):
        land = self.down_land.at[item, at]
        remote(
            land, land, self.down_send.at[0, 0], self.down_recv.at[item, at], self.me.to_down
        ).wait_recv()

    @property
    def slots(self):
        return self.items + self.lag(self.line) * (self.line - 1)

    def stages(self, s, first, up, down, last):
        me, line, items = self.me, self.line, self.items
        lag = self.lag(line)
        pl.when(s < items)(lambda: first(*self.item(s)))

        def at(item, found, body, *more):
            pl.when(found & (item >= 0) & (item < items))(lambda: body(item, *more))

        for k in range(line - 1):
            at(s - lag * k, me.spot == k, up, k, line - 1 - k)
        for k in range(1, line):
            at(s - lag * (line - 1 - k), me.spot == k, down, k, k)
        at(s - lag * (line - 1), s >= 0, last)

    @staticmethod
    def here(pair, half):
        return (pair > 0) & (half == 0)

    def joined(self, item):
        before = item - self.join_after
        paired, pair, half, _ = self.item(before)
        now_paired, now_pair, now_half, _ = self.item(item)
        soon = self.pairs - self.held_back
        late = now_paired & (now_half == 1) & (now_pair >= soon)
        joins = late | ((before >= 0) & paired & (half == 0) & (pair < soon))
        return joins, jnp.where(late, now_pair, pair)

    def fetches(self, s):
        me, line = self.me, self.line
        depth = self.ring.shape[0]
        for at, shared, number in self.sending:
            @pl.when(s == at)
            def _(shared=shared, number=number):
                (self.give_copy if shared else self.y_copy)(number).start()

        def first(paired, pair, half, number):
            held = self.ring.at[lax.rem(s, depth)]

            @pl.when(paired & jnp.logical_not(self.here(pair, half)))
            def _():
                side = jnp.where(half == 0, 1 - me.side, me.side)
                fetch(self.parts.at[self.pair_tile(pair), :, side], held, self.local.at[0])

            @pl.when(jnp.logical_not(paired))
            def _():
                fetch(self.parts.at[self.first_tile(number), :, me.side], held, self.local.at[0])
                self.y_copy(number).wait()
                fetch(self.y_land.at[number], self.got, self.local.at[1])

        def up(item, k, count):
            if k == 0:
                return

            @pl.when(item < self.items - 1)
            def _():
                for at in range(count + 1):
                    self.await_up(item, at)
                fetch(
                    self.up_land.at[item, 1 : count + 1], self.up_load.at[0:count],
                    self.local.at[2],
                )

        def down(item, k, count):
            if k == line - 1:
                return

            @pl.when(item < self.items - 1)
            def _():
                for at in range(count + 1):
                    self.await_down(item, at)
                fetch(
                    self.down_land.at[item, 0:count], self.down_load.at[0:count],
                    self.local.at[3],
                )

        def last(item):
            final = item == self.items - 1

            @pl.when((me.spot == line - 1) | (final & (me.spot > 0)))
            def _():
                self.await_up(item, 0)

            @pl.when((me.spot == 0) | (final & (me.spot < line - 1)))
            def _():
                self.await_down(item, me.spot)

            @pl.when(me.spot > 0)
            def _():
                fetch(self.up_land.at[item, 0], self.last.at[0], self.local.at[4])

            @pl.when(me.spot < line - 1)
            def _():
                fetch(self.down_land.at[item, me.spot], self.last.at[1], self.local.at[5])

            joins, pair = self.joined(item)

            @pl.when(joins)
            def _():
                self.last_copy(pair).wait()
                fetch(self.last_land.at[pair], self.last.at[3], self.local.at[6])

        self.stages(s, first, up, down, last)

    def loaded(self, target, at):
        pltpu.make_async_copy(target, target, self.local.at[at]).wait()

    def sums(self, s, emit, emit_shared):
        me, line = self.me, self.line
        depth = self.ring.shape[0]

        def first(paired, pair, half, number):
            held = lax.rem(s, depth)

            @pl.when(jnp.logical_not(paired & self.here(pair, half)))
            def _():
                self.loaded(self.ring.at[held], 0)

            @pl.when(jnp.logical_not(paired))
            def _():
                self.loaded(self.got, 1)
                self.ring[held] = self.ring[held] + self.got[...]

        def up(item, k, count):
            slot, held = lax.rem(item, 2), lax.rem(item, depth)
            order = range(count - 1, -1, -1)

            @pl.when(item >= 2)
            def _():
                for at in order:
                    self.up_copy(item, at).wait_send()

            if k == 0:
                self.up_buf[slot, 0:count] = self.ring[held, 1:line]
                for at in order:
                    self.up_copy(item, at).start()
                return

            @pl.when(item < self.items - 1)
            def _():
                self.loaded(self.up_load.at[0:count], 2)
                self.up_buf[slot, 0:count] = self.ring[held, k + 1 : line] + self.up_load[0:count]
                for at in order:
                    self.up_copy(item, at).start()

            @pl.when(item == self.items - 1)
            def _():
                for at in order:
                    self.await_up(item, at + 1)
                    fetch(
                        self.up_land.at[item, at + 1], self.up_load.at[at], self.local.at[2]
                    ).wait()
                    self.up_buf[slot, at] = self.ring[held, k + 1 + at] + self.up_load[at]
                    self.up_copy(item, at).start()

        def down(item, k, count):
            slot, held = lax.rem(item, 2), lax.rem(item, depth)
            order = range(count)

            @pl.when(item >= 2)
            def _():
                for at in order:
                    self.down_copy(item, at).wait_send()

            if k == line - 1:
                self.down_buf[slot, 0:count] = self.ring[held, 0:count]
                for at in order:
                    self.down_copy(item, at).start()
                return

            @pl.when(item < self.items - 1)
            def _():
                self.loaded(self.down_load.at[0:count], 3)
                self.down_buf[slot, 0:count] = self.ring[held, 0:count] + self.down_load[0:count]
                for at in order:
                    self.down_copy(item, at).start()

            @pl.when(item == self.items - 1)
            def _():
                for at in order:
                    self.await_down(item, at)
                    fetch(
                        self.down_land.at[item, at], self.down_load.at[at], self.local.at[3]
                    ).wait()
                    self.down_buf[slot, at] = self.ring[held, at] + self.down_load[at]
                    self.down_copy(item, at).start()

        def last(item):
            paired, pair, half, number = self.item(item)
            self.last[2] = self.ring[lax.rem(item, depth), me.spot]

            @pl.when(me.spot > 0)
            def _():
                self.loaded(self.last.at[0], 4)
                self.last[2] = self.last[2] + self.last[0]

            @pl.when(me.spot < line - 1)
            def _():
                self.loaded(self.last.at[1], 5)
                self.last[2] = self.last[2] + self.last[1]

            @pl.when(paired & (half == 0))
            def _():
                self.leave[lax.rem(pair, 3)] = self.last[2]
                self.last_copy(pair).start()

            @pl.when(paired & (half == 1))
            def _():
                self.hold[lax.rem(pair, 3)] = self.last[2]

            @pl.when(jnp.logical_not(paired))
            def _():
                emit(self.first_tile(number), self.last.at[2], 0)

            joins, pair = self.joined(item)

            @pl.when(joins)
            def _():
                self.loaded(self.last.at[3], 6)
                third = lax.rem(pair, 3)

                @pl.when(pair == 0)
                def _():
                    self.hold[third] = self.hold[third] + self.last[3]
                    emit(0, self.hold.at[third], 1)

                @pl.when(pair > 0)
                def _():
                    emit_shared(pair - 1, me.side, self.hold.at[third], 1)
                    emit_shared(pair - 1, 1 - me.side, self.last.at[3], 2)

        self.stages(s, first, up, down, last)

    def settle(self, s, emitted):
        def nothing(*_):
            pass

        def last(item):
            paired, _, _, _ = self.item(item)
            pl.when(jnp.logical_not(paired))(lambda: emitted(0))
            joins, pair = self.joined(item)
            pl.when(joins)(lambda: emitted(1))
            pl.when(joins & (pair > 0))(lambda: emitted(2))

        self.stages(s, nothing, nothing, nothing, last)

    def step(self, s, emit, emit_shared, emitted):
        self.fetches(s)
        self.sums(s, emit, emit_shared)
        self.settle(s, emitted)

    def finish(self):
        me, line = self.me, self.line
        for k in range(line - 1):
            @pl.when(me.spot == k)
            def _(k=k):
                for item in range(self.items - 2, self.items):
                    for at in range(line - 1 - k):
                        self.up_copy(item, at).wait_send()

        for k in range(1, line):
            @pl.when(me.spot == k)
            def _(k=k):
                for item in range(self.items - 2, self.items):
                    for at in range(k):
                        self.down_copy(item, at).wait_send()


class NarrowSum:
    @staticmethod
    def sems(chunks):
        dma = pltpu.SemaphoreType.DMA
        return [dma((chunks,)) for _ in range(8)]

    @staticmethod
    def buffers(quarter, width):
        return [
            pltpu.VMEM((2, 2, 2, quarter, width), f32),
            pltpu.VMEM((2, 2, quarter, width), f32),
            pltpu.VMEM((2, 2, quarter, width), f32),
            pltpu.VMEM((2, quarter, width), f32),
            pltpu.VMEM((3, 2, quarter, width), f32),
            pltpu.VMEM((2, 2, quarter, width), f32),
            pltpu.VMEM((2, 2, quarter, width), bf16),
        ]

    def __init__(self, me, sems, buffers):
        self.me = me
        (self.s0, self.r0, self.s1, self.r1, self.s2, self.r2, self.s3, self.r3) = sems
        (self.part, self.core_land, self.half, self.chip_land, self.pair, self.last_land,
         self.low) = buffers
        self.chunks = self.s0.shape[0]

    def copies(self, stage, c):
        me, slot, third = self.me, lax.rem(c, 2), lax.rem(c, 3)
        if stage == 0:
            return remote(self.part.at[slot, 1 - me.core], self.core_land.at[slot],
                          self.s0.at[c], self.r0.at[c], me.to_core)
        if stage == 1:
            return remote(self.half.at[slot, 1 - me.chip], self.chip_land.at[slot],
                          self.s1.at[c], self.r1.at[c], me.to_chip)
        if stage == 2:
            return remote(self.pair.at[third, me.chip], self.pair.at[third, me.chip],
                          self.s2.at[c], self.r2.at[c], me.to_chip)
        return remote(self.pair.at[third], self.last_land.at[slot],
                      self.s3.at[c], self.r3.at[c], me.to_core)

    @property
    def slots(self):
        return self.chunks + 4

    def at_stage(self, s, number, body):
        c = s - number
        pl.when((c >= 0) & (c < self.chunks))(lambda: body(c))

    def step(self, s, produce, work, lower, emit, beside=None, only=(4, 3, 2, 1, 0)):
        me = self.me

        def stage(number, body):
            def run(c):
                if number > 0:
                    self.copies(number - 1, c).wait()
                body(c, lax.rem(c, 2), lax.rem(c, 3))
                if number < 4:
                    self.copies(number, c).start()

            self.at_stage(s, number, run)

        def four(c, slot, third):
            self.low[me.core] = lower(self.pair[third])
            self.low[1 - me.core] = lower(self.last_land[slot])
            emit(c, self.low)

        def three(c, slot, third):
            if beside is not None:
                beside(c, self.pair.at[third])

        def two(c, slot, third):
            self.pair[third, me.chip] = work(c, self.half[slot, me.chip] + self.chip_land[slot])

        def one(c, slot, third):
            self.half[slot] = self.part[slot, me.core] + self.core_land[slot]

        def zero(c, slot, third):
            pl.when(slot == 0)(lambda: produce(c, self.part))

        for number in only:
            stage(number, (zero, one, two, three, four)[number])


def take(refs, count):
    return refs[:count], refs[count:]


def store_part(part, value, columns):
    part[:, :, :, :, columns] = value.reshape(2, 2, 2, value.shape[0] // 8, value.shape[1])


def norm_back(pulled, unit, scale, gain):
    scaled = pulled * gain
    return scale * (scaled - unit * jnp.mean(scaled * unit, axis=-1, keepdims=True))


def half_turn(values):
    return pltpu.roll(values, values.shape[-1] // 2, values.ndim - 1)


def allowed_pairs(keys, rows, starts):
    count = rows.stop - rows.start
    key = lax.broadcasted_iota(jnp.int32, (keys, count), 0)
    query = lax.broadcasted_iota(jnp.int32, (keys, count), 1) + rows.start
    return (key <= query) & (key >= starts)


def attend_kernel(wide, chunks, *refs):
    (tokens, cot, w_query, w_key, w_value, w_output, attn_gain, mlp_gain, query_gain, key_gain,
     cosine, sine, starts), refs = take(refs, 13)
    (mlp_in, mlp_in_t, cot_t, normed_t, hidden_out, q_out, k_out, v_out, q_raw_out, k_raw_out,
     context_out, lse_out, other_out, rest_out), refs = take(refs, 14)
    sems, refs = take(refs, 8)
    buffers, refs = take(refs, 7)
    (hidden_buf, q_low, k_low, v_low, v_t, q_raw, k_raw, context, lse, normed, normed_turn,
     cot_load, cot_turn, low_turn, sem, out_sem, give_sem, take_sem) = refs
    me = Spot(wide)
    me.greet(False)
    summing = NarrowSum(me, sems, buffers)
    token_count, width = tokens.shape
    rows = token_count // chunks
    quarter = rows // 4
    block = normed.shape[0]
    per_block = block // rows
    head = query_gain.shape[1]
    q_heads = w_query.shape[1] // head
    group = q_heads // (w_key.shape[1] // head)
    scale = head ** (-0.5)
    step = min(512, width)
    kept = (
        (q_low, q_out), (k_low, k_out), (v_low, v_out), (q_raw, q_raw_out), (k_raw, k_raw_out),
        (context, context_out), (lse, lse_out),
    )

    def attend(i):
        own = slice(i * block, (i + 1) * block)
        keys = (i + 1) * block
        x = tokens[own, :].astype(f32)
        normed[...] = (x * inverse_rms(x) * attn_gain[...]).astype(bf16)
        cos, sin = cosine[own, :], sine[own, :]

        def heads_of(raw, low, gain):
            for h in range(raw.shape[1] // head):
                cut = slice(h * head, (h + 1) * head)
                u = raw[own, cut]
                y = u * inverse_rms(u) * gain[...]
                low[own, cut] = (y * cos + half_turn(y) * sin).astype(bf16)

        q_raw[own, :] = forward_dot(normed[...], w_query[...])
        k_raw[own, :] = forward_dot(normed[...], w_key[...])
        value = forward_dot(normed[...], w_value[...])
        v_low[own, :] = value.astype(bf16)
        v_t[:, own] = value.T.astype(bf16)
        heads_of(q_raw, q_low, query_gain)
        heads_of(k_raw, k_low, key_gain)
        allowed = allowed_pairs(keys, own, starts[:, own])
        for h in range(q_heads):
            cut, kv = slice(h * head, (h + 1) * head), h // group
            kv_cut = slice(kv * head, (kv + 1) * head)
            scores = nt_dot(k_low[0:keys, kv_cut], q_low[own, cut]) * scale
            scores = jnp.where(allowed, scores, masked_score)
            top = jnp.max(scores, axis=0, keepdims=True)
            expd = jnp.exp(scores - top)
            total = jnp.sum(expd, axis=0, keepdims=True)
            probs = (expd / total).astype(bf16)
            lse[h : h + 1, own] = top + jnp.log(total)
            mixed = forward_dot(v_t[kv_cut, 0:keys], probs)
            context[own, cut] = mixed.T.astype(bf16)

    def produce(c, part):
        for i in range(token_count // block):
            pl.when(c == i * per_block)(functools.partial(attend, i))
        left = context[pl.ds(pl.multiple_of(c * rows, 2 * rows), 2 * rows), :]
        for at in range(0, width, step):
            store_part(part, forward_dot(left, w_output[:, at : at + step]), slice(at, at + step))

    def work(c, total):
        at = pl.multiple_of(c * rows + me.core * 2 * quarter + me.chip * quarter, quarter)
        hidden = tokens[pl.ds(at, quarter), :].astype(f32) + total
        hidden_buf[...] = hidden
        fetch(hidden_buf, hidden_out.at[c], sem.at[2])
        return hidden * inverse_rms(hidden)

    def lower(value):
        return (value * mlp_gain[...]).astype(bf16)

    def emit(c, low):
        @pl.when(c < chunks - 1)
        def _():
            beside(c, summing.pair.at[lax.rem(c, 3)]).wait_send()

        @pl.when(c == chunks - 1)
        def _():
            pltpu.make_async_copy(summing.pair.at[lax.rem(c, 3)], rest_out, sem.at[5]).wait()

        fetch(low, mlp_in.at[c], sem.at[3])
        low_turn[...] = low[...].reshape(rows, width).T
        at = pl.ds(pl.multiple_of(c * rows, rows), rows)
        fetch(low_turn, mlp_in_t.at[:, at], sem.at[4])

    def settle(s):
        def two(c):
            pltpu.make_async_copy(hidden_buf, hidden_out.at[c], sem.at[2]).wait()

        def four(c):
            pltpu.make_async_copy(summing.low, mlp_in.at[c], sem.at[3]).wait()
            at = pl.ds(pl.multiple_of(c * rows, rows), rows)
            pltpu.make_async_copy(low_turn, mlp_in_t.at[:, at], sem.at[4]).wait()

        summing.at_stage(s, 2, two)
        summing.at_stage(s, 4, four)

    def beside(c, half):
        return remote(half, other_out.at[c], give_sem.at[c], take_sem.at[c], me.to_side)

    def begin_beside(c, half):
        @pl.when(c < chunks - 1)
        def _():
            beside(c, half).start()

        @pl.when(c == chunks - 1)
        def _():
            fetch(half, rest_out, sem.at[5])

    def turn_rows(s):
        at = pl.ds(pl.multiple_of(s * rows, rows), rows)
        fetch(cot.at[at, :], cot_load, sem.at[0]).wait()
        cot_turn[...] = cot_load[...].T
        a = fetch(cot_turn, cot_t.at[:, at], sem.at[1])

        @pl.when(lax.rem(s, per_block) == 0)
        def _():
            normed_turn[...] = normed[...].T
            wide_at = pl.ds(pl.multiple_of(s * rows, block), block)
            fetch(normed_turn, normed_t.at[:, wide_at], sem.at[0]).wait()

        a.wait()

    def body(s, carry):
        summing.step(s, produce, work, lower, emit, begin_beside)
        pl.when(s < chunks)(lambda: turn_rows(s))

        @pl.when(s == chunks - 1)
        def _():
            for at, (a, b) in enumerate(kept):
                fetch(a, b, out_sem.at[at])

        settle(s)
        return carry

    lax.fori_loop(0, summing.slots, body, 0)
    for at, (a, b) in enumerate(kept):
        pltpu.make_async_copy(a, b, out_sem.at[at]).wait()
    for c in range(chunks - 1):
        beside(c, summing.pair.at[c % 3]).wait_recv()


def outer_tile(left_t, right, stage):
    line, _, rows, _ = stage.shape
    group = max(1, 512 // (2 * rows))
    while line % group:
        group -= 1

    def body(m, carry):
        at = pl.multiple_of(m * group * 2 * rows, group * 2 * rows)
        value = forward_dot(left_t[pl.ds(at, group * 2 * rows), :], right)
        stage[pl.ds(m * group, group)] = value.reshape((group, 2, rows, value.shape[1]))
        return carry

    lax.fori_loop(0, line // group, body, 0)


class SmallSum:
    def __init__(self, me, value, lands, sends, recvs):
        self.me, self.value, self.lands, self.sends, self.recvs = me, value, lands, sends, recvs

    def copy(self, k):
        me = self.me
        who = (me.to_core, me.to_chip, me.to_side)[k] if k < 3 else me.along(k - 2)
        return remote(self.value, self.lands.at[k], self.sends.at[k], self.recvs.at[k], who)

    def step(self, at):
        last = 2 + self.me.line
        stages = [[0], [1], [2], list(range(3, last)), []]
        for number, copies in enumerate(stages):
            @pl.when(at == number)
            def _(number=number, copies=copies):
                if number > 0:
                    for k in stages[number - 1]:
                        self.copy(k).wait()
                    for k in stages[number - 1]:
                        self.value[...] = self.value[...] + self.lands[k]
                for k in copies:
                    self.copy(k).start()


def main_kernel(wide, chunks, counts, *refs):
    (mlp_in, mlp_in_t, cot, cot_t, normed_t, hidden, other, rest, q_in, k_in, v_in, q_raw, k_raw,
     context, lse_in, tokens, w_gate, w_up, w_down, w_output, w_query, w_key, w_value, cosine, sine,
     starts, attn_gain, mlp_gain, query_gain, key_gain), refs = take(refs, 30)
    (output, grad_tokens, grad_query, grad_key, grad_value, grad_output, grad_gate, grad_up,
     grad_down, gains_out, grad_hidden, inner_out, other_land, rest_land, rest_core,
     other_t), refs = take(refs, 16)
    wide_lands, refs = take(refs, 7)
    wide_sems, refs = take(refs, 11)
    sems, refs = take(refs, 8)
    wide_buffers, refs = take(refs, 9)
    buffers, refs = take(refs, 7)
    (acts, gains, gain_lands, turned, gain_send, gain_recv, sem, w_sem, store_sem, emit_sem,
     att_sem, give_sem, other_sem, late_sem) = refs
    me = Spot(wide)
    me.greet(True)
    token_count, width = mlp_in.shape
    hidden_units = w_gate.shape[1]
    tiles, line, _, side_rows, cols = wide_lands[0].shape
    blocks = hidden_units // cols
    early_tiles, shared_tiles, late_tiles = counts
    late_from = early_tiles + shared_tiles
    query_width, kv_width = w_query.shape[1], w_key.shape[1]
    all_heads = query_width + 2 * kv_width
    head = query_gain.shape[1]
    q_heads = query_width // head
    group = q_heads // (kv_width // head)
    scale = head ** (-0.5)
    out_tiles = query_width // cols
    narrow_from, pace = 2, 10
    first_attend = chunks + 4
    heads_at_once = 2
    first_heads = first_attend + q_heads // heads_at_once

    def slot_at(r):
        return narrow_from + r - r // pace

    total = WideSum(
        me, counts, lambda late: slot_at(first_attend if late < out_tiles else first_heads),
        wide_lands, wide_sems, wide_buffers,
    )
    other_copy = remote(other, other_land, other_sem.at[0], other_sem.at[1], me.to_core)
    other_copy.start()
    rest_side = remote(rest, rest_land, other_sem.at[6], other_sem.at[7], me.to_side)
    rest_side.start()
    rest_pass = remote(rest_land, rest_core, other_sem.at[8], other_sem.at[9], me.to_core)
    half = token_count // 2
    rows = token_count // chunks
    quarter = rows // 4

    def block_of(t):
        return lax.rem(t, 2) * (blocks // 2) + lax.div(t, 2)

    def half_of(b):
        return lax.div(b, blocks // 2)

    def columns(at):
        return pl.ds(pl.multiple_of(at * cols, cols), cols)

    def emit_tile(tile, value, number):
        def part(first, count, target, turn, place):
            @pl.when((tile >= first) & (tile < first + count))
            def _():
                cut = columns(place(tile - first))
                if turn:
                    turned[number] = value[...].T
                    fetch(turned.at[number], target.at[cut, :], emit_sem.at[number])
                else:
                    fetch(value, target.at[:, cut], emit_sem.at[number])

        def same(at):
            return at

        part(0, early_tiles, grad_down, True, block_of)
        at = late_from
        part(at, out_tiles, grad_output, True, same)
        at += out_tiles
        part(at, query_width // cols, grad_query, False, same)
        at += query_width // cols
        part(at, kv_width // cols, grad_key, False, same)
        at += kv_width // cols
        part(at, kv_width // cols, grad_value, False, same)

    def emit_shared(t, side, value, number):
        cut = columns(side * (blocks // 2) + lax.div(t, 2))

        @pl.when(lax.rem(t, 2) == 0)
        def _():
            fetch(value, grad_gate.at[:, cut], emit_sem.at[number])

        @pl.when(lax.rem(t, 2) == 1)
        def _():
            fetch(value, grad_up.at[:, cut], emit_sem.at[number])

    def emitted(number):
        pltpu.make_async_copy(turned.at[0], turned.at[0], emit_sem.at[number]).wait()

    def compute(xs, cs, ct, gate_w, up_w, down_w, staged, inner, gives):
        pairs = ((mlp_in, xs), (cot, cs), (cot_t, ct))
        for at, (source, target) in enumerate(pairs[:2]):
            fetch(source, target, sem.at[at])

        def weights(t, slot):
            at = columns(block_of(t))
            return (
                pltpu.make_async_copy(w_gate.at[:, at], gate_w.at[slot], w_sem.at[slot, 0]),
                pltpu.make_async_copy(w_up.at[:, at], up_w.at[slot], w_sem.at[slot, 1]),
                pltpu.make_async_copy(w_down.at[at, :], down_w.at[slot], w_sem.at[slot, 2]),
            )

        for copy in weights(0, 0):
            copy.start()
        for at, (source, target) in enumerate(pairs[:2]):
            pltpu.make_async_copy(source, target, sem.at[at]).wait()
        fetch(cot_t, ct, sem.at[2])

        def store(tile):
            slot = lax.rem(tile, 2)
            return pltpu.make_async_copy(staged.at[slot], total.parts.at[tile], store_sem.at[slot])

        def store_inner(t):
            slot = lax.rem(t, 2)
            target = inner_out.at[:, columns(block_of(t))]
            return pltpu.make_async_copy(inner.at[slot], target, give_sem.at[2 + slot])

        def store_gives(t):
            return [
                pltpu.make_async_copy(
                    gives.at[j], total.give.at[2 * lax.div(t, 2) + j], give_sem.at[j]
                )
                for j in range(2)
            ]

        def leaves(t):
            return half_of(block_of(t)) != me.side

        def block(t, carry):
            slot = lax.rem(t, 2)
            for copy in weights(t, slot):
                copy.wait()

            @pl.when(t + 1 < blocks)
            def _():
                for copy in weights(t + 1, 1 - slot):
                    copy.start()

            @pl.when(t >= 2)
            def _():
                store_inner(t - 2).wait()

            at = columns(block_of(t))

            def some(m, carry):
                own = pl.ds(pl.multiple_of(m * half, half), half)
                gate = forward_dot(xs[own, :], gate_w[slot])
                up = forward_dot(xs[own, :], up_w[slot])
                back = nt_dot(cs[own, :], down_w[slot])
                sig = 1.0 / (1.0 + jnp.exp(-gate))
                silu = gate * sig
                inner[slot, own, :] = (silu * up).astype(bf16)
                grad_gate_low = (back * up * sig * (1.0 + gate * (1.0 - sig))).astype(bf16)
                grad_up_low = (back * silu).astype(bf16)
                acts[0, own, at] = grad_gate_low
                acts[1, own, at] = grad_up_low

                @pl.when(leaves(t))
                def _():
                    lines = line // 2
                    there = pl.ds(m * lines, lines)
                    shape = (lines, side_rows, cols)
                    gives[0, there] = grad_gate_low.astype(f32).reshape(shape)
                    gives[1, there] = grad_up_low.astype(f32).reshape(shape)

                return carry

            lax.fori_loop(0, 2, some, 0)
            store_inner(t).start()

            @pl.when(leaves(t))
            def _():
                for copy in store_gives(t):
                    copy.start()

            @pl.when(t == 0)
            def _():
                pltpu.make_async_copy(cot_t, ct, sem.at[2]).wait()

            outer_tile(ct, inner[slot], staged.at[slot])
            store(t).start()

            @pl.when(t == 0)
            def _():
                store(t).wait()

            @pl.when(t > 1)
            def _():
                store(t - 1).wait()
                total.begin(t - 1)

            @pl.when(leaves(t))
            def _():
                for copy in store_gives(t):
                    copy.wait()

            for number, after in enumerate((0, 2)):
                pl.when(t == after)(
                    lambda number=number: total.step(number, emit_tile, emit_shared, emitted)
                )
            return carry

        lax.fori_loop(0, blocks, block, 0)
        store(blocks - 1).wait()
        store_inner(blocks - 2).wait()
        store_inner(blocks - 1).wait()

    pl.run_scoped(
        compute,
        pltpu.VMEM(mlp_in.shape, bf16),
        pltpu.VMEM(mlp_in.shape, bf16),
        pltpu.VMEM(mlp_in_t.shape, bf16),
        pltpu.VMEM((2, width, cols), bf16),
        pltpu.VMEM((2, width, cols), bf16),
        pltpu.VMEM((2, cols, width), bf16),
        pltpu.VMEM((2, line, 2, side_rows, cols), f32),
        pltpu.VMEM((2, token_count, cols), bf16),
        pltpu.VMEM((2, line, side_rows, cols), f32),
    )

    def pass_on(*held):
        (gate_w, up_w, down_w, hidden_load, token_load, out_buf, out_w, left_t, staged, q_low,
         k_low, v_low, k_t, d_context, right, lse, cos, sin, raw, d_query, d_key, d_value,
         heads, inner_load, other_load, other_turn, left_cut) = held
        summing = NarrowSum(me, sems, buffers)
        small = SmallSum(me, gains, gain_lands, gain_send, gain_recv)
        gains[...] = jnp.zeros_like(gains)
        gain_at = (
            slice(0, width), slice(width, 2 * width), slice(2 * width, 2 * width + head),
            slice(2 * width + head, 2 * width + 2 * head),
        )
        loads = ((w_output, out_w), (q_in, q_low), (k_in, k_low), (v_in, v_low), (lse_in, lse),
                 (cosine, cos), (sine, sin))
        for a, b in loads:
            fetch(a, b, sem.at[0]).wait()
        k_t[...] = k_low[...].T
        step = gate_w.shape[1]

        def weights_of(kind, at, slot):
            cut = pl.ds(at * step, step)
            if kind == 0:
                gate = gate_w.at[slot, :, 0:hidden_units]
                return [
                    pltpu.make_async_copy(w_gate.at[cut, :], gate, w_sem.at[slot, 0]),
                    pltpu.make_async_copy(w_up.at[cut, :], up_w.at[slot], w_sem.at[slot, 1]),
                ]
            if kind == 1:
                return [
                    pltpu.make_async_copy(w_down.at[:, cut], down_w.at[slot], w_sem.at[slot, 2])
                ]
            start, found = 0, []
            for j, w in enumerate((w_query, w_key, w_value)):
                there = gate_w.at[slot, :, start : start + w.shape[1]]
                found.append(pltpu.make_async_copy(w.at[cut, :], there, w_sem.at[slot, j]))
                start += w.shape[1]
            return found

        def of_kind(c, body):
            kind = lax.div(c, chunks)
            for number in range(3):
                pl.when(kind == number)(functools.partial(body, number))

        def chunk_rows(c):
            at = lax.rem(c, chunks) * rows
            return pl.ds(pl.multiple_of(at, 2 * rows), 2 * rows)

        def inner_copy(c):
            return pltpu.make_async_copy(inner_out.at[chunk_rows(c), :], inner_load, sem.at[4])

        def ahead_of_produce(c):
            def start(kind):
                if kind == 1:
                    inner_copy(c).start()
                for at in range(2):
                    for copy in weights_of(kind, at, at):
                        copy.start()

            pl.when(lax.rem(c, 2) == 0)(lambda: of_kind(c, start))

        def produce(c, part):
            own = chunk_rows(c)
            count = width // step

            def make(kind):
                if kind == 1:
                    inner_copy(c).wait()
                for at in range(count):
                    slot = at % 2
                    if 1 <= at < count - 1:
                        for copy in weights_of(kind, at + 1, 1 - slot):
                            copy.start()
                    for copy in weights_of(kind, at, slot):
                        copy.wait()
                    if kind == 0:
                        value = nt_dot(acts[0, own, :], gate_w[slot, :, 0:hidden_units])
                        value = value + nt_dot(acts[1, own, :], up_w[slot])
                    elif kind == 1:
                        value = forward_dot(inner_load[...], down_w[slot])
                    else:
                        value = nt_dot(heads[own, :], gate_w[slot, :, 0:all_heads])
                    store_part(part, value, slice(at * step, (at + 1) * step))

            of_kind(c, make)

        def preload(c):
            chunk, kind = lax.rem(c, chunks), lax.div(c, chunks)

            @pl.when(kind < 2)
            def _():
                fetch(hidden.at[chunk], hidden_load, sem.at[0])

            @pl.when(kind == 0)
            def _():
                fetch(cot.at[own_rows(chunk), :], token_load, sem.at[1])

            @pl.when(kind == 2)
            def _():
                fetch(grad_hidden.at[chunk], hidden_load, sem.at[0])
                fetch(tokens.at[own_rows(chunk), :], token_load, sem.at[1])

        def work(c, pulled):
            kind = lax.div(c, chunks)
            pltpu.make_async_copy(hidden_load, hidden_load, sem.at[0]).wait()

            @pl.when(kind != 1)
            def _():
                pltpu.make_async_copy(token_load, token_load, sem.at[1]).wait()

            @pl.when(kind == 0)
            def _():
                mid = hidden_load[...]
                inverse = inverse_rms(mid)
                unit = mid * inverse
                gains[:, gain_at[1]] += jnp.sum(pulled * unit, axis=0, keepdims=True)
                back = norm_back(pulled, unit, inverse, mlp_gain[...])
                out_buf[...] = token_load[...].astype(f32) + back
                fetch(out_buf, grad_hidden.at[lax.rem(c, chunks)], sem.at[2])

            @pl.when(kind == 1)
            def _():
                out_buf[...] = hidden_load[...] + pulled

            @pl.when(kind == 2)
            def _():
                mid = token_load[...].astype(f32)
                inverse = inverse_rms(mid)
                unit = mid * inverse
                gains[:, gain_at[0]] += jnp.sum(pulled * unit, axis=0, keepdims=True)
                out_buf[...] = hidden_load[...] + norm_back(pulled, unit, inverse, attn_gain[...])

            return out_buf[...]

        def settle(s):
            def two(c):
                @pl.when(lax.div(c, chunks) == 0)
                def _():
                    pltpu.make_async_copy(out_buf, out_buf, sem.at[2]).wait()

            def four(c):
                @pl.when(lax.div(c, chunks) > 0)
                def _():
                    pltpu.make_async_copy(summing.low, summing.low, sem.at[3]).wait()

            summing.at_stage(s, 2, two)
            summing.at_stage(s, 4, four)

        def own_rows(chunk):
            at = chunk * rows + me.core * 2 * quarter + me.chip * quarter
            return pl.ds(pl.multiple_of(at, quarter), quarter)

        def lower(value):
            return value.astype(bf16)

        def emit_rows(c, low):
            chunk = lax.rem(c, chunks)
            kind = lax.div(c, chunks)

            @pl.when(kind == 0)
            def _():
                own = pl.ds(pl.multiple_of(chunk * rows, rows), rows)
                value = low[...].reshape(rows, width)
                d_context[own, :] = nt_dot(value, out_w[...]).astype(bf16)
                left_t[:, own] = value.T

            @pl.when(kind == 1)
            def _():
                fetch(low, output.at[chunk], sem.at[3])

            @pl.when(kind == 2)
            def _():
                fetch(low, grad_tokens.at[chunk], sem.at[3])

        def take_other(c):
            mine, theirs = other_load.at[me.core], other_load.at[1 - me.core]

            @pl.when(c < chunks - 1)
            def _():
                a = fetch(other.at[c], mine, att_sem.at[0])
                fetch(other_land.at[c], theirs, give_sem.at[0]).wait()
                a.wait()

            @pl.when(c == chunks - 1)
            def _():
                rest_pass.wait()
                a = fetch(rest_land, mine, att_sem.at[0])
                fetch(rest_core, theirs, give_sem.at[0]).wait()
                a.wait()

            value = (other_load[...] * mlp_gain[...][None, None]).astype(bf16)
            other_turn[...] = value.reshape(rows, width).T
            at = pl.ds(pl.multiple_of(c * rows, rows), rows)
            fetch(other_turn, other_t.at[:, at], att_sem.at[0]).wait()

        def left_copies(m, slot):
            group = left_cut.shape[2]
            at = pl.ds(pl.multiple_of(m * group, group), group)
            return (
                pltpu.make_async_copy(mlp_in_t.at[at, :], left_cut.at[slot, 0], other_sem.at[2 + slot]),
                pltpu.make_async_copy(other_t.at[at, :], left_cut.at[slot, 1], other_sem.at[4 + slot]),
            )

        def load_shared(t):
            for copy in left_copies(0, 0):
                copy.start()
            total.give_copy(t).wait()
            fetch(total.give_land.at[t], total.got, att_sem.at[0])

        def put_shared(t, s):
            pltpu.make_async_copy(total.got, total.got, att_sem.at[0]).wait()
            right[...] = total.got[...].reshape(token_count, cols).astype(bf16)
            mine = acts[lax.rem(t, 2), :, columns(me.side * (blocks // 2) + lax.div(t, 2))]
            group = left_cut.shape[2]
            count = width // group

            def one(m, carry):
                slot = lax.rem(m, 2)
                for copy in left_copies(m, slot):
                    copy.wait()

                @pl.when(m + 1 < count)
                def _():
                    for copy in left_copies(m + 1, 1 - slot):
                        copy.start()

                value = forward_dot(left_cut[slot, 0], mine) + forward_dot(left_cut[slot, 1], right[...])
                lines = group // (2 * side_rows)
                staged[pl.ds(m * lines, lines)] = value.reshape((lines, 2, side_rows, cols))
                return carry

            lax.fori_loop(0, count, one, 0)
            fetch(staged, total.parts.at[early_tiles + t], store_sem.at[0])
            total.ring[lax.rem(s, total.ring.shape[0])] = staged[:, 1 - me.side]

        def shared_stored():
            pltpu.make_async_copy(staged, total.parts.at[0], store_sem.at[0]).wait()

        def put(tile, right_value):
            outer_tile(left_t, right_value, staged)
            fetch(staged, total.parts.at[tile], store_sem.at[0]).wait()

        def rope_norm_back(grad, raw_value, gain, at):
            scaled = grad * cos[...] - half_turn(grad) * sin[...]
            inverse = inverse_rms(raw_value)
            unit = raw_value * inverse
            gains[:, at] += jnp.sum(scaled * unit, axis=0, keepdims=True)
            return norm_back(scaled, unit, inverse, gain[...])

        def attend_back(h):
            kv = lax.div(h, group)
            cut = pl.ds(pl.multiple_of(h * head, head), head)
            kv_cut = pl.ds(pl.multiple_of(kv * head, head), head)

            @pl.when(lax.rem(h, group) == 0)
            def _():
                d_key[...] = jnp.zeros_like(d_key)
                d_value[...] = jnp.zeros_like(d_value)

            load = fetch(q_raw.at[:, cut], raw, att_sem.at[0])
            size = min(256, token_count)
            for i in range(token_count // size):
                own, keys = slice(i * size, (i + 1) * size), (i + 1) * size
                q, dc = q_low[own, cut], d_context[own, cut]
                scores = nt_dot(k_low[0:keys, kv_cut], q) * scale
                expd = jnp.exp(scores - lse[pl.ds(h, 1), own])
                probs = jnp.where(allowed_pairs(keys, own, starts[:, own]), expd, 0.0)
                d_value[0:keys, :] += forward_dot(probs.astype(bf16), dc)
                d_probs = nt_dot(v_low[0:keys, kv_cut], dc)
                mean = jnp.sum(probs * d_probs, axis=0, keepdims=True)
                d_scores = (probs * (d_probs - mean)).astype(bf16)
                d_key[0:keys, :] += forward_dot(d_scores, q)
                d_query[own, :] = forward_dot(k_t[kv_cut, 0:keys], d_scores).T
            load.wait()
            heads[:, cut] = rope_norm_back(
                d_query[...] * scale, raw[...], query_gain, gain_at[2]
            ).astype(bf16)

            @pl.when(lax.rem(h, group) == group - 1)
            def _():
                fetch(k_raw.at[:, kv_cut], raw, att_sem.at[0]).wait()
                there = pl.ds(pl.multiple_of(query_width + kv * head, head), head)
                heads[:, there] = rope_norm_back(
                    d_key[...] * scale, raw[...], key_gain, gain_at[3]
                ).astype(bf16)
                there = pl.ds(pl.multiple_of(query_width + kv_width + kv * head, head), head)
                heads[:, there] = d_value[...].astype(bf16)

        small_at = summing.slots - 3
        steps = small_at + 5
        while slot_at(steps) < total.slots:
            steps += 1

        def shared_at(s):
            paired, pair, second, _ = total.item(s)
            return paired & total.here(pair, second) & (s < total.items)

        def settle_all(r):
            s = narrow_from + r - lax.div(r, pace)

            @pl.when((r >= 0) & (lax.rem(r, pace) != pace - 1))
            def _():
                total.settle(s, emitted)
                pl.when(shared_at(s))(shared_stored)

            settle(r)

        def body(r, carry):
            s = narrow_from + r - lax.div(r, pace)
            wide_too = lax.rem(r, pace) != pace - 1
            settle_all(r - 1)
            summing.at_stage(r, 0, ahead_of_produce)

            @pl.when(r == first_attend - 1)
            def _():
                fetch(context, heads.at[:, 0:query_width], late_sem.at[0])

            @pl.when(r == first_attend)
            def _():
                held = heads.at[:, 0:query_width]
                pltpu.make_async_copy(context, held, late_sem.at[0]).wait()
                for t in range(out_tiles):
                    put(late_from + t, heads[:, t * cols : (t + 1) * cols])
                fetch(normed_t, left_t, late_sem.at[0])

            @pl.when((r >= first_attend) & (r < first_heads))
            def _():
                def one(h, carry):
                    attend_back((r - first_attend) * heads_at_once + h)
                    return carry

                lax.fori_loop(0, heads_at_once, one, 0)

            @pl.when(r == first_heads)
            def _():
                pltpu.make_async_copy(normed_t, left_t, late_sem.at[0]).wait()

                def one(t, carry):
                    put(late_from + out_tiles + t, heads[:, columns(t)])
                    return carry

                lax.fori_loop(0, all_heads // cols, one, 0)

            @pl.when(r == 0)
            def _():
                other_copy.wait()
                rest_side.wait()
                rest_pass.start()

            @pl.when(r < chunks // 2)
            def _():
                for each in range(2):
                    take_other(r * 2 + each)

            pl.when(wide_too & shared_at(s))(lambda: load_shared(total.item(s)[1] - 1))
            summing.at_stage(r, 2, preload)
            pl.when(wide_too)(lambda: total.fetches(s))
            summing.step(r, produce, work, lower, emit_rows, only=(4, 3, 2, 1))
            pl.when(wide_too & shared_at(s))(lambda: put_shared(total.item(s)[1] - 1, s))

            @pl.when(wide_too)
            def _():
                total.sums(s, emit_tile, emit_shared)

            summing.step(r, produce, work, lower, emit_rows, only=(0,))
            pl.when(r >= small_at)(lambda: small.step(r - small_at))
            return carry

        lax.fori_loop(0, steps, body, 0)
        settle_all(steps - 1)
        total.finish()

    step = min(256, width)
    pl.run_scoped(
        pass_on,
        pltpu.VMEM((2, step, max(hidden_units, all_heads)), bf16),
        pltpu.VMEM((2, step, hidden_units), bf16),
        pltpu.VMEM((2, hidden_units, step), bf16),
        pltpu.VMEM((quarter, width), f32),
        pltpu.VMEM((quarter, width), bf16),
        pltpu.VMEM((quarter, width), f32),
        pltpu.VMEM(w_output.shape, bf16),
        pltpu.VMEM(normed_t.shape, bf16),
        pltpu.VMEM((line, 2, side_rows, cols), f32),
        pltpu.VMEM(q_in.shape, bf16),
        pltpu.VMEM(k_in.shape, bf16),
        pltpu.VMEM(v_in.shape, bf16),
        pltpu.VMEM((kv_width, token_count), bf16),
        pltpu.VMEM(q_in.shape, bf16),
        pltpu.VMEM((token_count, cols), bf16),
        pltpu.VMEM(lse_in.shape, f32),
        pltpu.VMEM(cosine.shape, f32),
        pltpu.VMEM(sine.shape, f32),
        pltpu.VMEM((token_count, head), f32),
        pltpu.VMEM((token_count, head), f32),
        pltpu.VMEM((token_count, head), f32),
        pltpu.VMEM((token_count, head), f32),
        pltpu.VMEM((token_count, all_heads), bf16),
        pltpu.VMEM((2 * rows, hidden_units), bf16),
        pltpu.VMEM((2, 2, quarter, width), f32),
        pltpu.VMEM((width, rows), bf16),
        pltpu.VMEM((2, 2, max(512, 2 * side_rows), token_count), bf16),
    )
    fetch(gains, gains_out, sem.at[0]).wait()


def call(kernel, collective_id, out_shape, in_specs, out_specs, scratch, arrays):
    return pl.pallas_call(
        kernel,
        out_shape=out_shape,
        in_specs=in_specs,
        out_specs=out_specs,
        scratch_shapes=scratch,
        compiler_params=pltpu.CompilerParams(
            collective_id=collective_id,
            has_side_effects=True,
            vmem_limit_bytes=62 * 1024 * 1024,
        ),
    )(*arrays)


def per_device(
    wide,
    tokens,
    seq_lengths,
    attn_gain,
    w_query,
    key_weight,
    value_weight,
    query_gain,
    key_norm_gain,
    w_output,
    mlp_gain,
    w_gate,
    w_up,
    w_down,
    cotangent,
):
    token_count, width = tokens.shape
    head_dim = query_gain.shape[0]
    query_width, kv_width = w_query.shape[1], key_weight.shape[1]
    hidden_units = w_gate.shape[1]
    all_heads = query_width + 2 * kv_width
    line = wide // 2
    side_rows = width // wide
    chunks = 8
    rows = token_count // chunks
    quarter = rows // 4
    block = min(256, token_count)
    dma = pltpu.SemaphoreType.DMA
    shape = jax.ShapeDtypeStruct

    segment_index, token_positions = layout(seq_lengths, token_count)
    token_positions = token_positions.reshape(-1)
    starts = (jnp.arange(token_count, dtype=jnp.int32) - token_positions)[None]
    cosine, sine = tables(token_positions, head_dim)
    cosine = cosine.reshape(token_count, head_dim)
    sign = jnp.where(jnp.arange(head_dim) < head_dim // 2, -1.0, 1.0).astype(f32)
    sine = sine.reshape(token_count, head_dim) * sign
    q_heads = query_width // head_dim

    kept = [
        shape((token_count, query_width), bf16),
        shape((token_count, kv_width), bf16),
        shape((token_count, kv_width), bf16),
        shape((token_count, query_width), f32),
        shape((token_count, kv_width), f32),
        shape((token_count, query_width), bf16),
        shape((q_heads, token_count), f32),
    ]
    vmem = [pltpu.VMEM(k.shape, k.dtype) for k in kept]
    outs = call(
        lambda *refs: attend_kernel(wide, chunks, *refs),
        1,
        [
            shape((chunks, 2, 2, quarter, width), bf16),
            shape((width, token_count), bf16),
            shape((width, token_count), bf16),
            shape((width, token_count), bf16),
            shape((chunks, quarter, width), f32),
            *kept,
            shape((chunks - 1, 2, quarter, width), f32),
            shape((2, quarter, width), f32),
        ],
        [in_vmem, any_space] + [in_vmem] * 11,
        [any_space] * 14,
        [
            *NarrowSum.sems(chunks),
            *NarrowSum.buffers(quarter, width),
            pltpu.VMEM((quarter, width), f32),
            *vmem[:3],
            pltpu.VMEM((kv_width, token_count), bf16),
            *vmem[3:],
            pltpu.VMEM((block, width), bf16),
            pltpu.VMEM((width, block), bf16),
            pltpu.VMEM((rows, width), bf16),
            pltpu.VMEM((width, rows), bf16),
            pltpu.VMEM((width, rows), bf16),
            dma((6,)),
            dma((7,)),
            dma((chunks,)),
            dma((chunks,)),
        ],
        (
            tokens, cotangent, w_query, key_weight, value_weight, w_output, attn_gain[None],
            mlp_gain[None], query_gain[None], key_norm_gain[None], cosine, sine, starts,
        ),
    )
    (mlp_in, mlp_in_t, cot_t, normed_t, hidden, q_low, k_low, v_low, q_raw, k_raw, context,
     lse, other, rest) = outs[:14]

    cols = min(256 if line <= 4 else 128, hidden_units // 6)
    counts = (hidden_units // cols, hidden_units // cols, (query_width + all_heads) // cols)
    gain_width = 2 * width + 2 * head_dim
    outs = call(
        lambda *refs: main_kernel(wide, chunks, counts, *refs),
        2,
        [
            shape((chunks, 2, 2, quarter, width), bf16),
            shape((chunks, 2, 2, quarter, width), bf16),
            shape((side_rows, query_width), f32),
            shape((side_rows, kv_width), f32),
            shape((side_rows, kv_width), f32),
            shape((query_width, side_rows), f32),
            shape((side_rows, hidden_units), f32),
            shape((side_rows, hidden_units), f32),
            shape((hidden_units, side_rows), f32),
            shape((1, gain_width), f32),
            shape((chunks, quarter, width), f32),
            shape((token_count, hidden_units), bf16),
            shape((chunks - 1, 2, quarter, width), f32),
            shape((2, quarter, width), f32),
            shape((2, quarter, width), f32),
            shape((width, token_count), bf16),
            *WideSum.lands(counts, line, side_rows, cols),
        ],
        [any_space] * 25 + [in_vmem] * 5,
        [any_space] * 23,
        [
            *WideSum.sems(counts, line),
            *NarrowSum.sems(3 * chunks),
            *WideSum.buffers(line, side_rows, cols),
            *NarrowSum.buffers(quarter, width),
            pltpu.VMEM((2, token_count, hidden_units), bf16),
            pltpu.VMEM((1, gain_width), f32),
            pltpu.VMEM((2 + line, 1, gain_width), f32),
            pltpu.VMEM((2, cols, side_rows), f32),
            dma((2 + line,)),
            dma((2 + line,)),
            dma((5,)),
            dma((2, 3)),
            dma((2,)),
            dma((3,)),
            dma((1,)),
            dma((4,)),
            dma((10,)),
            dma((1,)),
        ],
        (
            mlp_in.reshape(token_count, width), mlp_in_t, cotangent, cot_t, normed_t, hidden,
            other, rest, q_low, k_low, v_low, q_raw, k_raw, context, lse, tokens, w_gate, w_up, w_down,
            w_output, w_query, key_weight, value_weight, cosine, sine, starts, attn_gain[None],
            mlp_gain[None], query_gain[None], key_norm_gain[None],
        ),
    )
    (output, grad_tokens, shard_query, shard_key, shard_value, shard_output, shard_gate,
     shard_up, shard_down, gains) = outs[:10]
    gains = gains[0]
    at = lax.axis_index("wide")
    head_part = head_dim // wide

    def own(start, size):
        return lax.dynamic_slice_in_dim(gains, start + at * size, size)

    return (
        output.reshape(token_count, width),
        grad_tokens.reshape(token_count, width),
        own(0, side_rows),
        shard_query,
        shard_key,
        shard_value,
        own(2 * width, head_part),
        own(2 * width + head_dim, head_part),
        shard_output,
        own(width, side_rows),
        shard_gate,
        shard_up,
        shard_down,
    )


def solution(mesh):
    def run(*arrays):
        return per_device(mesh.shape["wide"], *arrays)

    return jax.shard_map(
        run,
        mesh=mesh,
        in_specs=(
            P("wide", None),
            P("wide", None),
            P(),
            P(None, "narrow"),
            P(None, "narrow"),
            P(None, "narrow"),
            P(),
            P(),
            P("narrow", None),
            P(),
            P(None, "narrow"),
            P(None, "narrow"),
            P("narrow", None),
            P("wide", None),
        ),
        out_specs=(
            P("wide", None),
            P("wide", None),
            P("wide"),
            P("wide", "narrow"),
            P("wide", "narrow"),
            P("wide", "narrow"),
            P("wide"),
            P("wide"),
            P("narrow", "wide"),
            P("wide"),
            P("wide", "narrow"),
            P("wide", "narrow"),
            P("narrow", "wide"),
        ),
        check_vma=False,
    )
```
